128 devices in a mesh: section: 4 (over z), table: 32 (over x, y, core).
Axes of the slice: x: 4, y: 4, z: 4, core: 2. Of those that a mesh axis runs over, the one named last changes fastest.
Arguments:
- saved_inputs: bfloat16 [4, 4, 2048, 4096], P('section', None, 'table'), may hold values from -6 to 6
- memory: bfloat16 [4, 4, 2048, 8, 1024], P('section', None, 'table'), may hold values from -6 to 6
- value_weight: bfloat16 [4, 8, 1024, 512], P('section'), may hold values from -0.1875 to 0.1875
- conv_weight: float32 [4, 4, 4, 4096], P('section'), may hold values from -3 to 3
- norm_gain: float32 [4, 4, 4096], P('section'), may hold values from 0.25 to 1.75
- layer_counts: int32 [4], P('section'), may hold values from 1 to 4
- row_ids: int32 [4, 4, 2048, 8], P('section', None, 'table'), may hold values from 0 to 32767, as said below
- out_grad: bfloat16 [4, 2048, 4096], P(None, 'table'), may hold values from -6 to 6
Outputs:
- section_grads: bfloat16 [4, 4, 2048, 4096], P('section', None, 'table')
- table_grad: float32 [4, 32768, 1024], P('section', 'table')
The draws below stay inside these ranges and needn't reach their ends.
Inputs may be any that keep to these rules, and one draw needn't show every extreme that they name: `row_ids`: the owner of a row id is id // 1024. In every section and micro-batch, at most 24 of the ids of the 64 tokens of one index of table fall to one owner.
All inputs are finite; a program needn't handle non-finite values.
Results may differ from the reference program's by a relative error of at most 0.0062.
Values may be sent and summed in bfloat16 or wider, within the bound.
No kernel may reach another device: no remote copies, remote signals or barrier semaphores. Data moves between devices by JAX's collectives and lax.ppermute only.
A program may use at most 256 MiB of HBM per device.

```python
import math
import jax
import jax.numpy as jnp
from jax import lax

D = 4096
HEADS = 8
ROW = 1024
KERNEL = 4
LAYERS = 4
MB = 4
TOKC = 64
TABLE_DEV = 1024
VALW = 512
SECTIONS = 4
TOKENS = 2048
TABLE_ROWS = 32768
CAP = 24


def draw_layer_counts(key, part):
    key = jax.random.fold_in(key, 3)
    order = jax.random.permutation(key, SECTIONS)
    return (order % LAYERS + 1).astype(jnp.int32)


def draw_row_ids(key, part):
    key = jax.random.fold_in(key, 7)
    keys = jax.random.split(key, 5)
    owners = TABLE_ROWS // TABLE_DEV
    block = TOKC * HEADS
    shape = (SECTIONS, MB, owners, block)
    scores = jax.random.randint(keys[0], shape, 0, 1 << 20) * block + lax.broadcasted_iota(jnp.int32, shape, 3)
    order = jnp.argsort(scores, axis=3)
    ranks = jnp.argsort(order, axis=3).astype(jnp.int32)
    hot_owner = jax.random.randint(keys[1], (SECTIONS, MB, 1, 1), 0, owners)
    spread_owner = (hot_owner + 1 + (ranks - CAP) % (owners - 1)) % owners
    owner = jnp.where(ranks < CAP, hot_owner, spread_owner)
    common = jax.random.randint(keys[2], shape, 0, 4) == 0
    offset = jnp.where(common, jax.random.randint(keys[3], shape, 0, 16), jax.random.randint(keys[4], shape, 0, TABLE_DEV))
    ids_all = owner * TABLE_DEV + offset
    return ids_all.reshape(SECTIONS, MB, TOKENS, HEADS).astype(jnp.int32)


def level_of(own_key, dims, shards, least, high):
    def one(axis_at, blocks):
        draws = jax.random.uniform(jax.random.fold_in(jax.random.fold_in(own_key, 6), axis_at), (blocks,), jnp.float32, least / len(shards), high / len(shards))
        return jnp.repeat(jnp.exp(draws), dims[axis_at] // blocks).reshape((-1,) + (1,) * (len(dims) - axis_at - 1))

    level = one(*shards[0])
    for cut in shards[1:]:
        level = level * one(*cut)
    return level


def centred(stream_key, dims, spread, reach, pieces=(), kind=jnp.bfloat16):
    level = level_of(stream_key, dims, pieces, -0.22, 0.18) if pieces else 1.0
    values = jax.random.normal(stream_key, dims, jnp.float32) * spread * level
    return jnp.minimum(jnp.maximum(values, -reach), reach).astype(kind)


def setup_inputs(seed: int = 0) -> dict:
    splits = jax.random.split(jax.random.key(seed), 9)
    return {
        "saved_inputs": centred(splits[0], (SECTIONS, MB, TOKENS, D), 1.0, 6.0, ((0, 4), (2, 32))),
        "memory": centred(splits[1], (SECTIONS, MB, TOKENS, HEADS, ROW), 1.0, 6.0, ((0, 4), (2, 32))),
        "value_weight": centred(splits[2], (SECTIONS, HEADS, ROW, VALW), ROW ** -0.5, 0.1875, ((0, 4),)),
        "conv_weight": centred(splits[3], (SECTIONS, LAYERS, KERNEL, D), 0.5, 3.0, ((0, 4),), jnp.float32),
        "norm_gain": jnp.clip(1.0 + 0.15 * jax.random.normal(splits[4], (SECTIONS, LAYERS, D), jnp.float32), 0.25, 1.75),
        "layer_counts": draw_layer_counts(jax.random.fold_in(splits[8], 71), 0),
        "row_ids": draw_row_ids(jax.random.fold_in(splits[8], 71), 0),
        "out_grad": centred(splits[7], (MB, TOKENS, D), 1.0, 6.0, ((1, 32),)),
    }


epsilon = 1e-06

def rms_unit(values):
    return values * lax.rsqrt(lax.optimization_barrier(jnp.mean(values * values, -1, keepdims=True)) + epsilon)

def gate_mix(inputs, values):
    score = lax.optimization_barrier(jnp.sum(rms_unit(inputs) * rms_unit(values), -1, keepdims=True)) / math.sqrt(inputs.shape[-1])
    return inputs + jax.nn.sigmoid(score) * values

def conv_layer(hidden, kernel_taps, gain):
    normed = rms_unit(hidden) * gain
    width = kernel_taps.shape[0]
    length = hidden.shape[0]
    padded = jnp.concatenate([jnp.zeros((width - 1, hidden.shape[1]), hidden.dtype), normed], 0)
    mixed = kernel_taps[0] * padded[width - 1:width - 1 + length]
    for offset in range(1, width):
        mixed = mixed + kernel_taps[offset] * padded[width - 1 - offset:width - 1 - offset + length]
    return hidden + jax.nn.silu(mixed)

def reference(saved_inputs, memory, value_weight, conv_weight, norm_gain, layer_counts, row_ids, out_grad):
    sections = saved_inputs.shape[0]
    grads_list = []
    tables_list = []
    upper = out_grad
    for section_id in reversed(range(sections)):
        weight = value_weight[section_id].astype(jnp.float32)

        def section_map(inputs, values):
            hidden = gate_mix(inputs, values)
            for layer in range(LAYERS):
                fresh = conv_layer(hidden, conv_weight[section_id, layer], norm_gain[section_id, layer])
                hidden = jnp.where(layer < layer_counts[section_id], fresh, hidden)
            return hidden

        def one_batch(operands):
            inputs_b, memory_b, grad_b = operands
            length = inputs_b.shape[0]
            values = jnp.einsum('thr,hrc->thc', memory_b.astype(jnp.float32), weight).reshape(length, -1)
            pull = jax.vjp(section_map, inputs_b.astype(jnp.float32), values)[1]
            grad_in, grad_values = pull(grad_b.astype(jnp.float32))
            grad_values = grad_values.astype(jnp.bfloat16).reshape(length, HEADS, -1)
            row_grads = jnp.einsum('thc,hrc->thr', grad_values.astype(jnp.float32), weight)
            return (grad_in.astype(jnp.bfloat16), row_grads)
        grad_all, row_all = lax.map(one_batch, (saved_inputs[section_id], memory[section_id], upper))
        flat_ids = row_ids[section_id].reshape(-1).astype(jnp.int32)
        table_sum = jnp.zeros((TABLE_ROWS, ROW), jnp.float32).at[flat_ids].add(row_all.reshape(-1, ROW))
        grads_list.append(grad_all)
        tables_list.append(table_sum)
        upper = grad_all
    return (jnp.stack(grads_list[::-1]), jnp.stack(tables_list[::-1]))
```

```python
import functools
import math

import jax
import jax.numpy as jnp
from jax import lax
from jax.experimental import pallas as pl
from jax.experimental.pallas import tpu as pltpu
from jax.sharding import PartitionSpec as P

TABLE_DEV = 1024
HALO = 16
EPS = 1e-06
LANES = 128
MIB = 1 << 20

f32 = jnp.float32
bf16 = jnp.bfloat16


def row_total(partial):
    return jnp.broadcast_to(jnp.sum(partial, -1, keepdims=True), partial.shape)


def columns(chunk):
    return pl.ds(pl.multiple_of(chunk * LANES, LANES), LANES)


def forward_kernel(
    live_ref, xb, xm, xa, vb, vm, va, taps, hid_out, der_out, scal_out,
    x_win, v_win, hid, der, scal, rms_now, sems,
):
    width = xm.shape[-1]
    rows = x_win.shape[0]
    keep = rows - HALO
    chunks = width // LANES
    live = live_ref[0]
    length = xm.shape[-2]

    def load(chunk, sums):
        cols = columns(chunk)
        for ref, at, size in ((xb, 0, HALO), (xm, HALO, length), (xa, HALO + length, HALO)):
            x_win[at : at + size, cols] = ref[0, :, cols].astype(f32)
        for ref, at, size in ((vb, 0, HALO), (vm, HALO, length), (va, HALO + length, HALO)):
            v_win[at : at + size, cols] = ref[0, :, cols]
        x = x_win[:, cols]
        v = v_win[:, cols]
        return sums[0] + x * x, sums[1] + v * v, sums[2] + x * v

    zero = jnp.zeros((rows, LANES), f32)
    xx, vv, xv = lax.fori_loop(0, chunks, load, (zero, zero, zero))
    xv = row_total(xv)
    rx = lax.rsqrt(row_total(xx) / width + EPS)
    rv = lax.rsqrt(row_total(vv) / width + EPS)
    gate = jax.nn.sigmoid(rx * rv * xv / math.sqrt(width))
    scal[4] = rx[HALO:]
    scal[5] = rv[HALO:]
    scal[6] = xv[HALO:]
    scal[7] = gate[HALO:]
    rms_now[...] = gate

    def mix(chunk, total):
        cols = columns(chunk)
        hidden = x_win[:, cols] + rms_now[...] * v_win[:, cols]
        hid[0, :, cols] = hidden
        return total + hidden * hidden

    total = lax.fori_loop(0, chunks, mix, zero)

    def hidden_copy(layer):
        return pltpu.make_async_copy(
            hid.at[layer, pl.ds(HALO, keep)], hid_out.at[layer], sems.at[0, layer]
        )

    def slope_copy(layer):
        return pltpu.make_async_copy(der.at[layer], der_out.at[layer], sems.at[1, layer])

    def layer_step(layer, total):
        hidden_copy(layer).start()
        rms = lax.rsqrt(row_total(total) / width + EPS)
        scal[layer] = rms[HALO:]
        rms_now[...] = rms

        def one(chunk, total):
            cols = columns(chunk)
            hidden = hid[layer, :, cols]
            unit = hidden * rms_now[...]
            mixed = taps[layer, 0:1, cols] * unit
            for k in range(1, 4):
                mixed = mixed + taps[layer, k : k + 1, cols] * pltpu.roll(unit, k, 0)
            sigma = 0.5 * jnp.tanh(0.5 * mixed) + 0.5
            silu = mixed * sigma
            der[layer, :, cols] = (sigma + silu * (1.0 - sigma))[HALO:]
            after = hidden + silu
            hid[layer + 1, :, cols] = after
            return total + after * after

        total = lax.fori_loop(0, chunks, one, zero)
        slope_copy(layer).start()
        return total

    lax.fori_loop(0, live, layer_step, total)
    out = pltpu.make_async_copy(scal, scal_out, sems.at[0, 4])
    out.start()

    def finish(layer, carry):
        hidden_copy(layer).wait()
        slope_copy(layer).wait()
        return carry

    lax.fori_loop(0, live, finish, 0)
    out.wait()


def forward_map(batch, live, x, x_before, x_after, v, v_before, v_after, taps):
    length, width = x.shape[1:]
    keep = length + HALO
    rows = keep + HALO
    layers = taps.shape[0]

    def part(size):
        return pl.BlockSpec((1, size, width), lambda i, *_: (batch, 0, 0))

    return pl.pallas_call(
        forward_kernel,
        out_shape=(
            jax.ShapeDtypeStruct((layers, keep, width), f32),
            jax.ShapeDtypeStruct((layers, keep, width), f32),
            jax.ShapeDtypeStruct((8, keep, LANES), f32),
        ),
        grid_spec=pltpu.PrefetchScalarGridSpec(
            num_scalar_prefetch=1,
            grid=(1,),
            in_specs=[
                part(HALO), part(length), part(HALO),
                part(HALO), part(length), part(HALO),
                pl.BlockSpec(taps.shape, lambda i, *_: (0, 0, 0)),
            ],
            out_specs=[pl.BlockSpec(memory_space=pl.ANY)] * 3,
            scratch_shapes=[
                pltpu.VMEM((rows, width), f32),
                pltpu.VMEM((rows, width), f32),
                pltpu.VMEM((layers + 1, rows, width), f32),
                pltpu.VMEM((layers, keep, width), f32),
                pltpu.VMEM((8, keep, LANES), f32),
                pltpu.VMEM((rows, LANES), f32),
                pltpu.SemaphoreType.DMA((2, layers + 1)),
            ],
        ),
        compiler_params=pltpu.CompilerParams(vmem_limit_bytes=44 * MIB),
        cost_estimate=pl.CostEstimate(flops=30 * layers * rows * width, bytes_accessed=16 * MIB, transcendentals=layers * rows * width),
        name="forward_map",
    )(live, x_before, x, x_after, v_before, v, v_after, taps)


def backward_kernel(
    held, info, near, near_halo, top, top_halo, x_all, xa_all, v_all, va_all, taps, *refs,
):
    saved = [refs[3 * i : 3 * i + 3] for i in range(held[1])]
    refs = refs[3 * held[1] :]
    if held[2]:
        refs = refs[2:]
    (
        grad_send, halo_send, grads_all, gv_all,
        hid, der, scal, x_win, v_win, g, u, coef, x_in, xa_in, g_in, ga_in, gv, sems,
    ) = refs
    which = info[0]
    active = info[1]
    is_top = info[2]
    live = info[3]
    length, width = grad_send.shape
    rows = g.shape[0]
    chunks = width // LANES
    first, count = held[0], held[1]

    def scal_copy(i):
        return pltpu.make_async_copy(saved[i][2], scal, sems.at[2, 0])

    def hidden_copy(i, layer):
        return pltpu.make_async_copy(saved[i][0].at[layer], hid.at[layer], sems.at[0, layer])

    def slope_copy(i, layer):
        return pltpu.make_async_copy(saved[i][1].at[layer], der.at[layer], sems.at[1, layer])

    def input_copies():
        return (
            pltpu.make_async_copy(x_all.at[which], x_in, sems.at[2, 1]),
            pltpu.make_async_copy(xa_all.at[which], xa_in, sems.at[2, 2]),
            pltpu.make_async_copy(v_all.at[which], v_win.at[pl.ds(0, length)], sems.at[2, 3]),
            pltpu.make_async_copy(va_all.at[which], v_win.at[pl.ds(length, HALO)], sems.at[2, 4]),
        )

    def grad_copies(source, source_halo):
        return (
            pltpu.make_async_copy(source, g_in, sems.at[3, 0]),
            pltpu.make_async_copy(source_halo, ga_in, sems.at[3, 1]),
        )

    @pl.when(active == 1)
    def _():
        @pl.when(is_top == 1)
        def _():
            for copy in grad_copies(top.at[which], top_halo.at[which]):
                copy.start()

        @pl.when(is_top == 0)
        def _():
            for copy in grad_copies(near, near_halo):
                copy.start()

        for i in range(count):
            @pl.when(which == first + i)
            def _():
                scal_copy(i).start()

                def begin(step, carry):
                    layer = live - 1 - step
                    slope_copy(i, layer).start()
                    hidden_copy(i, layer).start()
                    return carry

                lax.fori_loop(0, live, begin, 0)

        for copy in input_copies():
            copy.start()

        zero = jnp.zeros((rows, LANES), f32)
        for copy in grad_copies(near, near_halo):
            copy.wait()
        scal_copy(0).wait()

        def into_taps(layer, cols, grad):
            slope = grad * der[layer, :, cols]
            out = taps[layer, 0:1, cols] * slope
            for k in range(1, 4):
                out = out + taps[layer, k : k + 1, cols] * pltpu.roll(slope, rows - k, 0)
            u[:, cols] = out
            return out * hid[layer, :, cols]

        last = live - 1
        slope_copy(0, last).wait()
        hidden_copy(0, last).wait()

        def begin(chunk, total):
            cols = columns(chunk)
            g[0:length, cols] = g_in[:, cols].astype(f32)
            g[length:rows, cols] = ga_in[:, cols].astype(f32)
            return total + into_taps(last, cols, g[:, cols])

        total = lax.fori_loop(0, chunks, begin, zero)

        def coefficients(layer, total):
            rms = scal[layer]
            coef[0] = rms
            coef[1] = -rms * rms * rms * (row_total(total) / width)

        def through_rms(layer, cols):
            return g[:, cols] + (coef[0] * u[:, cols] + coef[1] * hid[layer, :, cols])

        def layer_step(step, total):
            layer = live - 1 - step
            coefficients(layer, total)
            slope_copy(0, layer - 1).wait()
            hidden_copy(0, layer - 1).wait()

            def one(chunk, total):
                cols = columns(chunk)
                grad = through_rms(layer, cols)
                g[:, cols] = grad
                return total + into_taps(layer - 1, cols, grad)

            return lax.fori_loop(0, chunks, one, zero)

        total = lax.fori_loop(0, live - 1, layer_step, total)
        coefficients(0, total)
        for copy in input_copies():
            copy.wait()

        def to_gate(chunk, total):
            cols = columns(chunk)
            grad = through_rms(0, cols)
            g[:, cols] = grad
            return total + grad * v_win[:, cols]

        total = row_total(lax.fori_loop(0, chunks, to_gate, zero))
        rx, rv, xv, gate = scal[4], scal[5], scal[6], scal[7]
        both = total * gate * (1.0 - gate) * (1.0 / math.sqrt(width)) * rx * rv
        mean = xv / width
        coef[0] = both
        coef[1] = -both * rx * rx * mean
        coef[2] = -both * rv * rv * mean
        coef[3] = gate

        def finish(chunk, carry):
            cols = columns(chunk)
            grad = g[0:length, cols]
            x = x_in[:, cols].astype(f32)
            v = v_win[0:length, cols]
            grad_x = grad + coef[0, 0:length] * v + coef[1, 0:length] * x
            grad_v = coef[3, 0:length] * grad + coef[0, 0:length] * x + coef[2, 0:length] * v
            grad_x = grad_x.astype(bf16)
            grad_send[:, cols] = grad_x
            halo_send[:, cols] = grad_x[0:HALO]
            gv[:, cols] = grad_v.astype(bf16)
            return carry

        lax.fori_loop(0, chunks, finish, 0)
        outs = (
            pltpu.make_async_copy(grad_send, grads_all.at[which], sems.at[3, 2]),
            pltpu.make_async_copy(gv, gv_all.at[which], sems.at[3, 3]),
        )
        for copy in outs:
            copy.start()
        for copy in outs:
            copy.wait()


def backward_map(info, near, near_halo, top, top_halo, x, x_after, v, v_after, taps, first, saved, previous):
    batches, length, width = x.shape
    rows = length + HALO
    layers = taps.shape[0]
    flat = [array for group in saved for array in group]
    some = pl.BlockSpec(memory_space=pl.ANY)
    extra = () if previous is None else previous
    operands = (info, near, near_halo, top, top_halo, x, x_after, v, v_after, taps, *flat, *extra)
    aliases = {} if previous is None else {len(operands) - 2: 2, len(operands) - 1: 3}
    return pl.pallas_call(
        functools.partial(backward_kernel, (first, len(saved), previous is not None)),
        out_shape=(
            jax.ShapeDtypeStruct((length, width), bf16),
            jax.ShapeDtypeStruct((HALO, width), bf16),
            jax.ShapeDtypeStruct((batches, length, width), bf16),
            jax.ShapeDtypeStruct((batches, length, width), bf16),
        ),
        in_specs=[pl.BlockSpec(memory_space=pltpu.SMEM)]
        + [some] * 8
        + [pl.BlockSpec(memory_space=pltpu.VMEM)]
        + [some] * (len(flat) + len(extra)),
        out_specs=[pl.BlockSpec(memory_space=pltpu.VMEM)] * 2 + [some] * 2,
        scratch_shapes=[
            pltpu.VMEM((layers, rows, width), f32),
            pltpu.VMEM((layers, rows, width), f32),
            pltpu.VMEM((8, rows, LANES), f32),
            pltpu.VMEM((rows, width), f32),
            pltpu.VMEM((rows, width), f32),
            pltpu.VMEM((rows, width), f32),
            pltpu.VMEM((rows, width), f32),
            pltpu.VMEM((4, rows, LANES), f32),
            pltpu.VMEM((length, width), bf16),
            pltpu.VMEM((HALO, width), bf16),
            pltpu.VMEM((length, width), bf16),
            pltpu.VMEM((HALO, width), bf16),
            pltpu.VMEM((length, width), bf16),
            pltpu.SemaphoreType.DMA((4, 5)),
        ],
        input_output_aliases=aliases,
        compiler_params=pltpu.CompilerParams(vmem_limit_bytes=44 * MIB),
        cost_estimate=pl.CostEstimate(flops=25 * layers * rows * width, bytes_accessed=14 * MIB, transcendentals=0),
        name="backward_map",
    )(*operands)


def pack_kernel(dest, gv_all, out, stacked):
    heads, width = 8, out.shape[-1]
    length = gv_all.shape[1]
    for head in range(heads):
        stacked[head * length : (head + 1) * length, :] = gv_all[0, :, head * width : (head + 1) * width]
    slots = out.shape[0]
    step = 256

    def one(tile, carry):
        at = pl.multiple_of(tile * step, step)
        slot = lax.broadcasted_iota(jnp.int32, (step, heads * length), 0) + at
        place = jnp.where(slot == dest[...], 1.0, 0.0).astype(bf16)
        out[pl.ds(at, step), :] = jnp.dot(
            place, stacked[...], preferred_element_type=f32
        ).astype(bf16)
        return carry

    lax.fori_loop(0, slots // step, one, 0)


def pack_values(batch, dest, gv_all, slots):
    batches, length, model = gv_all.shape
    feature = model // 8
    return pl.pallas_call(
        pack_kernel,
        out_shape=jax.ShapeDtypeStruct((slots, feature), bf16),
        grid=(1,),
        in_specs=[
            pl.BlockSpec(dest.shape, lambda i: (0, 0)),
            pl.BlockSpec((1, length, model), lambda i: (batch, 0, 0)),
        ],
        out_specs=pl.BlockSpec((slots, feature), lambda i: (0, 0)),
        scratch_shapes=[pltpu.VMEM((8 * length, feature), bf16)],
        compiler_params=pltpu.CompilerParams(vmem_limit_bytes=24 * MIB),
        cost_estimate=pl.CostEstimate(flops=2 * slots * 8 * length * feature, bytes_accessed=2 * MIB, transcendentals=0),
        name="pack_values",
    )(dest, gv_all)


def owner_kernel(has_table, got, head_of, row_of, weight, *refs):
    if has_table:
        table_in, refs = refs[0], refs[1:]
    table, spread, flat, place, sems = refs
    heads, row_width, feature = weight.shape
    slots = got.shape[0]
    copies = [
        pltpu.make_async_copy(
            weight.at[h], flat.at[:, pl.ds(h * feature, feature)], sems.at[h]
        )
        for h in range(heads)
    ]
    for copy in copies:
        copy.start()
    step = 128

    def expand(tile, carry):
        at = pl.ds(pl.multiple_of(tile * step, step), step)
        own = head_of[at, :]
        block = got[at, :]
        for h in range(heads):
            mask = jnp.broadcast_to(own == h, block.shape)
            spread[at, h * feature : (h + 1) * feature] = jnp.where(mask, block, jnp.zeros_like(block))
        return carry

    lax.fori_loop(0, slots // step, expand, 0)
    table_rows = table.shape[0]

    def mark(tile, carry):
        at = pl.multiple_of(tile * step, step)
        row = lax.broadcasted_iota(jnp.int32, (step, slots), 0) + at
        place[pl.ds(at, step), :] = jnp.where(row == row_of[...], 1.0, 0.0).astype(bf16)
        return carry

    lax.fori_loop(0, table_rows // step, mark, 0)
    for copy in copies:
        copy.wait()
    tile = 256

    def add(block, carry):
        at = pl.ds(pl.multiple_of(block * tile, tile), tile)
        rows = lax.dot_general(
            spread[...], flat[at, :], (((1,), (1,)), ((), ())), preferred_element_type=f32
        )
        total = jnp.dot(place[...], rows.astype(bf16), preferred_element_type=f32)
        if has_table:
            total = total + table_in[:, at]
        table[:, at] = total
        return carry

    lax.fori_loop(0, row_width // tile, add, 0)


def owner_add(table, got, head_of, row_of, weight):
    heads, row_width, feature = weight.shape
    slots = got.shape[0]
    vmem = pl.BlockSpec(memory_space=pltpu.VMEM)
    operands = [got, head_of, row_of, weight]
    specs = [vmem, vmem, vmem, pl.BlockSpec(memory_space=pl.ANY)]
    if table is not None:
        operands.append(table)
        specs.append(vmem)
    return pl.pallas_call(
        functools.partial(owner_kernel, table is not None),
        out_shape=jax.ShapeDtypeStruct((TABLE_DEV, row_width), f32),
        in_specs=specs,
        out_specs=vmem,
        scratch_shapes=[
            pltpu.VMEM((slots, heads * feature), bf16),
            pltpu.VMEM((row_width, heads * feature), bf16),
            pltpu.VMEM((TABLE_DEV, slots), bf16),
            pltpu.SemaphoreType.DMA((heads,)),
        ],
        compiler_params=pltpu.CompilerParams(vmem_limit_bytes=48 * MIB),
        cost_estimate=pl.CostEstimate(flops=2 * slots * row_width * (heads * feature + TABLE_DEV), bytes_accessed=18 * MIB, transcendentals=0),
        name="owner_add",
    )(*operands)


def slots_of(row_ids, owners, capacity):
    batches, length, heads = row_ids.shape
    ids = row_ids.transpose(0, 2, 1).reshape(batches, heads * length)
    owner = ids // TABLE_DEV
    local = ids - owner * TABLE_DEV
    head = jnp.arange(heads * length, dtype=jnp.int32) // length
    order = jnp.arange(heads * length, dtype=jnp.int32)
    ahead = (owner[:, None, :] == owner[:, :, None]) & (order[None, :] < order[:, None])
    rank = jnp.sum(ahead.astype(jnp.int32), -1)
    dest = owner * capacity + rank
    code = local * heads + head
    slot = jnp.arange(owners * capacity, dtype=jnp.int32)
    hit = dest[:, None, :] == slot[:, None]
    holds = jnp.sum(jnp.where(hit, code[:, None, :] + 1, 0), -1) - 1
    return dest, holds


def after(value, *others):
    return lax.optimization_barrier((value, *others))[0]


def shards(
    saved_inputs, memory, value_weight, conv_weight, norm_gain, layer_counts, row_ids, out_grad
):
    section = lax.axis_index("section")
    sections = lax.axis_size("section")
    owners = lax.axis_size("table")
    batches, length, width = out_grad.shape
    heads = memory.shape[3]
    capacity = 3 * length * heads // (2 * owners)
    slots = owners * capacity
    weight = value_weight[0]
    live = layer_counts[0]
    taps = conv_weight[0] * norm_gain[0][:, None, :]
    x = saved_inputs[0]
    is_top = section == sections - 1

    to_next = [(i, i + 1) for i in range(owners - 1)]
    to_last = [(i + 1, i) for i in range(owners - 1)]
    down = [(i + 1, i) for i in range(sections - 1)]
    down_halo = [
        ((i + 1) * owners + t + 1, i * owners + t)
        for i in range(sections - 1)
        for t in range(owners - 1)
    ]
    x_before = lax.ppermute(x[:, length - HALO :], "table", to_next)
    x_after = lax.ppermute(x[:, :HALO], "table", to_last)
    top_halo = lax.ppermute(out_grad[:, :HALO], "table", to_last)
    v = jnp.einsum("bthr,hrc->bthc", memory[0], weight, preferred_element_type=f32)
    v = v.reshape(batches, length, width)
    v_before = lax.ppermute(v[:, length - HALO :], "table", to_next)
    v_after = lax.ppermute(v[:, :HALO], "table", to_last)

    saved = []
    near = jnp.zeros((length, width), bf16)
    near_halo = jnp.zeros((HALO, width), bf16)
    outputs = None
    table = None
    head_of = row_of = dest = None
    ticks = batches + sections - 1
    grad_send = None
    for tick in range(ticks):
        if tick < batches:
            number = live.reshape(1)
            if tick > 0:
                number = after(number, grad_send)
            saved.append(
                forward_map(tick, number, x, x_before, x_after, v, v_before, v_after, taps)
            )
        if tick == 2:
            ids = after(row_ids[0], grad_send)
            dest, holds = slots_of(ids, owners, capacity)
            holds = holds.reshape(batches, owners, capacity).transpose(1, 0, 2)
            holds = lax.all_to_all(
                holds.reshape(owners, batches * capacity), "table", 0, 0, tiled=True
            )
            holds = holds.reshape(owners, batches, capacity).transpose(1, 0, 2)
            holds = holds.reshape(batches, slots)
            row_of = jnp.where(holds < 0, -1, holds // heads)
            head_of = jnp.where(holds < 0, -1, holds % heads)
        position = tick - (sections - 1 - section)
        which = jnp.clip(position, 0, batches - 1)
        active = (position >= 0) & (position < batches)
        info = jnp.stack([which, active, is_top, live]).astype(jnp.int32)
        first = max(0, tick - (sections - 1))
        grad_send, halo_send, *outputs = backward_map(
            info, near, near_halo, out_grad, top_halo, x, x_after, v, v_after, taps,
            first, saved[first : tick + 1], outputs,
        )
        if tick < ticks - 1:
            near = lax.ppermute(grad_send, "section", down)
            near_halo = lax.ppermute(halo_send, ("section", "table"), down_halo)
        batch = tick - (sections - 1)
        if batch >= 0:
            packed = pack_values(batch, dest[batch][None, :], outputs[1], slots)
            got = lax.all_to_all(packed, "table", 0, 0, tiled=True)
            table = owner_add(
                table, got, head_of[batch][:, None], row_of[batch][None, :], weight
            )
    return (outputs[0][None], table[None])


def solution(mesh):
    placed = (
        P("section", None, "table", None),
        P("section", None, "table", None, None),
        P("section", None, None, None),
        P("section", None, None, None),
        P("section", None, None),
        P("section"),
        P("section", None, "table", None),
        P(None, "table", None),
    )
    return jax.shard_map(
        shards,
        mesh=mesh,
        in_specs=placed,
        out_specs=(P("section", None, "table", None), P("section", "table", None)),
        check_vma=False,
    )
```

```python
import functools
import math

import jax
import jax.numpy as jnp
from jax import lax
from jax.experimental import pallas as pl
from jax.experimental.pallas import tpu as pltpu
from jax.sharding import PartitionSpec as P

TABLE_DEV = 1024
HALO = 16
EPS = 1e-06
LANES = 128
MIB = 1 << 20
UNROLL = (1, 2, 2, 2)
VMEM_LIMIT = 60 * MIB

f32 = jnp.float32
bf16 = jnp.bfloat16


def row_total(partial):
    return jnp.broadcast_to(jnp.sum(partial, -1, keepdims=True), partial.shape)


def columns(chunk):
    return pl.ds(pl.multiple_of(chunk * LANES, LANES), LANES)


def forward_kernel(
    batch, live_ref, xb, xm, xa, vb, vm, va, taps, order, hid_out, der_out, scal_out,
    x_win, v_win, hid, der, scal, rms_now, sems,
):
    width = xm.shape[-1]
    rows = x_win.shape[0]
    keep = rows - HALO
    chunks = width // LANES
    live = live_ref[0]
    length = xm.shape[-2]
    parts = ((xb, vb, 0, HALO), (xm, vm, HALO, length), (xa, va, HALO + length, HALO))
    loads = []
    for i, (x_part, v_part, at, size) in enumerate(parts):
        for j, (part, window) in enumerate(((x_part, x_win), (v_part, v_win))):
            loads.append(
                pltpu.make_async_copy(
                    part.at[batch], window.at[pl.ds(at, size)], sems.at[2 + j, i]
                )
            )
    for copy in loads:
        copy.start()
    for copy in loads:
        copy.wait()

    def load(chunk, sums):
        cols = columns(chunk)
        x = x_win[:, cols].astype(f32)
        v = v_win[:, cols]
        return sums[0] + x * x, sums[1] + v * v, sums[2] + x * v

    zero = jnp.zeros((rows, LANES), f32)
    xx, vv, xv = lax.fori_loop(0, chunks, load, (zero, zero, zero), unroll=UNROLL[0])
    xv = row_total(xv)
    rx = lax.rsqrt(row_total(xx) / width + EPS)
    rv = lax.rsqrt(row_total(vv) / width + EPS)
    gate = jax.nn.sigmoid(rx * rv * xv / math.sqrt(width))
    scal[4] = rx[HALO:]
    scal[5] = rv[HALO:]
    scal[6] = xv[HALO:]
    scal[7] = gate[HALO:]
    rms_now[...] = gate

    def mix(chunk, total):
        cols = columns(chunk)
        hidden = x_win[:, cols].astype(f32) + rms_now[...] * v_win[:, cols]
        hid[0, :, cols] = hidden
        return total + hidden * hidden

    total = lax.fori_loop(0, chunks, mix, zero, unroll=UNROLL[0])

    def hidden_copy(layer):
        return pltpu.make_async_copy(
            hid.at[layer, pl.ds(HALO, keep)], hid_out.at[layer], sems.at[0, layer]
        )

    def slope_copy(layer):
        return pltpu.make_async_copy(der.at[layer], der_out.at[layer], sems.at[1, layer])

    def layer_step(layer, total):
        hidden_copy(layer).start()
        rms = lax.rsqrt(row_total(total) / width + EPS)
        scal[layer] = rms[HALO:]
        rms_now[...] = rms

        def one(chunk, total):
            cols = columns(chunk)
            hidden = hid[layer, :, cols]
            unit = hidden * rms_now[...]
            mixed = taps[layer, 0:1, cols] * unit
            for k in range(1, 4):
                mixed = mixed + taps[layer, k : k + 1, cols] * pltpu.roll(unit, k, 0)
            sigma = 0.5 * jnp.tanh(0.5 * mixed) + 0.5
            silu = mixed * sigma
            der[layer, :, cols] = (sigma + silu * (1.0 - sigma))[HALO:]
            after = hidden + silu
            hid[layer + 1, :, cols] = after
            return total + after * after

        total = lax.fori_loop(0, chunks, one, zero, unroll=UNROLL[1])
        slope_copy(layer).start()
        return total

    lax.fori_loop(0, live, layer_step, total)
    out = pltpu.make_async_copy(scal, scal_out, sems.at[0, 4])
    out.start()

    def finish(layer, carry):
        hidden_copy(layer).wait()
        slope_copy(layer).wait()
        return carry

    lax.fori_loop(0, live, finish, 0)
    out.wait()


def forward_map(batch, live, x, x_before, x_after, v, v_before, v_after, taps, order):
    length, width = x.shape[1:]
    keep = length + HALO
    rows = keep + HALO
    layers = taps.shape[0]
    hbm = pl.BlockSpec(memory_space=pltpu.HBM)
    return pl.pallas_call(
        functools.partial(forward_kernel, batch),
        out_shape=(
            jax.ShapeDtypeStruct((layers, keep, width), f32),
            jax.ShapeDtypeStruct((layers, keep, width), f32),
            jax.ShapeDtypeStruct((8, keep, LANES), f32),
        ),
        in_specs=[pl.BlockSpec(memory_space=pltpu.SMEM)]
        + [hbm] * 6
        + [pl.BlockSpec(memory_space=pltpu.VMEM), pl.BlockSpec(memory_space=pltpu.SMEM)],
        out_specs=[hbm] * 3,
        scratch_shapes=[
            pltpu.VMEM((rows, width), bf16),
            pltpu.VMEM((rows, width), f32),
            pltpu.VMEM((layers + 1, rows, width), f32),
            pltpu.VMEM((layers, keep, width), f32),
            pltpu.VMEM((8, keep, LANES), f32),
            pltpu.VMEM((rows, LANES), f32),
            pltpu.SemaphoreType.DMA((4, layers + 1)),
        ],
        compiler_params=pltpu.CompilerParams(vmem_limit_bytes=VMEM_LIMIT),
        cost_estimate=pl.CostEstimate(
            flops=30 * layers * rows * width,
            bytes_accessed=16 * MIB,
            transcendentals=layers * rows * width,
        ),
        name="forward_map",
    )(live, x_before, x, x_after, v_before, v, v_after, taps, order)


def backward_kernel(
    held, info, near, near_halo, top, top_halo, x_all, xa_all, v_all, va_all, taps, *refs,
):
    saved = [refs[3 * i : 3 * i + 3] for i in range(held[1])]
    refs = refs[3 * held[1] :]
    if held[2]:
        refs = refs[2:]
    (
        grad_send, halo_send, grads_all, gv_all, order_out,
        hid, der, scal, x_win, v_win, g, u, coef, x_in, xa_in, g_in, ga_in, gv, sems,
    ) = refs
    which = info[0]
    active = info[1]
    is_top = info[2]
    live = info[3]
    length, width = grad_send.shape
    rows = g.shape[0]
    chunks = width // LANES
    first, count = held[0], held[1]
    order_out[0] = 0

    def scal_copy(i):
        return pltpu.make_async_copy(saved[i][2], scal, sems.at[2, 0])

    def hidden_copy(i, layer):
        return pltpu.make_async_copy(saved[i][0].at[layer], hid.at[layer], sems.at[0, layer])

    def slope_copy(i, layer):
        return pltpu.make_async_copy(saved[i][1].at[layer], der.at[layer], sems.at[1, layer])

    def input_copies():
        return (
            pltpu.make_async_copy(x_all.at[which], x_in, sems.at[2, 1]),
            pltpu.make_async_copy(xa_all.at[which], xa_in, sems.at[2, 2]),
            pltpu.make_async_copy(v_all.at[which], v_win.at[pl.ds(0, length)], sems.at[2, 3]),
            pltpu.make_async_copy(va_all.at[which], v_win.at[pl.ds(length, HALO)], sems.at[2, 4]),
        )

    def grad_copies(source, source_halo):
        return (
            pltpu.make_async_copy(source, g_in, sems.at[3, 0]),
            pltpu.make_async_copy(source_halo, ga_in, sems.at[3, 1]),
        )

    @pl.when(active == 1)
    def _():
        @pl.when(is_top == 1)
        def _():
            for copy in grad_copies(top.at[which], top_halo.at[which]):
                copy.start()

        @pl.when(is_top == 0)
        def _():
            for copy in grad_copies(near, near_halo):
                copy.start()

        for i in range(count):
            @pl.when(which == first + i)
            def _():
                scal_copy(i).start()

                def begin(step, carry):
                    layer = live - 1 - step
                    slope_copy(i, layer).start()
                    hidden_copy(i, layer).start()
                    return carry

                lax.fori_loop(0, live, begin, 0)

        for copy in input_copies():
            copy.start()

        zero = jnp.zeros((rows, LANES), f32)
        for copy in grad_copies(near, near_halo):
            copy.wait()
        scal_copy(0).wait()

        def into_taps(layer, cols, grad):
            slope = grad * der[layer, :, cols]
            out = taps[layer, 0:1, cols] * slope
            for k in range(1, 4):
                out = out + taps[layer, k : k + 1, cols] * pltpu.roll(slope, rows - k, 0)
            u[:, cols] = out
            return out * hid[layer, :, cols]

        last = live - 1
        slope_copy(0, last).wait()
        hidden_copy(0, last).wait()

        def begin(chunk, total):
            cols = columns(chunk)
            g[0:length, cols] = g_in[:, cols].astype(f32)
            g[length:rows, cols] = ga_in[:, cols].astype(f32)
            return total + into_taps(last, cols, g[:, cols])

        total = lax.fori_loop(0, chunks, begin, zero, unroll=UNROLL[2])

        def coefficients(layer, total):
            rms = scal[layer]
            coef[0] = rms
            coef[1] = -rms * rms * rms * (row_total(total) / width)

        def through_rms(layer, cols):
            return g[:, cols] + (coef[0] * u[:, cols] + coef[1] * hid[layer, :, cols])

        def layer_step(step, total):
            layer = live - 1 - step
            coefficients(layer, total)
            slope_copy(0, layer - 1).wait()
            hidden_copy(0, layer - 1).wait()

            def one(chunk, total):
                cols = columns(chunk)
                grad = through_rms(layer, cols)
                g[:, cols] = grad
                return total + into_taps(layer - 1, cols, grad)

            return lax.fori_loop(0, chunks, one, zero, unroll=UNROLL[2])

        total = lax.fori_loop(0, live - 1, layer_step, total)
        coefficients(0, total)
        for copy in input_copies():
            copy.wait()

        def to_gate(chunk, total):
            cols = columns(chunk)
            grad = through_rms(0, cols)
            g[:, cols] = grad
            return total + grad * v_win[:, cols]

        total = row_total(lax.fori_loop(0, chunks, to_gate, zero, unroll=UNROLL[3]))
        rx, rv, xv, gate = scal[4], scal[5], scal[6], scal[7]
        both = total * gate * (1.0 - gate) * (1.0 / math.sqrt(width)) * rx * rv
        mean = xv / width
        coef[0] = both
        coef[1] = -both * rx * rx * mean
        coef[2] = -both * rv * rv * mean
        coef[3] = gate

        def finish(chunk, carry):
            cols = columns(chunk)
            grad = g[0:length, cols]
            x = x_in[:, cols].astype(f32)
            v = v_win[0:length, cols]
            grad_x = grad + coef[0, 0:length] * v + coef[1, 0:length] * x
            grad_v = coef[3, 0:length] * grad + coef[0, 0:length] * x + coef[2, 0:length] * v
            grad_x = grad_x.astype(bf16)
            grad_send[:, cols] = grad_x
            halo_send[:, cols] = grad_x[0:HALO]
            gv[:, cols] = grad_v.astype(bf16)
            return carry

        lax.fori_loop(0, chunks, finish, 0, unroll=UNROLL[3])
        outs = (
            pltpu.make_async_copy(grad_send, grads_all.at[which], sems.at[3, 2]),
            pltpu.make_async_copy(gv, gv_all.at[which], sems.at[3, 3]),
        )
        for copy in outs:
            copy.start()
        for copy in outs:
            copy.wait()


def backward_map(info, near, near_halo, top, top_halo, x, x_after, v, v_after, taps, first, saved, previous):
    batches, length, width = x.shape
    rows = length + HALO
    layers = taps.shape[0]
    flat = [array for group in saved for array in group]
    some = pl.BlockSpec(memory_space=pl.ANY)
    hbm = pl.BlockSpec(memory_space=pltpu.HBM)
    extra = () if previous is None else previous
    operands = (info, near, near_halo, top, top_halo, x, x_after, v, v_after, taps, *flat, *extra)
    aliases = {} if previous is None else {len(operands) - 2: 2, len(operands) - 1: 3}
    return pl.pallas_call(
        functools.partial(backward_kernel, (first, len(saved), previous is not None)),
        out_shape=(
            jax.ShapeDtypeStruct((length, width), bf16),
            jax.ShapeDtypeStruct((HALO, width), bf16),
            jax.ShapeDtypeStruct((batches, length, width), bf16),
            jax.ShapeDtypeStruct((batches, length, width), bf16),
            jax.ShapeDtypeStruct((1,), jnp.int32),
        ),
        in_specs=[pl.BlockSpec(memory_space=pltpu.SMEM)]
        + [some] * 2
        + [hbm] * 6
        + [pl.BlockSpec(memory_space=pltpu.VMEM)]
        + [hbm] * (len(flat) + len(extra)),
        out_specs=[pl.BlockSpec(memory_space=pltpu.VMEM)] * 2
        + [hbm] * 2
        + [pl.BlockSpec(memory_space=pltpu.SMEM)],
        scratch_shapes=[
            pltpu.VMEM((layers, rows, width), f32),
            pltpu.VMEM((layers, rows, width), f32),
            pltpu.VMEM((8, rows, LANES), f32),
            pltpu.VMEM((rows, width), f32),
            pltpu.VMEM((rows, width), f32),
            pltpu.VMEM((rows, width), f32),
            pltpu.VMEM((rows, width), f32),
            pltpu.VMEM((4, rows, LANES), f32),
            pltpu.VMEM((length, width), bf16),
            pltpu.VMEM((HALO, width), bf16),
            pltpu.VMEM((length, width), bf16),
            pltpu.VMEM((HALO, width), bf16),
            pltpu.VMEM((length, width), bf16),
            pltpu.SemaphoreType.DMA((4, 5)),
        ],
        input_output_aliases=aliases,
        compiler_params=pltpu.CompilerParams(vmem_limit_bytes=VMEM_LIMIT),
        cost_estimate=pl.CostEstimate(flops=25 * layers * rows * width, bytes_accessed=14 * MIB, transcendentals=0),
        name="backward_map",
    )(*operands)


def pack_kernel(dest, gv_all, order, arrived, out, stacked):
    heads, width = 8, out.shape[-1]
    length = gv_all.shape[1]
    for head in range(heads):
        stacked[head * length : (head + 1) * length, :] = gv_all[0, :, head * width : (head + 1) * width]
    slots = out.shape[0]
    step = 256

    def one(tile, carry):
        at = pl.multiple_of(tile * step, step)
        slot = lax.broadcasted_iota(jnp.int32, (step, heads * length), 0) + at
        place = jnp.where(slot == dest[...], 1.0, 0.0).astype(bf16)
        out[pl.ds(at, step), :] = jnp.dot(
            place, stacked[...], preferred_element_type=f32
        ).astype(bf16)
        return carry

    lax.fori_loop(0, slots // step, one, 0)


def pack_values(batch, dest, gv_all, slots, order, arrived):
    batches, length, model = gv_all.shape
    feature = model // 8
    return pl.pallas_call(
        pack_kernel,
        out_shape=jax.ShapeDtypeStruct((slots, feature), bf16),
        grid=(1,),
        in_specs=[
            pl.BlockSpec(dest.shape, lambda i: (0, 0)),
            pl.BlockSpec((1, length, model), lambda i: (batch, 0, 0)),
            pl.BlockSpec(memory_space=pltpu.SMEM),
            pl.BlockSpec(memory_space=pl.ANY),
        ],
        out_specs=pl.BlockSpec((slots, feature), lambda i: (0, 0)),
        scratch_shapes=[pltpu.VMEM((8 * length, feature), bf16)],
        compiler_params=pltpu.CompilerParams(vmem_limit_bytes=VMEM_LIMIT),
        cost_estimate=pl.CostEstimate(flops=2 * slots * 8 * length * feature, bytes_accessed=2 * MIB, transcendentals=0),
        name="pack_values",
    )(dest, gv_all, order, arrived)


def owner_kernel(batch, has_table, got, place_of, row_of, groups, order, weight, *refs):
    if has_table:
        table_in, refs = refs[0], refs[1:]
    table, order_out, sorted_in, rows, place, flat, total, sems = refs
    heads, row_width, feature = weight.shape
    table_rows = table.shape[0]
    slots = got.shape[0]
    room = place.shape[1]
    order_out[0] = 0
    copies = [pltpu.make_async_copy(weight.at[h], flat.at[h], sems.at[h]) for h in range(heads)]
    for copy in copies:
        copy.start()
    if has_table:
        table_copy = pltpu.make_async_copy(table_in, total, sems.at[heads])
        table_copy.start()
    step = 128

    def sort(tile, carry):
        at = pl.multiple_of(tile * step, step)
        slot = lax.broadcasted_iota(jnp.int32, (step, slots), 0) + at
        pick = jnp.where(slot == place_of[batch : batch + 1, :], 1.0, 0.0).astype(bf16)
        sorted_in[pl.ds(at, step), :] = jnp.dot(
            pick, got[...], preferred_element_type=f32
        ).astype(bf16)
        rows[pl.ds(at, step), :] = jnp.zeros((step, row_width), bf16)
        return carry

    lax.fori_loop(0, room // step, sort, 0)

    def mark(tile, carry):
        at = pl.multiple_of(tile * step, step)
        row = lax.broadcasted_iota(jnp.int32, (step, room), 0) + at
        place[pl.ds(at, step), :] = jnp.where(
            row == row_of[batch : batch + 1, :], 1.0, 0.0
        ).astype(bf16)
        return carry

    lax.fori_loop(0, table_rows // step, mark, 0)

    for h in range(heads):
        copies[h].wait()

        def multiply(tile, carry):
            at = pl.ds(pl.multiple_of(groups[batch, h] + tile * step, 16), step)
            rows[at, :] = lax.dot_general(
                sorted_in[at, :], flat[h], (((1,), (1,)), ((), ())), preferred_element_type=f32
            ).astype(bf16)
            return carry

        lax.fori_loop(0, groups[batch, heads + h], multiply, 0)
    if has_table:
        table_copy.wait()
    tile = 256
    outs = []
    for block in range(row_width // tile):
        cols = pl.ds(block * tile, tile)
        part = jnp.dot(place[...], rows[0:room, cols], preferred_element_type=f32)
        if has_table:
            part = part + total[:, cols]
        total[:, cols] = part
        outs.append(
            pltpu.make_async_copy(
                total.at[:, cols], table.at[:, cols], sems.at[heads + 1 + block]
            )
        )
        outs[-1].start()
    for copy in outs:
        copy.wait()


def owner_add(batch, table, got, place_of, row_of, groups, weight, order):
    heads, row_width, feature = weight.shape
    slots = got.shape[0]
    room = row_of.shape[1]
    vmem = pl.BlockSpec(memory_space=pltpu.VMEM)
    hbm = pl.BlockSpec(memory_space=pltpu.HBM)
    smem = pl.BlockSpec(memory_space=pltpu.SMEM)
    operands = [got, place_of, row_of, groups, order, weight]
    specs = [vmem, vmem, vmem, smem, smem, hbm]
    if table is not None:
        operands.append(table)
        specs.append(hbm)
    return pl.pallas_call(
        functools.partial(owner_kernel, batch, table is not None),
        out_shape=(
            jax.ShapeDtypeStruct((TABLE_DEV, row_width), f32),
            jax.ShapeDtypeStruct((1,), jnp.int32),
        ),
        in_specs=specs,
        out_specs=(hbm, smem),
        scratch_shapes=[
            pltpu.VMEM((room + 128, feature), bf16),
            pltpu.VMEM((room + 128, row_width), bf16),
            pltpu.VMEM((TABLE_DEV, room), bf16),
            pltpu.VMEM((heads, row_width, feature), bf16),
            pltpu.VMEM((TABLE_DEV, row_width), f32),
            pltpu.SemaphoreType.DMA((heads + 5,)),
        ],
        compiler_params=pltpu.CompilerParams(vmem_limit_bytes=VMEM_LIMIT),
        cost_estimate=pl.CostEstimate(
            flops=6 * slots * row_width * TABLE_DEV, bytes_accessed=18 * MIB, transcendentals=0
        ),
        name="owner_add",
    )(*operands)


def slots_of(row_ids, owners, capacity):
    batches, length, heads = row_ids.shape
    ids = row_ids.transpose(0, 2, 1).reshape(batches, heads * length)
    owner = ids // TABLE_DEV
    local = ids - owner * TABLE_DEV
    head = jnp.arange(heads * length, dtype=jnp.int32) // length
    order = jnp.arange(heads * length, dtype=jnp.int32)
    ahead = (owner[:, None, :] == owner[:, :, None]) & (order[None, :] < order[:, None])
    rank = jnp.sum(ahead.astype(jnp.int32), -1)
    dest = owner * capacity + rank
    code = local * heads + head
    slot = jnp.arange(owners * capacity, dtype=jnp.int32)
    hit = dest[:, None, :] == slot[:, None]
    holds = jnp.sum(jnp.where(hit, code[:, None, :] + 1, 0), -1) - 1
    return dest, holds


def groups_of(holds, heads):
    batches, slots = holds.shape
    room = -(-(slots + 15 * heads) // 128) * 128
    valid = holds >= 0
    head = jnp.where(valid, holds % heads, -1)
    member = head[..., None] == jnp.arange(heads, dtype=jnp.int32)
    order = jnp.arange(slots, dtype=jnp.int32)
    below = (order[None, :] < order[:, None]).astype(bf16)
    rank = jnp.einsum("ij,bjh->bih", below, member.astype(bf16), preferred_element_type=f32)
    counts = jnp.sum(member.astype(jnp.int32), 1)
    padded = (counts + 15) // 16 * 16
    number = jnp.arange(heads, dtype=jnp.int32)
    starts = jnp.sum(jnp.where(number[None, :] < number[:, None], padded[:, None, :], 0), -1)
    place = jnp.sum(jnp.where(member, rank.astype(jnp.int32) + starts[:, None, :] + 1, 0), -1) - 1
    spot = jnp.arange(room, dtype=jnp.int32)
    hit = place[:, None, :] == spot[:, None]
    row = jnp.sum(jnp.where(hit, (holds // heads)[:, None, :] + 1, 0), -1) - 1
    groups = jnp.concatenate([starts, (counts + 127) // 128], 1)
    return place, row, groups


def shards(
    saved_inputs, memory, value_weight, conv_weight, norm_gain, layer_counts, row_ids, out_grad
):
    section = lax.axis_index("section")
    sections = lax.axis_size("section")
    owners = lax.axis_size("table")
    batches, length, width = out_grad.shape
    heads = memory.shape[3]
    capacity = 3 * length * heads // (2 * owners)
    slots = owners * capacity
    weight = value_weight[0]
    live = layer_counts[0]
    taps = conv_weight[0] * norm_gain[0][:, None, :]
    x = saved_inputs[0]
    is_top = section == sections - 1

    to_next = [(i, i + 1) for i in range(owners - 1)]
    to_last = [(i + 1, i) for i in range(owners - 1)]
    down = [(i + 1, i) for i in range(sections - 1)]
    down_halo = [
        ((i + 1) * owners + t + 1, i * owners + t)
        for i in range(sections - 1)
        for t in range(owners - 1)
    ]
    x_before = lax.ppermute(x[:, length - HALO :], "table", to_next)
    x_after = lax.ppermute(x[:, :HALO], "table", to_last)
    top_halo = lax.ppermute(out_grad[:, :HALO], "table", to_last)
    v = jnp.einsum("bthr,hrc->bthc", memory[0], weight, preferred_element_type=f32)
    v = v.reshape(batches, length, width)
    v_before = lax.ppermute(v[:, length - HALO :], "table", to_next)
    v_after = lax.ppermute(v[:, :HALO], "table", to_last)

    saved = []
    near = jnp.zeros((length, width), bf16)
    near_halo = jnp.zeros((HALO, width), bf16)
    outputs = table = dest = holds = place_of = row_of = groups = got = None
    order = jnp.zeros((1,), jnp.int32)
    ticks = batches + sections - 1
    for tick in range(ticks):
        if tick < batches:
            saved.append(
                forward_map(
                    tick, live.reshape(1), x, x_before, x_after, v, v_before, v_after, taps, order
                )
            )
        position = tick - (sections - 1 - section)
        which = jnp.clip(position, 0, batches - 1)
        active = (position >= 0) & (position < batches)
        info = jnp.stack([which, active, is_top, live]).astype(jnp.int32)
        first = max(0, tick - (sections - 1))
        grad_send, halo_send, *outputs, order = backward_map(
            info, near, near_halo, out_grad, top_halo, x, x_after, v, v_after, taps,
            first, saved[first : tick + 1], outputs,
        )
        if tick < ticks - 1:
            near = lax.ppermute(grad_send, "section", down)
            near_halo = lax.ppermute(halo_send, ("section", "table"), down_halo)
        if tick == 0:
            dest, holds = slots_of(row_ids[0] + order, owners, capacity)
            holds = holds.reshape(batches, owners, capacity).transpose(1, 0, 2)
            holds = holds.reshape(owners, batches * capacity)
        if tick == 1:
            holds = lax.all_to_all(holds + order, "table", 0, 0, tiled=True)
            holds = holds.reshape(owners, batches, capacity).transpose(1, 0, 2)
            holds = holds.reshape(batches, slots)
        if tick == 2:
            place_of, row_of, groups = groups_of(holds + order, heads)
        batch = tick - (sections - 1)
        if batch >= 0:
            token = order
            if got is not None:
                table, token = owner_add(
                    batch - 1, table, got, place_of, row_of, groups, weight, order
                )
            packed = pack_values(
                batch, dest[batch][None, :], outputs[1], slots, token, near_halo
            )
            got = lax.all_to_all(packed, "table", 0, 0, tiled=True)
    table, _ = owner_add(batches - 1, table, got, place_of, row_of, groups, weight, order)
    return (outputs[0][None], table[None])


def solution(mesh):
    placed = (
        P("section", None, "table", None),
        P("section", None, "table", None, None),
        P("section", None, None, None),
        P("section", None, None, None),
        P("section", None, None),
        P("section"),
        P("section", None, "table", None),
        P(None, "table", None),
    )
    return jax.shard_map(
        shards,
        mesh=mesh,
        in_specs=placed,
        out_specs=(P("section", None, "table", None), P("section", "table", None)),
        check_vma=False,
    )
```

```python
import functools
import math

import jax
import jax.numpy as jnp
from jax import lax
from jax.experimental import pallas as pl
from jax.experimental.pallas import tpu as pltpu
from jax.sharding import PartitionSpec as P

TABLE_DEV = 1024
HALO = 16
EPS = 1e-06
LANES = 128
STEP = 512
SPLIT = 4
MIB = 1 << 20
VMEM_LIMIT = 60 * MIB

f32 = jnp.float32
bf16 = jnp.bfloat16


def row_total(partial):
    return jnp.broadcast_to(jnp.sum(partial, -1, keepdims=True), partial.shape)


def columns(chunk):
    return pl.ds(pl.multiple_of(chunk * STEP, STEP), STEP)


def wide(narrow):
    return jnp.concatenate([narrow] * (STEP // LANES), 1)


def fold(chunk):
    return sum(chunk[:, i : i + LANES] for i in range(0, STEP, LANES))


def forward_kernel(
    batch, live_ref, xb, xm, xa, vb, vm, va, taps, order, hid_out, der_out, scal_out,
    x_win, v_win, hid, der, scal, rms_now, sems,
):
    width = xm.shape[-1]
    rows = x_win.shape[0]
    keep = rows - HALO
    chunks = width // STEP
    live = live_ref[0]
    length = xm.shape[-2]
    parts = ((xb, vb, 0, HALO), (xm, vm, HALO, length), (xa, va, HALO + length, HALO))
    loads = []
    for q in range(SPLIT):
        cols = pl.ds(q * (width // SPLIT), width // SPLIT)
        loads.append([])
        for i, (x_part, v_part, at, size) in enumerate(parts):
            for j, (part, window) in enumerate(((x_part, x_win), (v_part, v_win))):
                loads[q].append(
                    pltpu.make_async_copy(
                        part.at[batch, :, cols],
                        window.at[pl.ds(at, size), cols],
                        sems.at[2 + 3 * j + i, q],
                    )
                )
                loads[q][-1].start()

    def load(chunk, sums):
        cols = columns(chunk)
        x = x_win[:, cols].astype(f32)
        v = v_win[:, cols]
        return sums[0] + fold(x * x), sums[1] + fold(v * v), sums[2] + fold(x * v)

    zero = jnp.zeros((rows, LANES), f32)
    sums = (zero, zero, zero)
    for q in range(SPLIT):
        for copy in loads[q]:
            copy.wait()
        sums = lax.fori_loop(q * chunks // SPLIT, (q + 1) * chunks // SPLIT, load, sums)
    xx, vv, xv = sums
    xv = row_total(xv)
    rx = lax.rsqrt(row_total(xx) / width + EPS)
    rv = lax.rsqrt(row_total(vv) / width + EPS)
    gate = jax.nn.sigmoid(rx * rv * xv / math.sqrt(width))
    scal[4] = rx[HALO:]
    scal[5] = rv[HALO:]
    scal[6] = xv[HALO:]
    scal[7] = gate[HALO:]
    rms_now[...] = gate

    def mix(chunk, total):
        cols = columns(chunk)
        hidden = x_win[:, cols].astype(f32) + wide(rms_now[...]) * v_win[:, cols]
        hid[0, :, cols] = hidden
        return total + fold(hidden * hidden)

    total = lax.fori_loop(0, chunks, mix, zero)

    def hidden_copy(layer):
        return pltpu.make_async_copy(
            hid.at[layer, pl.ds(HALO, keep)], hid_out.at[layer], sems.at[0, layer]
        )

    def slope_copy(layer):
        return pltpu.make_async_copy(der.at[layer], der_out.at[layer], sems.at[1, layer])

    def layer_step(layer, total):
        hidden_copy(layer).start()
        rms = lax.rsqrt(row_total(total) / width + EPS)
        scal[layer] = rms[HALO:]
        rms_now[...] = rms

        def one(chunk, total):
            cols = columns(chunk)
            hidden = hid[layer, :, cols]
            unit = hidden * wide(rms_now[...])
            mixed = taps[layer, 0:1, cols] * unit
            for k in range(1, 4):
                mixed = mixed + taps[layer, k : k + 1, cols] * pltpu.roll(unit, k, 0)
            bend = jnp.tanh(mixed)
            rise = 1.0 + bend
            silu = mixed * rise
            der[layer, :, cols] = (rise + silu * (1.0 - bend))[HALO:]
            after = hidden + silu
            hid[layer + 1, :, cols] = after
            return total + fold(after * after)

        total = lax.fori_loop(0, chunks, one, zero)
        slope_copy(layer).start()
        return total

    lax.fori_loop(0, live, layer_step, total)
    out = pltpu.make_async_copy(scal, scal_out, sems.at[0, 4])
    out.start()

    def finish(layer, carry):
        hidden_copy(layer).wait()
        slope_copy(layer).wait()
        return carry

    lax.fori_loop(0, live, finish, 0)
    out.wait()


def forward_map(batch, live, x, x_before, x_after, v, v_before, v_after, taps, order):
    length, width = x.shape[1:]
    keep = length + HALO
    rows = keep + HALO
    layers = taps.shape[0]
    hbm = pl.BlockSpec(memory_space=pltpu.HBM)
    return pl.pallas_call(
        functools.partial(forward_kernel, batch),
        out_shape=(
            jax.ShapeDtypeStruct((layers, keep, width), f32),
            jax.ShapeDtypeStruct((layers, keep, width), f32),
            jax.ShapeDtypeStruct((8, keep, LANES), f32),
        ),
        in_specs=[pl.BlockSpec(memory_space=pltpu.SMEM)]
        + [hbm] * 6
        + [pl.BlockSpec(memory_space=pltpu.VMEM), pl.BlockSpec(memory_space=pltpu.SMEM)],
        out_specs=[hbm] * 3,
        scratch_shapes=[
            pltpu.VMEM((rows, width), bf16),
            pltpu.VMEM((rows, width), f32),
            pltpu.VMEM((layers + 1, rows, width), f32),
            pltpu.VMEM((layers, keep, width), f32),
            pltpu.VMEM((8, keep, LANES), f32),
            pltpu.VMEM((rows, LANES), f32),
            pltpu.SemaphoreType.DMA((8, layers + 1)),
        ],
        compiler_params=pltpu.CompilerParams(vmem_limit_bytes=VMEM_LIMIT),
        cost_estimate=pl.CostEstimate(
            flops=30 * layers * rows * width,
            bytes_accessed=16 * MIB,
            transcendentals=layers * rows * width,
        ),
        name="forward_map",
    )(live, x_before, x, x_after, v_before, v, v_after, taps, order)


def backward_kernel(
    held, info, near, near_halo, top, top_halo, x_all, xa_all, v_all, va_all, taps, *refs,
):
    saved = [refs[3 * i : 3 * i + 3] for i in range(held[1])]
    refs = refs[3 * held[1] :]
    if held[2]:
        refs = refs[2:]
    (
        grad_send, halo_send, grads_all, gv_all, order_out,
        hid, der, scal, v_in, g, u, coef, x_in, g_in, ga_in, gx, gv, sems,
    ) = refs
    which = info[0]
    active = info[1]
    is_top = info[2]
    live = info[3]
    length, width = grad_send.shape
    rows = g.shape[0]
    chunks = width // STEP
    quarter = width // SPLIT
    first, count = held[0], held[1]
    order_out[0] = 0

    def part(q):
        return pl.ds(pl.multiple_of(q * quarter, quarter), quarter)

    def scal_copy(i):
        return pltpu.make_async_copy(saved[i][2], scal, sems.at[2, 0])

    def layer_copies(i, layer, q):
        cols = part(q)
        return (
            pltpu.make_async_copy(
                saved[i][1].at[layer, :, cols], der.at[layer, :, cols], sems.at[1, 4 * layer + q]
            ),
            pltpu.make_async_copy(
                saved[i][0].at[layer, :, cols], hid.at[layer, :, cols], sems.at[0, 4 * layer + q]
            ),
        )

    def input_copies():
        return (
            pltpu.make_async_copy(x_all.at[which], x_in, sems.at[2, 1]),
            pltpu.make_async_copy(v_all.at[which], v_in, sems.at[2, 3]),
        )

    def grad_copies(source, source_halo):
        return (
            pltpu.make_async_copy(source, g_in, sems.at[3, 0]),
            pltpu.make_async_copy(source_halo, ga_in, sems.at[3, 1]),
        )

    @pl.when(active == 1)
    def _():
        @pl.when(is_top == 1)
        def _():
            for copy in grad_copies(top.at[which], top_halo.at[which]):
                copy.start()

        @pl.when(is_top == 0)
        def _():
            for copy in grad_copies(near, near_halo):
                copy.start()

        for i in range(count):
            @pl.when(which == first + i)
            def _():
                def begin(step, carry):
                    layer = live - 1 - step
                    for q in range(SPLIT):
                        for copy in layer_copies(i, layer, q):
                            copy.start()
                    return carry

                begin(0, 0)
                scal_copy(i).start()
                lax.fori_loop(1, live, begin, 0)

        for copy in input_copies():
            copy.start()

        for copy in grad_copies(near, near_halo):
            copy.wait()

        def into_taps(layer, cols, grad):
            size = grad.shape[0]
            slope = grad * der[layer, 0:size, cols]
            out = taps[layer, 0:1, cols] * slope
            for k in range(1, 4):
                out = out + taps[layer, k : k + 1, cols] * pltpu.roll(slope, size - k, 0)
            u[0:size, cols] = out
            return fold(out * hid[layer, 0:size, cols])

        last = live - 1
        total = jnp.zeros((rows, LANES), f32)
        for q in range(SPLIT):
            for copy in layer_copies(0, last, q):
                copy.wait()

            def start(chunk, total):
                cols = columns(chunk)
                g[0:length, cols] = g_in[:, cols].astype(f32)
                g[length:rows, cols] = ga_in[:, cols].astype(f32)
                return total + into_taps(last, cols, g[:, cols])

            total = lax.fori_loop(q * chunks // SPLIT, (q + 1) * chunks // SPLIT, start, total)
        scal_copy(0).wait()

        def coefficients(layer, total):
            size = total.shape[0]
            rms = scal[layer, 0:size]
            coef[0, 0:size] = rms
            coef[1, 0:size] = -rms * rms * rms * (row_total(total) / width)

        def through_rms(layer, cols, size):
            return g[0:size, cols] + (
                wide(coef[0, 0:size]) * u[0:size, cols]
                + wide(coef[1, 0:size]) * hid[layer, 0:size, cols]
            )

        def layer_step(size, step, total):
            layer = live - 1 - step
            coefficients(layer, total)
            for q in range(SPLIT):
                for copy in layer_copies(0, layer - 1, q):
                    copy.wait()

            def one(chunk, total):
                cols = columns(chunk)
                grad = through_rms(layer, cols, size)
                g[0:size, cols] = grad
                return total + into_taps(layer - 1, cols, grad)

            return lax.fori_loop(0, chunks, one, jnp.zeros((size, LANES), f32))

        total = lax.fori_loop(
            0, jnp.minimum(live - 1, 1), functools.partial(layer_step, rows), total
        )
        fewer = rows - HALO // 2
        total = lax.fori_loop(
            1, live - 1, functools.partial(layer_step, fewer), total[0:fewer]
        )
        coefficients(0, total[0:length])
        for copy in input_copies():
            copy.wait()

        def to_gate(chunk, total):
            cols = columns(chunk)
            grad = through_rms(0, cols, length)
            g[0:length, cols] = grad
            return total + fold(grad * v_in[:, cols])

        total = row_total(lax.fori_loop(0, chunks, to_gate, jnp.zeros((length, LANES), f32)))
        rx, rv, xv, gate = (scal[i, 0:length] for i in range(4, 8))
        both = total * gate * (1.0 - gate) * (1.0 / math.sqrt(width)) * rx * rv
        mean = xv / width
        coef[0, 0:length] = both
        coef[1, 0:length] = -both * rx * rx * mean
        coef[2, 0:length] = -both * rv * rv * mean
        coef[3, 0:length] = gate

        def finish(chunk, carry):
            cols = columns(chunk)
            grad = g[0:length, cols]
            x = x_in[:, cols].astype(f32)
            v = v_in[:, cols]
            cross = wide(coef[0, 0:length])
            grad_x = grad + cross * v + wide(coef[1, 0:length]) * x
            grad_v = wide(coef[3, 0:length]) * grad + cross * x + wide(coef[2, 0:length]) * v
            gx[:, cols] = grad_x.astype(bf16)
            gv[:, cols] = grad_v.astype(bf16)
            return carry

        outs = []
        for q in range(SPLIT):
            lax.fori_loop(q * chunks // SPLIT, (q + 1) * chunks // SPLIT, finish, 0)
            cols = part(q)
            for i, (source, target) in enumerate((
                (gx.at[:, cols], grad_send.at[:, cols]),
                (gx.at[pl.ds(0, HALO), cols], halo_send.at[:, cols]),
                (gx.at[:, cols], grads_all.at[which, :, cols]),
                (gv.at[:, cols], gv_all.at[which, :, cols]),
            )):
                outs.append(pltpu.make_async_copy(source, target, sems.at[4, 4 * i + q]))
                outs[-1].start()
        for copy in outs:
            copy.wait()


def backward_map(info, near, near_halo, top, top_halo, x, x_after, v, v_after, taps, first, saved, previous):
    batches, length, width = x.shape
    rows = length + HALO
    layers = taps.shape[0]
    flat = [array for group in saved for array in group]
    some = pl.BlockSpec(memory_space=pl.ANY)
    hbm = pl.BlockSpec(memory_space=pltpu.HBM)
    extra = () if previous is None else previous
    operands = (info, near, near_halo, top, top_halo, x, x_after, v, v_after, taps, *flat, *extra)
    aliases = {} if previous is None else {len(operands) - 2: 2, len(operands) - 1: 3}
    return pl.pallas_call(
        functools.partial(backward_kernel, (first, len(saved), previous is not None)),
        out_shape=(
            jax.ShapeDtypeStruct((length, width), bf16),
            jax.ShapeDtypeStruct((HALO, width), bf16),
            jax.ShapeDtypeStruct((batches, length, width), bf16),
            jax.ShapeDtypeStruct((batches, length, width), bf16),
            jax.ShapeDtypeStruct((1,), jnp.int32),
        ),
        in_specs=[pl.BlockSpec(memory_space=pltpu.SMEM)]
        + [some] * 2
        + [hbm] * 6
        + [pl.BlockSpec(memory_space=pltpu.VMEM)]
        + [hbm] * (len(flat) + len(extra)),
        out_specs=[some] * 2
        + [hbm] * 2
        + [pl.BlockSpec(memory_space=pltpu.SMEM)],
        scratch_shapes=[
            pltpu.VMEM((layers, rows, width), f32),
            pltpu.VMEM((layers, rows, width), f32),
            pltpu.VMEM((8, rows, LANES), f32),
            pltpu.VMEM((length, width), f32),
            pltpu.VMEM((rows, width), f32),
            pltpu.VMEM((rows, width), f32),
            pltpu.VMEM((4, rows, LANES), f32),
            pltpu.VMEM((length, width), bf16),
            pltpu.VMEM((length, width), bf16),
            pltpu.VMEM((HALO, width), bf16),
            pltpu.VMEM((length, width), bf16),
            pltpu.VMEM((length, width), bf16),
            pltpu.SemaphoreType.DMA((5, 16)),
        ],
        input_output_aliases=aliases,
        compiler_params=pltpu.CompilerParams(vmem_limit_bytes=VMEM_LIMIT),
        cost_estimate=pl.CostEstimate(flops=25 * layers * rows * width, bytes_accessed=14 * MIB, transcendentals=0),
        name="backward_map",
    )(*operands)


def pack_kernel(dest, gv_all, order, *refs):
    out, stacked = refs[-2:]
    heads, width = 8, out.shape[-1]
    length = gv_all.shape[1]
    for head in range(heads):
        stacked[head * length : (head + 1) * length, :] = gv_all[0, :, head * width : (head + 1) * width]
    slot = lax.broadcasted_iota(jnp.int32, (out.shape[0], heads * length), 0)
    place = jnp.where(slot == dest[...], 1.0, 0.0).astype(bf16)
    out[...] = jnp.dot(place, stacked[...], preferred_element_type=f32).astype(bf16)


def pack_values(batch, dest, gv_all, slots, order, into, at, total):
    batches, length, model = gv_all.shape
    feature = model // 8
    operands = [dest, gv_all, order] + ([] if into is None else [into])
    specs = [
        pl.BlockSpec(dest.shape, lambda i: (0, 0)),
        pl.BlockSpec((1, length, model), lambda i: (batch, 0, 0)),
        pl.BlockSpec(memory_space=pltpu.SMEM),
    ] + ([] if into is None else [pl.BlockSpec(memory_space=pltpu.HBM)])
    return pl.pallas_call(
        pack_kernel,
        out_shape=jax.ShapeDtypeStruct((slots, total * feature), bf16),
        grid=(1,),
        in_specs=specs,
        out_specs=pl.BlockSpec((slots, feature), lambda i: (0, at)),
        scratch_shapes=[pltpu.VMEM((8 * length, feature), bf16)],
        input_output_aliases={} if into is None else {3: 0},
        compiler_params=pltpu.CompilerParams(vmem_limit_bytes=VMEM_LIMIT),
        cost_estimate=pl.CostEstimate(
            flops=2 * slots * 8 * length * feature, bytes_accessed=2 * MIB, transcendentals=0
        ),
        name="pack_values",
    )(*operands)


def owner_kernel(first, count, has_table, got, place_of, row_of, groups, order, weight, *refs):
    if has_table:
        table_in, refs = refs[0], refs[1:]
    table, sorted_in, joined, rows, place = refs
    heads, row_width, feature = weight.shape
    table_rows = table.shape[0]
    slots = got.shape[0]
    room = rows.shape[1] - 128
    step = 128
    half = room // 2
    for m in range(count):
        b = first + m

        def sort(tile, carry):
            at = pl.multiple_of(tile * half, half)
            slot = lax.broadcasted_iota(jnp.int32, (half, slots), 0) + at
            pick = jnp.where(slot == place_of[b : b + 1, :], 1.0, 0.0).astype(bf16)
            sorted_in[m, pl.ds(at, half), :] = jnp.dot(
                pick, got[:, m * feature : (m + 1) * feature], preferred_element_type=f32
            ).astype(bf16)
            return carry

        lax.fori_loop(0, 2, sort, 0)

        def mark(tile, carry):
            at = pl.multiple_of(tile * step, step)
            row = lax.broadcasted_iota(jnp.int32, (step, room), 0) + at
            place[pl.ds(at, step), m * room : (m + 1) * room] = jnp.where(
                row == row_of[b : b + 1, :], 1.0, 0.0
            ).astype(bf16)
            return carry

        lax.fori_loop(0, table_rows // step, mark, 0)
        rows[m, 0:room, :] = jnp.zeros((room, row_width), bf16)

    def head_step(h, carry):
        most = groups[first, heads + h]
        for m in range(1, count):
            most = jnp.maximum(most, groups[first + m, heads + h])

        def multiply(tile, carry):
            ats = []
            for m in range(count):
                at = jnp.where(
                    tile < groups[first + m, heads + h], groups[first + m, h] + tile * step, room
                )
                ats.append(pl.ds(pl.multiple_of(at, 16), step))
                joined[m * step : (m + 1) * step, :] = sorted_in[m, ats[m], :]
            out = lax.dot_general(
                joined[...], weight[h], (((1,), (1,)), ((), ())), preferred_element_type=f32
            ).astype(bf16)
            for m in range(count):
                rows[m, ats[m], :] = out[m * step : (m + 1) * step]
            return carry

        return lax.fori_loop(0, most, multiply, carry)

    lax.fori_loop(0, heads, head_step, 0)
    tile = 512
    for block in range(row_width // tile):
        cols = pl.ds(block * tile, tile)
        part = None
        for m in range(count):
            more = jnp.dot(
                place[:, m * room : (m + 1) * room], rows[m, 0:room, cols], preferred_element_type=f32
            )
            part = more if part is None else part + more
        if has_table:
            part = part + table_in[:, cols]
        table[:, cols] = part


def owner_add(first, count, table, got, place_of, row_of, groups, weight, order):
    heads, row_width, feature = weight.shape
    slots = got.shape[0]
    room = row_of.shape[1]
    vmem = pl.BlockSpec(memory_space=pltpu.VMEM)
    smem = pl.BlockSpec(memory_space=pltpu.SMEM)
    operands = [got, place_of, row_of, groups, order, weight]
    specs = [vmem, vmem, vmem, smem, smem, vmem]
    if table is not None:
        operands.append(table)
        specs.append(vmem)
    return pl.pallas_call(
        functools.partial(owner_kernel, first, count, table is not None),
        out_shape=jax.ShapeDtypeStruct((TABLE_DEV, row_width), f32),
        in_specs=specs,
        out_specs=vmem,
        scratch_shapes=[
            pltpu.VMEM((count, room + 128, feature), bf16),
            pltpu.VMEM((count * 128, feature), bf16),
            pltpu.VMEM((count, room + 128, row_width), bf16),
            pltpu.VMEM((TABLE_DEV, count * room), bf16),
        ],
        compiler_params=pltpu.CompilerParams(vmem_limit_bytes=44 * MIB),
        cost_estimate=pl.CostEstimate(
            flops=6 * count * slots * row_width * TABLE_DEV,
            bytes_accessed=18 * MIB,
            transcendentals=0,
        ),
        name="owner_add",
    )(*operands)


def slots_of(row_ids, owners, capacity):
    batches, length, heads = row_ids.shape
    ids = row_ids.transpose(0, 2, 1).reshape(batches, heads * length)
    owner = ids // TABLE_DEV
    local = ids - owner * TABLE_DEV
    head = jnp.arange(heads * length, dtype=jnp.int32) // length
    order = jnp.arange(heads * length, dtype=jnp.int32)
    ahead = (owner[:, None, :] == owner[:, :, None]) & (order[None, :] < order[:, None])
    rank = jnp.sum(ahead.astype(jnp.int32), -1)
    dest = owner * capacity + rank
    code = local * heads + head
    slot = jnp.arange(owners * capacity, dtype=jnp.int32)
    hit = dest[:, None, :] == slot[:, None]
    holds = jnp.sum(jnp.where(hit, code[:, None, :] + 1, 0), -1) - 1
    return dest, holds


def groups_of(holds, heads):
    batches, slots = holds.shape
    room = -(-(slots + 15 * heads) // 128) * 128
    valid = holds >= 0
    head = jnp.where(valid, holds % heads, -1)
    member = head[..., None] == jnp.arange(heads, dtype=jnp.int32)
    order = jnp.arange(slots, dtype=jnp.int32)
    below = (order[None, :] < order[:, None]).astype(bf16)
    rank = jnp.einsum("ij,bjh->bih", below, member.astype(bf16), preferred_element_type=f32)
    counts = jnp.sum(member.astype(jnp.int32), 1)
    padded = (counts + 15) // 16 * 16
    number = jnp.arange(heads, dtype=jnp.int32)
    starts = jnp.sum(jnp.where(number[None, :] < number[:, None], padded[:, None, :], 0), -1)
    place = jnp.sum(jnp.where(member, rank.astype(jnp.int32) + starts[:, None, :] + 1, 0), -1) - 1
    spot = jnp.arange(room, dtype=jnp.int32)
    hit = place[:, None, :] == spot[:, None]
    row = jnp.sum(jnp.where(hit, (holds // heads)[:, None, :] + 1, 0), -1) - 1
    groups = jnp.concatenate([starts, (counts + 127) // 128], 1)
    return place, row, groups


def shards(
    saved_inputs, memory, value_weight, conv_weight, norm_gain, layer_counts, row_ids, out_grad
):
    section = lax.axis_index("section")
    sections = lax.axis_size("section")
    owners = lax.axis_size("table")
    batches, length, width = out_grad.shape
    heads = memory.shape[3]
    capacity = 3 * length * heads // (2 * owners)
    slots = owners * capacity
    weight = value_weight[0]
    live = layer_counts[0]
    taps = 0.5 * conv_weight[0] * norm_gain[0][:, None, :]
    x = saved_inputs[0]
    is_top = section == sections - 1

    to_next = [(i, i + 1) for i in range(owners - 1)]
    to_last = [(i + 1, i) for i in range(owners - 1)]
    down = [(i + 1, i) for i in range(sections - 1)]
    down_halo = [
        ((i + 1) * owners + t + 1, i * owners + t)
        for i in range(sections - 1)
        for t in range(owners - 1)
    ]
    x_before = lax.ppermute(x[:, length - HALO :], "table", to_next)
    x_after = lax.ppermute(x[:, :HALO], "table", to_last)
    top_halo = lax.ppermute(out_grad[:, :HALO], "table", to_last)
    v = jnp.einsum("bthr,hrc->bthc", memory[0], weight, preferred_element_type=f32)
    v = v.reshape(batches, length, width)
    v_before = lax.ppermute(v[:, length - HALO :], "table", to_next)
    v_after = lax.ppermute(v[:, :HALO], "table", to_last)

    saved = []
    near = jnp.zeros((length, width), bf16)
    near_halo = jnp.zeros((HALO, width), bf16)
    outputs = table = dest = holds = place_of = row_of = groups = got = packed = None
    order = jnp.zeros((1,), jnp.int32)
    ticks = batches + sections - 1
    for tick in range(ticks):
        if tick < batches:
            saved.append(
                forward_map(
                    tick, live.reshape(1), x, x_before, x_after, v, v_before, v_after, taps, order
                )
            )
        position = tick - (sections - 1 - section)
        which = jnp.clip(position, 0, batches - 1)
        active = (position >= 0) & (position < batches)
        info = jnp.stack([which, active, is_top, live]).astype(jnp.int32)
        first = max(0, tick - (sections - 1))
        grad_send, halo_send, *outputs, order = backward_map(
            info, near, near_halo, out_grad, top_halo, x, x_after, v, v_after, taps,
            first, saved[first : tick + 1], outputs,
        )
        if tick < ticks - 1:
            near = lax.ppermute(grad_send, "section", down)
            near_halo = lax.ppermute(halo_send, ("section", "table"), down_halo)
        if tick == 0:
            dest, holds = slots_of(row_ids[0] + order, owners, capacity)
            holds = holds.reshape(batches, owners, capacity).transpose(1, 0, 2)
            holds = holds.reshape(owners, batches * capacity)
        if tick == sections - 1:
            holds = lax.all_to_all(holds + order, "table", 0, 0, tiled=True)
            holds = holds.reshape(owners, batches, capacity).transpose(1, 0, 2)
            holds = holds.reshape(batches, slots)
        if tick == sections:
            place_of, row_of, groups = groups_of(holds + order, heads)
        batch = tick - (sections - 1)
        if 0 <= batch < batches - 1:
            packed = pack_values(
                batch, dest[batch][None, :], outputs[1], slots, order, packed, batch, batches - 1
            )
        if batch == batches - 2:
            got = lax.all_to_all(packed, "table", 0, 0, tiled=True)
    last = batches - 1
    packed = pack_values(last, dest[last][None, :], outputs[1], slots, order, None, 0, 1)
    rest = lax.all_to_all(packed, "table", 0, 0, tiled=True)
    table = owner_add(0, last, None, got, place_of, row_of, groups, weight, order)
    table = owner_add(last, 1, table, rest, place_of, row_of, groups, weight, order)
    return (outputs[0][None], table[None])


def solution(mesh):
    placed = (
        P("section", None, "table", None),
        P("section", None, "table", None, None),
        P("section", None, None, None),
        P("section", None, None, None),
        P("section", None, None),
        P("section"),
        P("section", None, "table", None),
        P(None, "table", None),
    )
    return jax.shard_map(
        shards,
        mesh=mesh,
        in_specs=placed,
        out_specs=(P("section", None, "table", None), P("section", "table", None)),
        check_vma=False,
    )
```

```python
import functools
import math

import jax
import jax.numpy as jnp
from jax import lax
from jax.experimental import pallas as pl
from jax.experimental.pallas import tpu as pltpu
from jax.sharding import PartitionSpec as P

TABLE_DEV = 1024
HALO = 16
EPS = 1e-06
LANES = 128
STEP = 512
SPLIT = 4
MIB = 1 << 20
VMEM_LIMIT = 60 * MIB

f32 = jnp.float32
bf16 = jnp.bfloat16


def row_total(partial):
    return jnp.broadcast_to(jnp.sum(partial, -1, keepdims=True), partial.shape)


def columns(chunk):
    return pl.ds(pl.multiple_of(chunk * STEP, STEP), STEP)


def wide(narrow):
    return jnp.concatenate([narrow] * (STEP // LANES), 1)


def fold(chunk):
    return sum(chunk[:, i : i + LANES] for i in range(0, STEP, LANES))


def values_kernel(memory, weight, v_out, low_one, high_one, low_rest, high_rest, held, wide_held, flat, v, sems):
    batches, rows = held.shape[:2]
    heads, _, feature = weight.shape
    length = rows // heads
    loads = [pltpu.make_async_copy(memory.at[b], held.at[b], sems.at[0, b]) for b in range(batches)]
    copies = [pltpu.make_async_copy(weight.at[h], flat.at[h], sems.at[1, h]) for h in range(heads)]
    for copy in loads + copies:
        copy.start()
    step = 64
    for b in range(batches):
        loads[b].wait()

        def widen(tile, carry):
            at = pl.multiple_of(tile * step, step)
            block = held[b, pl.ds(at, step), :].astype(f32)
            for c in range(block.shape[1] // LANES):
                wide_held[c, pl.ds(b * rows + at, step), :] = block[:, c * LANES : (c + 1) * LANES]
            return carry

        lax.fori_loop(0, rows // step, widen, 0)
    outs = []
    for h in range(heads):
        copies[h].wait()
        taken = [
            wide_held[c, pl.ds(h, batches * length, stride=heads), :].astype(bf16)
            for c in range(wide_held.shape[0])
        ]
        cols = pl.ds(h * feature, feature)
        v[:, cols] = jnp.dot(
            jnp.concatenate(taken, 1), flat[h], preferred_element_type=f32
        )
        outs.append(pltpu.make_async_copy(v.at[:, cols], v_out.at[:, cols], sems.at[2, h]))
        outs[-1].start()
    for b in range(batches):
        low = low_one.at[0] if b == 0 else low_rest.at[b - 1]
        high = high_one.at[0] if b == 0 else high_rest.at[b - 1]
        for i, (target, at) in enumerate(((low, 0), (high, length - HALO))):
            outs.append(
                pltpu.make_async_copy(v.at[pl.ds(b * length + at, HALO)], target, sems.at[3 + i, b])
            )
            outs[-1].start()
    for copy in outs:
        copy.wait()


def all_values(memory, weight):
    batches, length, heads, row_width = memory.shape
    feature = weight.shape[2]
    hbm = pl.BlockSpec(memory_space=pltpu.HBM)
    one = jax.ShapeDtypeStruct((1, HALO, heads * feature), f32)
    rest = jax.ShapeDtypeStruct((batches - 1, HALO, heads * feature), f32)
    v, *halos = pl.pallas_call(
        values_kernel,
        out_shape=(
            jax.ShapeDtypeStruct((batches * length, heads * feature), f32), one, one, rest, rest
        ),
        in_specs=[hbm] * 2,
        out_specs=[hbm] * 5,
        scratch_shapes=[
            pltpu.VMEM((batches, length * heads, row_width), bf16),
            pltpu.VMEM((row_width // LANES, batches * length * heads, LANES), f32),
            pltpu.VMEM(weight.shape, bf16),
            pltpu.VMEM((batches * length, heads * feature), f32),
            pltpu.SemaphoreType.DMA((5, heads)),
        ],
        compiler_params=pltpu.CompilerParams(vmem_limit_bytes=VMEM_LIMIT),
        cost_estimate=pl.CostEstimate(
            flops=2 * batches * length * heads * row_width * feature,
            bytes_accessed=18 * MIB,
            transcendentals=0,
        ),
        name="all_values",
    )(memory.reshape(batches, length * heads, row_width), weight)
    return v.reshape(batches, length, heads * feature), halos


def forward_kernel(
    batch, v_halo, live_ref, xb, xm, xa, vb, vm, va, taps, order, hid_out, der_out, scal_out,
    x_win, v_win, hid, der, scal, rms_now, sems,
):
    width = xm.shape[-1]
    rows = x_win.shape[0]
    keep = rows - HALO
    chunks = width // STEP
    live = live_ref[0]
    length = xm.shape[-2]
    parts = ((xb, vb, 0, HALO), (xm, vm, HALO, length), (xa, va, HALO + length, HALO))
    loads = []
    for q in range(SPLIT):
        cols = pl.ds(q * (width // SPLIT), width // SPLIT)
        loads.append([])
        for i, (x_part, v_part, at, size) in enumerate(parts):
            here = batch if i == 1 else v_halo
            for j, (part, window, b) in enumerate(((x_part, x_win, batch), (v_part, v_win, here))):
                loads[q].append(
                    pltpu.make_async_copy(
                        part.at[b, :, cols],
                        window.at[pl.ds(at, size), cols],
                        sems.at[2 + 3 * j + i, q],
                    )
                )
                loads[q][-1].start()

    def load(chunk, sums):
        cols = columns(chunk)
        x = x_win[:, cols].astype(f32)
        v = v_win[:, cols]
        return sums[0] + fold(x * x), sums[1] + fold(v * v), sums[2] + fold(x * v)

    zero = jnp.zeros((rows, LANES), f32)
    sums = (zero, zero, zero)
    for q in range(SPLIT):
        for copy in loads[q]:
            copy.wait()
        sums = lax.fori_loop(q * chunks // SPLIT, (q + 1) * chunks // SPLIT, load, sums)
    xx, vv, xv = sums
    xv = row_total(xv)
    rx = lax.rsqrt(row_total(xx) / width + EPS)
    rv = lax.rsqrt(row_total(vv) / width + EPS)
    gate = jax.nn.sigmoid(rx * rv * xv / math.sqrt(width))
    scal[4] = rx[HALO:]
    scal[5] = rv[HALO:]
    scal[6] = xv[HALO:]
    scal[7] = gate[HALO:]
    rms_now[...] = gate

    def mix(chunk, total):
        cols = columns(chunk)
        hidden = x_win[:, cols].astype(f32) + wide(rms_now[...]) * v_win[:, cols]
        hid[0, :, cols] = hidden
        return total + fold(hidden * hidden)

    total = lax.fori_loop(0, chunks, mix, zero)

    def hidden_copy(layer):
        return pltpu.make_async_copy(
            hid.at[layer, pl.ds(HALO, keep)], hid_out.at[layer], sems.at[0, layer]
        )

    def slope_copy(layer):
        return pltpu.make_async_copy(der.at[layer], der_out.at[layer], sems.at[1, layer])

    def layer_step(layer, total):
        hidden_copy(layer).start()
        rms = lax.rsqrt(row_total(total) / width + EPS)
        scal[layer] = rms[HALO:]
        rms_now[...] = rms

        def one(chunk, total):
            cols = columns(chunk)
            hidden = hid[layer, :, cols]
            unit = hidden * wide(rms_now[...])
            mixed = taps[layer, 0:1, cols] * unit
            for k in range(1, 4):
                mixed = mixed + taps[layer, k : k + 1, cols] * pltpu.roll(unit, k, 0)
            bend = jnp.tanh(mixed)
            rise = 1.0 + bend
            silu = mixed * rise
            der[layer, :, cols] = (rise + silu * (1.0 - bend))[HALO:]
            after = hidden + silu
            hid[layer + 1, :, cols] = after
            return total + fold(after * after)

        total = lax.fori_loop(0, chunks, one, zero)
        slope_copy(layer).start()
        return total

    lax.fori_loop(0, live, layer_step, total)
    out = pltpu.make_async_copy(scal, scal_out, sems.at[0, 4])
    out.start()

    def finish(layer, carry):
        hidden_copy(layer).wait()
        slope_copy(layer).wait()
        return carry

    lax.fori_loop(0, live, finish, 0)
    out.wait()


def forward_map(batch, v_halo, live, x, x_before, x_after, v, v_before, v_after, taps, order):
    length, width = x.shape[1:]
    keep = length + HALO
    rows = keep + HALO
    layers = taps.shape[0]
    hbm = pl.BlockSpec(memory_space=pltpu.HBM)
    return pl.pallas_call(
        functools.partial(forward_kernel, batch, v_halo),
        out_shape=(
            jax.ShapeDtypeStruct((layers, keep, width), f32),
            jax.ShapeDtypeStruct((layers, keep, width), f32),
            jax.ShapeDtypeStruct((8, keep, LANES), f32),
        ),
        in_specs=[pl.BlockSpec(memory_space=pltpu.SMEM)]
        + [hbm] * 6
        + [pl.BlockSpec(memory_space=pltpu.VMEM), pl.BlockSpec(memory_space=pltpu.SMEM)],
        out_specs=[hbm] * 3,
        scratch_shapes=[
            pltpu.VMEM((rows, width), bf16),
            pltpu.VMEM((rows, width), f32),
            pltpu.VMEM((layers + 1, rows, width), f32),
            pltpu.VMEM((layers, keep, width), f32),
            pltpu.VMEM((8, keep, LANES), f32),
            pltpu.VMEM((rows, LANES), f32),
            pltpu.SemaphoreType.DMA((8, layers + 1)),
        ],
        compiler_params=pltpu.CompilerParams(vmem_limit_bytes=VMEM_LIMIT),
        cost_estimate=pl.CostEstimate(
            flops=30 * layers * rows * width,
            bytes_accessed=16 * MIB,
            transcendentals=layers * rows * width,
        ),
        name="forward_map",
    )(live, x_before, x, x_after, v_before, v, v_after, taps, order)


def backward_kernel(
    held, info, near, near_halo, top, top_halo, x_all, v_all, taps, *refs,
):
    saved = [refs[3 * i : 3 * i + 3] for i in range(held[1])]
    refs = refs[3 * held[1] :]
    if held[2]:
        gv_held, refs = refs[1], refs[2:]
    if held[3]:
        dest, refs = refs[0], refs[2:]
        packed, stacked, slots_now = refs[5], refs[-2], refs[-1]
        refs = refs[:5] + refs[6:-2]
    (
        grad_send, halo_send, grads_all, gv_all, order_out,
        hid, der, scal, v_in, g, u, coef, x_in, g_in, ga_in, gx, gv, sems,
    ) = refs
    which = info[0]
    active = info[1]
    is_top = info[2]
    live = info[3]
    length, width = grad_send.shape
    rows = g.shape[0]
    chunks = width // STEP
    quarter = width // SPLIT
    first, count = held[0], held[1]
    order_out[0] = 0

    def part(q):
        return pl.ds(pl.multiple_of(q * quarter, quarter), quarter)

    def scal_copy(i):
        return pltpu.make_async_copy(saved[i][2], scal, sems.at[2, 0])

    def layer_copies(i, layer, q):
        cols = part(q)
        return (
            pltpu.make_async_copy(
                saved[i][1].at[layer, :, cols], der.at[layer, :, cols], sems.at[1, 4 * layer + q]
            ),
            pltpu.make_async_copy(
                saved[i][0].at[layer, :, cols], hid.at[layer, :, cols], sems.at[0, 4 * layer + q]
            ),
        )

    def input_copies():
        return (
            pltpu.make_async_copy(x_all.at[which], x_in, sems.at[2, 1]),
            pltpu.make_async_copy(v_all.at[which], v_in, sems.at[2, 3]),
        )

    def grad_copies(source, source_halo):
        return (
            pltpu.make_async_copy(source, g_in, sems.at[3, 0]),
            pltpu.make_async_copy(source_halo, ga_in, sems.at[3, 1]),
        )

    def pack():
        spread_heads(gv, stacked)
        into_slots(dest, stacked, slots_now)
        feature = slots_now.shape[1]
        at = pl.ds(packed.shape[1] - feature, feature)
        copy = pltpu.make_async_copy(slots_now, packed.at[:, at], sems.at[3, 3])
        copy.start()
        copy.wait()

    @pl.when(active == 1)
    def _():
        @pl.when(is_top == 1)
        def _():
            for copy in grad_copies(top.at[which], top_halo.at[which]):
                copy.start()

        @pl.when(is_top == 0)
        def _():
            for copy in grad_copies(near, near_halo):
                copy.start()

        for i in range(count):
            @pl.when(which == first + i)
            def _():
                def begin(step, carry):
                    layer = live - 1 - step
                    for q in range(SPLIT):
                        for copy in layer_copies(i, layer, q):
                            copy.start()
                    return carry

                begin(0, 0)
                scal_copy(i).start()
                lax.fori_loop(1, live, begin, 0)

        for copy in input_copies():
            copy.start()

        for copy in grad_copies(near, near_halo):
            copy.wait()

        def into_taps(layer, cols, grad):
            size = grad.shape[0]
            slope = grad * der[layer, 0:size, cols]
            out = taps[layer, 0:1, cols] * slope
            for k in range(1, 4):
                out = out + taps[layer, k : k + 1, cols] * pltpu.roll(slope, size - k, 0)
            u[0:size, cols] = out
            return fold(out * hid[layer, 0:size, cols])

        last = live - 1
        total = jnp.zeros((rows, LANES), f32)
        for q in range(SPLIT):
            for copy in layer_copies(0, last, q):
                copy.wait()

            def start(chunk, total):
                cols = columns(chunk)
                g[0:length, cols] = g_in[:, cols].astype(f32)
                g[length:rows, cols] = ga_in[:, cols].astype(f32)
                return total + into_taps(last, cols, g[:, cols])

            total = lax.fori_loop(q * chunks // SPLIT, (q + 1) * chunks // SPLIT, start, total)
        scal_copy(0).wait()

        def coefficients(layer, total):
            size = total.shape[0]
            rms = scal[layer, 0:size]
            coef[0, 0:size] = rms
            coef[1, 0:size] = -rms * rms * rms * (row_total(total) / width)

        def through_rms(layer, cols, size):
            return g[0:size, cols] + (
                wide(coef[0, 0:size]) * u[0:size, cols]
                + wide(coef[1, 0:size]) * hid[layer, 0:size, cols]
            )

        def layer_step(size, step, total):
            layer = live - 1 - step
            coefficients(layer, total)
            for q in range(SPLIT):
                for copy in layer_copies(0, layer - 1, q):
                    copy.wait()

            def one(chunk, total):
                cols = columns(chunk)
                grad = through_rms(layer, cols, size)
                g[0:size, cols] = grad
                return total + into_taps(layer - 1, cols, grad)

            return lax.fori_loop(0, chunks, one, jnp.zeros((size, LANES), f32))

        total = lax.fori_loop(
            0, jnp.minimum(live - 1, 1), functools.partial(layer_step, rows), total
        )
        fewer = rows - HALO // 2
        total = lax.fori_loop(
            1, live - 1, functools.partial(layer_step, fewer), total[0:fewer]
        )
        coefficients(0, total[0:length])
        for copy in input_copies():
            copy.wait()

        def to_gate(chunk, total):
            cols = columns(chunk)
            grad = through_rms(0, cols, length)
            g[0:length, cols] = grad
            return total + fold(grad * v_in[:, cols])

        total = row_total(lax.fori_loop(0, chunks, to_gate, jnp.zeros((length, LANES), f32)))
        rx, rv, xv, gate = (scal[i, 0:length] for i in range(4, 8))
        both = total * gate * (1.0 - gate) * (1.0 / math.sqrt(width)) * rx * rv
        mean = xv / width
        coef[0, 0:length] = both
        coef[1, 0:length] = -both * rx * rx * mean
        coef[2, 0:length] = -both * rv * rv * mean
        coef[3, 0:length] = gate

        def finish(chunk, carry):
            cols = columns(chunk)
            grad = g[0:length, cols]
            x = x_in[:, cols].astype(f32)
            v = v_in[:, cols]
            cross = wide(coef[0, 0:length])
            grad_x = grad + cross * v + wide(coef[1, 0:length]) * x
            grad_v = wide(coef[3, 0:length]) * grad + cross * x + wide(coef[2, 0:length]) * v
            gx[:, cols] = grad_x.astype(bf16)
            gv[:, cols] = grad_v.astype(bf16)
            return carry

        outs = []
        for q in range(SPLIT):
            lax.fori_loop(q * chunks // SPLIT, (q + 1) * chunks // SPLIT, finish, 0)
            cols = part(q)
            for i, (source, target) in enumerate((
                (gx.at[:, cols], grad_send.at[:, cols]),
                (gx.at[pl.ds(0, HALO), cols], halo_send.at[:, cols]),
                (gx.at[:, cols], grads_all.at[which, :, cols]),
                (gv.at[:, cols], gv_all.at[which, :, cols]),
            )):
                outs.append(pltpu.make_async_copy(source, target, sems.at[4, 4 * i + q]))
                outs[-1].start()
        if held[3]:
            pack()
        for copy in outs:
            copy.wait()

    if held[3]:
        @pl.when(active == 0)
        def _():
            copy = pltpu.make_async_copy(gv_held.at[held[3] - 1], gv, sems.at[3, 2])
            copy.start()
            copy.wait()
            pack()


def backward_map(info, near, near_halo, top, top_halo, x, v, taps, first, saved, previous, packing=None):
    batches, length, width = x.shape
    rows = length + HALO
    layers = taps.shape[0]
    flat = [array for group in saved for array in group]
    some = pl.BlockSpec(memory_space=pl.ANY)
    hbm = pl.BlockSpec(memory_space=pltpu.HBM)
    vmem = pl.BlockSpec(memory_space=pltpu.VMEM)
    smem = pl.BlockSpec(memory_space=pltpu.SMEM)
    operands = [info, near, near_halo, top, top_halo, x, v, taps, *flat]
    specs = [smem] + [some] * 2 + [hbm] * 4 + [vmem] + [hbm] * len(flat)
    shapes = [
        jax.ShapeDtypeStruct((length, width), bf16),
        jax.ShapeDtypeStruct((HALO, width), bf16),
        jax.ShapeDtypeStruct((batches, length, width), bf16),
        jax.ShapeDtypeStruct((batches, length, width), bf16),
        jax.ShapeDtypeStruct((1,), jnp.int32),
    ]
    out_specs = [some] * 2 + [hbm] * 2 + [smem]
    scratch = [
        pltpu.VMEM((layers, rows, width), f32),
        pltpu.VMEM((layers, rows, width), f32),
        pltpu.VMEM((8, rows, LANES), f32),
        pltpu.VMEM((length, width), f32),
        pltpu.VMEM((rows, width), f32),
        pltpu.VMEM((rows, width), f32),
        pltpu.VMEM((4, rows, LANES), f32),
        pltpu.VMEM((length, width), bf16),
        pltpu.VMEM((length, width), bf16),
        pltpu.VMEM((HALO, width), bf16),
        pltpu.VMEM((length, width), bf16),
        pltpu.VMEM((length, width), bf16),
        pltpu.SemaphoreType.DMA((5, 16)),
    ]
    aliases = {}
    if previous is not None:
        aliases = {len(operands): 2, len(operands) + 1: 3}
        operands += previous
        specs += [hbm] * 2
    if packing is not None:
        batch, dest, packed = packing
        aliases[len(operands) + 1] = 5
        operands += [dest, packed]
        specs += [vmem, hbm]
        shapes.append(jax.ShapeDtypeStruct(packed.shape, packed.dtype))
        out_specs.append(hbm)
        feature = width // 8
        scratch += [pltpu.VMEM((8 * length, feature), bf16), pltpu.VMEM((packed.shape[0], feature), bf16)]
    pack_flag = 0 if packing is None else packing[0] + 1
    return pl.pallas_call(
        functools.partial(backward_kernel, (first, len(saved), previous is not None, pack_flag)),
        out_shape=shapes,
        in_specs=specs,
        out_specs=out_specs,
        scratch_shapes=scratch,
        input_output_aliases=aliases,
        compiler_params=pltpu.CompilerParams(vmem_limit_bytes=VMEM_LIMIT),
        cost_estimate=pl.CostEstimate(
            flops=25 * layers * rows * width, bytes_accessed=14 * MIB, transcendentals=0
        ),
        name="backward_map",
    )(*operands)


def spread_heads(gv, stacked):
    length, width = gv.shape[0], stacked.shape[1]
    for head in range(stacked.shape[0] // length):
        stacked[head * length : (head + 1) * length, :] = gv[:, head * width : (head + 1) * width]


def into_slots(dest, stacked, out):
    slot = lax.broadcasted_iota(jnp.int32, (out.shape[0], stacked.shape[0]), 0)
    place = jnp.where(slot == dest[...], 1.0, 0.0).astype(bf16)
    out[...] = jnp.dot(place, stacked[...], preferred_element_type=f32).astype(bf16)


def pack_kernel(dest, gv_all, order, *refs):
    out, stacked = refs[-2:]
    spread_heads(gv_all.at[0], stacked)
    into_slots(dest, stacked, out)


def pack_values(batch, dest, gv_all, slots, order, into, at, total):
    batches, length, model = gv_all.shape
    feature = model // 8
    operands = [dest, gv_all, order] + ([] if into is None else [into])
    specs = [
        pl.BlockSpec(dest.shape, lambda i: (0, 0)),
        pl.BlockSpec((1, length, model), lambda i: (batch, 0, 0)),
        pl.BlockSpec(memory_space=pltpu.SMEM),
    ] + ([] if into is None else [pl.BlockSpec(memory_space=pltpu.HBM)])
    return pl.pallas_call(
        pack_kernel,
        out_shape=jax.ShapeDtypeStruct((slots, total * feature), bf16),
        grid=(1,),
        in_specs=specs,
        out_specs=pl.BlockSpec((slots, feature), lambda i: (0, at)),
        scratch_shapes=[pltpu.VMEM((8 * length, feature), bf16)],
        input_output_aliases={} if into is None else {3: 0},
        compiler_params=pltpu.CompilerParams(vmem_limit_bytes=VMEM_LIMIT),
        cost_estimate=pl.CostEstimate(
            flops=2 * slots * 8 * length * feature, bytes_accessed=2 * MIB, transcendentals=0
        ),
        name="pack_values",
    )(*operands)


def owner_kernel(first, count, has_table, got, place_of, row_of, groups, order, weight_in, *refs):
    if has_table:
        table_in, refs = refs[0], refs[1:]
    table, sorted_in, joined, rows, place, weight, total, sems = refs
    heads, row_width, feature = weight.shape
    table_rows = table.shape[0]
    copies = [
        pltpu.make_async_copy(weight_in.at[h], weight.at[h], sems.at[h]) for h in range(heads)
    ]
    if has_table:
        copies.append(pltpu.make_async_copy(table_in, total, sems.at[heads]))
    for copy in copies:
        copy.start()
    slots = got.shape[0]
    room = rows.shape[1] - 128
    step = 128
    half = room // 2
    for m in range(count):
        b = first + m

        def sort(tile, carry):
            at = pl.multiple_of(tile * half, half)
            slot = lax.broadcasted_iota(jnp.int32, (half, slots), 0) + at
            pick = jnp.where(slot == place_of[b : b + 1, :], 1.0, 0.0).astype(bf16)
            sorted_in[m, pl.ds(at, half), :] = jnp.dot(
                pick, got[:, m * feature : (m + 1) * feature], preferred_element_type=f32
            ).astype(bf16)
            return carry

        lax.fori_loop(0, 2, sort, 0)

        def mark(tile, carry):
            at = pl.multiple_of(tile * step, step)
            row = lax.broadcasted_iota(jnp.int32, (step, room), 0) + at
            place[pl.ds(at, step), m * room : (m + 1) * room] = jnp.where(
                row == row_of[b : b + 1, :], 1.0, 0.0
            ).astype(bf16)
            return carry

        lax.fori_loop(0, table_rows // step, mark, 0)
        rows[m, 0:room, :] = jnp.zeros((room, row_width), bf16)

    def head_step(h, carry):
        most = groups[first, heads + h]
        for m in range(1, count):
            most = jnp.maximum(most, groups[first + m, heads + h])

        def multiply(tile, carry):
            ats = []
            for m in range(count):
                at = jnp.where(
                    tile < groups[first + m, heads + h], groups[first + m, h] + tile * step, room
                )
                ats.append(pl.ds(pl.multiple_of(at, 16), step))
                joined[m * step : (m + 1) * step, :] = sorted_in[m, ats[m], :]
            out = lax.dot_general(
                joined[...], weight[h], (((1,), (1,)), ((), ())), preferred_element_type=f32
            ).astype(bf16)
            for m in range(count):
                rows[m, ats[m], :] = out[m * step : (m + 1) * step]
            return carry

        return lax.fori_loop(0, most, multiply, carry)

    for h in range(heads):
        copies[h].wait()
        head_step(h, 0)
    if has_table:
        copies[heads].wait()
    tile = 256
    outs = []
    for block in range(row_width // tile):
        cols = pl.ds(block * tile, tile)
        part = None
        for m in range(count):
            more = jnp.dot(
                place[:, m * room : (m + 1) * room], rows[m, 0:room, cols], preferred_element_type=f32
            )
            part = more if part is None else part + more
        if has_table:
            part = part + total[:, cols]
        total[:, cols] = part
        outs.append(
            pltpu.make_async_copy(
                total.at[:, cols], table.at[:, cols], sems.at[heads + 1 + block]
            )
        )
        outs[-1].start()
    for copy in outs:
        copy.wait()


def owner_add(first, count, table, got, place_of, row_of, groups, weight, order):
    heads, row_width, feature = weight.shape
    slots = got.shape[0]
    room = row_of.shape[1]
    vmem = pl.BlockSpec(memory_space=pltpu.VMEM)
    smem = pl.BlockSpec(memory_space=pltpu.SMEM)
    operands = [got, place_of, row_of, groups, order, weight]
    hbm = pl.BlockSpec(memory_space=pltpu.HBM)
    specs = [vmem, vmem, vmem, smem, smem, hbm]
    if table is not None:
        operands.append(table)
        specs.append(hbm)
    return pl.pallas_call(
        functools.partial(owner_kernel, first, count, table is not None),
        out_shape=jax.ShapeDtypeStruct((TABLE_DEV, row_width), f32),
        in_specs=specs,
        out_specs=hbm,
        scratch_shapes=[
            pltpu.VMEM((count, room + 128, feature), bf16),
            pltpu.VMEM((count * 128, feature), bf16),
            pltpu.VMEM((count, room + 128, row_width), bf16),
            pltpu.VMEM((TABLE_DEV, count * room), bf16),
            pltpu.VMEM(weight.shape, bf16),
            pltpu.VMEM((TABLE_DEV, row_width), f32),
            pltpu.SemaphoreType.DMA((heads + 1 + row_width // 256,)),
        ],
        compiler_params=pltpu.CompilerParams(vmem_limit_bytes=VMEM_LIMIT),
        cost_estimate=pl.CostEstimate(
            flops=6 * count * slots * row_width * TABLE_DEV,
            bytes_accessed=18 * MIB,
            transcendentals=0,
        ),
        name="owner_add",
    )(*operands)


def slots_of(row_ids, owners, capacity):
    batches, length, heads = row_ids.shape
    ids = row_ids.transpose(0, 2, 1).reshape(batches, heads * length)
    owner = ids // TABLE_DEV
    local = ids - owner * TABLE_DEV
    head = jnp.arange(heads * length, dtype=jnp.int32) // length
    order = jnp.arange(heads * length, dtype=jnp.int32)
    ahead = (owner[:, None, :] == owner[:, :, None]) & (order[None, :] < order[:, None])
    rank = jnp.sum(ahead.astype(jnp.int32), -1)
    dest = owner * capacity + rank
    code = local * heads + head
    slot = jnp.arange(owners * capacity, dtype=jnp.int32)
    hit = dest[:, None, :] == slot[:, None]
    holds = jnp.sum(jnp.where(hit, code[:, None, :] + 1, 0), -1) - 1
    return dest, holds


def groups_of(holds, heads):
    batches, slots = holds.shape
    room = -(-(slots + 15 * heads) // 128) * 128
    valid = holds >= 0
    head = jnp.where(valid, holds % heads, -1)
    member = head[..., None] == jnp.arange(heads, dtype=jnp.int32)
    order = jnp.arange(slots, dtype=jnp.int32)
    below = (order[None, :] < order[:, None]).astype(bf16)
    rank = jnp.einsum("ij,bjh->bih", below, member.astype(bf16), preferred_element_type=f32)
    counts = jnp.sum(member.astype(jnp.int32), 1)
    padded = (counts + 15) // 16 * 16
    number = jnp.arange(heads, dtype=jnp.int32)
    starts = jnp.sum(jnp.where(number[None, :] < number[:, None], padded[:, None, :], 0), -1)
    place = jnp.sum(jnp.where(member, rank.astype(jnp.int32) + starts[:, None, :] + 1, 0), -1) - 1
    spot = jnp.arange(room, dtype=jnp.int32)
    hit = place[:, None, :] == spot[:, None]
    row = jnp.sum(jnp.where(hit, (holds // heads)[:, None, :] + 1, 0), -1) - 1
    groups = jnp.concatenate([starts, (counts + 127) // 128], 1)
    return place, row, groups


def shards(
    saved_inputs, memory, value_weight, conv_weight, norm_gain, layer_counts, row_ids, out_grad
):
    section = lax.axis_index("section")
    sections = lax.axis_size("section")
    owners = lax.axis_size("table")
    batches, length, width = out_grad.shape
    heads = memory.shape[3]
    capacity = 3 * length * heads // (2 * owners)
    slots = owners * capacity
    weight = value_weight[0]
    live = layer_counts[0]
    taps = 0.5 * conv_weight[0] * norm_gain[0][:, None, :]
    x = saved_inputs[0]
    is_top = section == sections - 1

    to_next = [(i, i + 1) for i in range(owners - 1)]
    to_last = [(i + 1, i) for i in range(owners - 1)]
    down = [(i + 1, i) for i in range(sections - 1)]
    down_halo = [
        ((i + 1) * owners + t + 1, i * owners + t)
        for i in range(sections - 1)
        for t in range(owners - 1)
    ]
    x_before = lax.ppermute(x[:, length - HALO :], "table", to_next)
    x_after = lax.ppermute(x[:, :HALO], "table", to_last)
    v, (low_one, high_one, low_rest, high_rest) = all_values(memory[0], weight)
    v_before = [lax.ppermute(high_one, "table", to_next)]
    v_after = [lax.ppermute(low_one, "table", to_last)]
    top_halo = lax.ppermute(out_grad[:, :HALO], "table", to_last)
    v_before.append(lax.ppermute(high_rest, "table", to_next))
    v_after.append(lax.ppermute(low_rest, "table", to_last))

    saved = []
    near = jnp.zeros((length, width), bf16)
    near_halo = jnp.zeros((HALO, width), bf16)
    outputs = table = dest = holds = place_of = row_of = groups = got = None
    packed = [None, None]
    order = jnp.zeros((1,), jnp.int32)
    ticks = batches + sections - 1
    for tick in range(ticks):
        if tick < batches:
            which_halo = min(tick, 1)
            saved.append(
                forward_map(
                    tick, max(tick - 1, 0), live.reshape(1), x, x_before, x_after,
                    v, v_before[which_halo], v_after[which_halo], taps, order,
                )
            )
        position = tick - (sections - 1 - section)
        which = jnp.clip(position, 0, batches - 1)
        active = (position >= 0) & (position < batches)
        info = jnp.stack([which, active, is_top, live]).astype(jnp.int32)
        first = max(0, tick - (sections - 1))
        packing = (batches - 1, dest[batches - 1][None, :], packed[1]) if tick == ticks - 1 else None
        grad_send, halo_send, *outputs = backward_map(
            info, near, near_halo, out_grad, top_halo, x, v, taps,
            first, saved[first : tick + 1], outputs, packing,
        )
        if packing is not None:
            packed[1] = outputs.pop()
        order = outputs.pop()
        if tick < ticks - 1:
            near = lax.ppermute(grad_send, "section", down)
            near_halo = lax.ppermute(halo_send, ("section", "table"), down_halo)
        if tick == 0:
            dest, holds = slots_of(row_ids[0] + order, owners, capacity)
            holds = holds.reshape(batches, owners, capacity).transpose(1, 0, 2)
            holds = holds.reshape(owners, batches * capacity)
        if tick == sections - 1:
            holds = lax.all_to_all(holds + order, "table", 0, 0, tiled=True)
            holds = holds.reshape(owners, batches, capacity).transpose(1, 0, 2)
            holds = holds.reshape(batches, slots)
        if tick == sections:
            place_of, row_of, groups = groups_of(holds + order, heads)
        batch = tick - (sections - 1)
        if 0 <= batch < batches - 1:
            pair, at = batch // 2, batch % 2
            packed[pair] = pack_values(
                batch, dest[batch][None, :], outputs[1], slots, order, packed[pair], at, 2
            )
        if batch == 2:
            got = lax.all_to_all(packed[0], "table", 0, 0, tiled=True)
    rest = lax.all_to_all(packed[1], "table", 0, 0, tiled=True)
    table = owner_add(0, 2, None, got, place_of, row_of, groups, weight, order)
    table = owner_add(2, 2, table, rest, place_of, row_of, groups, weight, order)
    return (outputs[0][None], table[None])


def solution(mesh):
    placed = (
        P("section", None, "table", None),
        P("section", None, "table", None, None),
        P("section", None, None, None),
        P("section", None, None, None),
        P("section", None, None),
        P("section"),
        P("section", None, "table", None),
        P(None, "table", None),
    )
    return jax.shard_map(
        shards,
        mesh=mesh,
        in_specs=placed,
        out_specs=(P("section", None, "table", None), P("section", "table", None)),
        check_vma=False,
    )
```

```python
import functools
import math

import jax
import jax.numpy as jnp
from jax import lax
from jax.experimental import pallas as pl
from jax.experimental.pallas import tpu as pltpu
from jax.sharding import PartitionSpec as P

TABLE_DEV = 1024
HALO = 16
EPS = 1e-06
LANES = 128
STEP = 512
SPLIT = 4
MIB = 1 << 20
VMEM_LIMIT = 51 * MIB

f32 = jnp.float32
bf16 = jnp.bfloat16


def row_total(partial):
    return jnp.broadcast_to(jnp.sum(partial, -1, keepdims=True), partial.shape)


def columns(chunk):
    return pl.ds(pl.multiple_of(chunk * STEP, STEP), STEP)


def wide(narrow):
    return jnp.concatenate([narrow] * (STEP // LANES), 1)


def fold(chunk):
    return sum(chunk[:, i : i + LANES] for i in range(0, STEP, LANES))


def edges_kernel(x, top, for_next, for_last, sems):
    length = x.shape[1]
    copies = (
        pltpu.make_async_copy(x.at[:, pl.ds(length - HALO, HALO)], for_next, sems.at[0]),
        pltpu.make_async_copy(x.at[:, pl.ds(0, HALO)], for_last.at[:, pl.ds(0, HALO)], sems.at[1]),
        pltpu.make_async_copy(top.at[:, pl.ds(0, HALO)], for_last.at[:, pl.ds(HALO, HALO)], sems.at[2]),
    )
    for copy in copies:
        copy.start()
    for copy in copies:
        copy.wait()


def edges(x, top):
    batches, length, width = x.shape
    hbm = pl.BlockSpec(memory_space=pltpu.HBM)
    return pl.pallas_call(
        edges_kernel,
        out_shape=(
            jax.ShapeDtypeStruct((batches, HALO, width), bf16),
            jax.ShapeDtypeStruct((batches, 2 * HALO, width), bf16),
        ),
        in_specs=[hbm] * 2,
        out_specs=[hbm] * 2,
        scratch_shapes=[pltpu.SemaphoreType.DMA((3,))],
        compiler_params=pltpu.CompilerParams(vmem_limit_bytes=VMEM_LIMIT),
        cost_estimate=pl.CostEstimate(flops=0, bytes_accessed=4 * MIB, transcendentals=0),
        name="edges",
    )(x, top)


def values_kernel(
    memory, weight, convs, gains, v_out, low_one, high_one, low_rest, high_rest, taps,
    held, wide_held, flat, v, sems,
):
    batches, rows = held.shape[:2]
    heads, _, feature = weight.shape
    length = rows // heads
    loads = [pltpu.make_async_copy(memory.at[b], held.at[b], sems.at[0, b]) for b in range(batches)]
    copies = [pltpu.make_async_copy(weight.at[h], flat.at[h], sems.at[1, h]) for h in range(heads)]
    for copy in loads + copies:
        copy.start()
    for layer in range(taps.shape[0]):
        taps[layer] = 0.5 * convs[layer] * gains[layer : layer + 1, :]
    step = 64
    for b in range(batches):
        loads[b].wait()

        def widen(tile, carry):
            at = pl.multiple_of(tile * step, step)
            block = held[b, pl.ds(at, step), :].astype(f32)
            for c in range(block.shape[1] // LANES):
                wide_held[c, pl.ds(b * rows + at, step), :] = block[:, c * LANES : (c + 1) * LANES]
            return carry

        lax.fori_loop(0, rows // step, widen, 0)
    outs = []
    for h in range(heads):
        copies[h].wait()
        taken = [
            wide_held[c, pl.ds(h, batches * length, stride=heads), :].astype(bf16)
            for c in range(wide_held.shape[0])
        ]
        cols = pl.ds(h * feature, feature)
        v[:, cols] = jnp.dot(
            jnp.concatenate(taken, 1), flat[h], preferred_element_type=f32
        )
        outs.append(pltpu.make_async_copy(v.at[:, cols], v_out.at[:, cols], sems.at[2, h]))
        outs[-1].start()
    for b in range(batches):
        low = low_one.at[0] if b == 0 else low_rest.at[b - 1]
        high = high_one.at[0] if b == 0 else high_rest.at[b - 1]
        for i, (target, at) in enumerate(((low, 0), (high, length - HALO))):
            outs.append(
                pltpu.make_async_copy(v.at[pl.ds(b * length + at, HALO)], target, sems.at[3 + i, b])
            )
            outs[-1].start()
    for copy in outs:
        copy.wait()


def all_values(memory, weight, convs, gains):
    batches, length, heads, row_width = memory.shape
    feature = weight.shape[2]
    hbm = pl.BlockSpec(memory_space=pltpu.HBM)
    one = jax.ShapeDtypeStruct((1, HALO, heads * feature), f32)
    rest = jax.ShapeDtypeStruct((batches - 1, HALO, heads * feature), f32)
    vmem = pl.BlockSpec(memory_space=pltpu.VMEM)
    v, *halos, taps = pl.pallas_call(
        values_kernel,
        out_shape=(
            jax.ShapeDtypeStruct((batches * length, heads * feature), f32), one, one, rest, rest,
            jax.ShapeDtypeStruct(convs.shape, f32),
        ),
        in_specs=[hbm] * 2 + [vmem] * 2,
        out_specs=[hbm] * 5 + [vmem],
        scratch_shapes=[
            pltpu.VMEM((batches, length * heads, row_width), bf16),
            pltpu.VMEM((row_width // LANES, batches * length * heads, LANES), f32),
            pltpu.VMEM(weight.shape, bf16),
            pltpu.VMEM((batches * length, heads * feature), f32),
            pltpu.SemaphoreType.DMA((5, heads)),
        ],
        compiler_params=pltpu.CompilerParams(vmem_limit_bytes=VMEM_LIMIT),
        cost_estimate=pl.CostEstimate(
            flops=2 * batches * length * heads * row_width * feature,
            bytes_accessed=18 * MIB,
            transcendentals=0,
        ),
        name="all_values",
    )(memory.reshape(batches, length * heads, row_width), weight, convs, gains)
    return v.reshape(batches, length, heads * feature), halos, taps


def forward_kernel(
    batch, v_halo, carried, live_ref, xb, xm, xa, vb, vm, va, taps, order, *refs,
):
    hid_out, der_out, scal_out = refs[carried : carried + 3]
    x_win, v_win, hid, der, scal, rms_now, sems = refs[2 * carried + 3 :]
    width = xm.shape[-1]
    rows = x_win.shape[0]
    keep = rows - HALO
    chunks = width // STEP
    live = live_ref[0]
    length = xm.shape[-2]
    parts = ((xb, vb, 0, HALO), (xm, vm, HALO, length), (xa, va, HALO + length, HALO))
    loads = []
    for q in range(SPLIT):
        cols = pl.ds(q * (width // SPLIT), width // SPLIT)
        loads.append([])
        for i, (x_part, v_part, at, size) in enumerate(parts):
            here = batch if i == 1 else v_halo
            for j, (part, window, b) in enumerate(((x_part, x_win, batch), (v_part, v_win, here))):
                loads[q].append(
                    pltpu.make_async_copy(
                        part.at[b, pl.ds(0, size), cols],
                        window.at[pl.ds(at, size), cols],
                        sems.at[2 + 3 * j + i, q],
                    )
                )
                loads[q][-1].start()

    def load(chunk, sums):
        cols = columns(chunk)
        x = x_win[:, cols].astype(f32)
        v = v_win[:, cols]
        return sums[0] + fold(x * x), sums[1] + fold(v * v), sums[2] + fold(x * v)

    zero = jnp.zeros((rows, LANES), f32)
    sums = (zero, zero, zero)
    for q in range(SPLIT):
        for copy in loads[q]:
            copy.wait()
        sums = lax.fori_loop(q * chunks // SPLIT, (q + 1) * chunks // SPLIT, load, sums)
    xx, vv, xv = sums
    xv = row_total(xv)
    rx = lax.rsqrt(row_total(xx) / width + EPS)
    rv = lax.rsqrt(row_total(vv) / width + EPS)
    gate = jax.nn.sigmoid(rx * rv * xv / math.sqrt(width))
    scal[4] = rx[HALO:]
    scal[5] = rv[HALO:]
    scal[6] = xv[HALO:]
    scal[7] = gate[HALO:]
    rms_now[...] = gate

    def mix(chunk, total):
        cols = columns(chunk)
        hidden = x_win[:, cols].astype(f32) + wide(rms_now[...]) * v_win[:, cols]
        hid[0, :, cols] = hidden
        return total + fold(hidden * hidden)

    total = lax.fori_loop(0, chunks, mix, zero)

    def hidden_copy(layer):
        return pltpu.make_async_copy(
            hid.at[layer, pl.ds(HALO, keep)], hid_out.at[layer], sems.at[0, layer]
        )

    def slope_copy(layer):
        return pltpu.make_async_copy(der.at[layer], der_out.at[layer], sems.at[1, layer])

    def layer_step(layer, total):
        hidden_copy(layer).start()
        rms = lax.rsqrt(row_total(total) / width + EPS)
        scal[layer] = rms[HALO:]
        rms_now[...] = rms

        def one(chunk, total):
            cols = columns(chunk)
            hidden = hid[layer, :, cols]
            unit = hidden * wide(rms_now[...])
            mixed = taps[layer, 0:1, cols] * unit
            for k in range(1, 4):
                mixed = mixed + taps[layer, k : k + 1, cols] * pltpu.roll(unit, k, 0)
            bend = jnp.tanh(mixed)
            rise = 1.0 + bend
            silu = mixed * rise
            der[layer, :, cols] = (rise + silu * (1.0 - bend))[HALO:]
            after = hidden + silu
            hid[layer + 1, :, cols] = after
            return total + fold(after * after)

        total = lax.fori_loop(0, chunks, one, zero)
        slope_copy(layer).start()
        return total

    lax.fori_loop(0, live, layer_step, total)
    out = pltpu.make_async_copy(scal, scal_out, sems.at[0, 4])
    out.start()

    def finish(layer, carry):
        hidden_copy(layer).wait()
        slope_copy(layer).wait()
        return carry

    lax.fori_loop(0, live, finish, 0)
    out.wait()


def forward_map(batch, v_halo, live, x, x_before, x_after, v, v_before, v_after, taps, order, carry):
    length, width = x.shape[1:]
    keep = length + HALO
    rows = keep + HALO
    layers = taps.shape[0]
    hbm = pl.BlockSpec(memory_space=pltpu.HBM)
    return pl.pallas_call(
        functools.partial(forward_kernel, batch, v_halo, len(carry)),
        out_shape=(
            jax.ShapeDtypeStruct((layers, keep, width), f32),
            jax.ShapeDtypeStruct((layers, keep, width), f32),
            jax.ShapeDtypeStruct((8, keep, LANES), f32),
            *(jax.ShapeDtypeStruct(array.shape, array.dtype) for array in carry),
        ),
        in_specs=[pl.BlockSpec(memory_space=pltpu.SMEM)]
        + [hbm] * 6
        + [pl.BlockSpec(memory_space=pltpu.VMEM), pl.BlockSpec(memory_space=pltpu.SMEM)]
        + [hbm] * len(carry),
        out_specs=[hbm] * (3 + len(carry)),
        input_output_aliases={9 + i: 3 + i for i in range(len(carry))},
        scratch_shapes=[
            pltpu.VMEM((rows, width), bf16),
            pltpu.VMEM((rows, width), f32),
            pltpu.VMEM((layers + 1, rows, width), f32),
            pltpu.VMEM((layers, keep, width), f32),
            pltpu.VMEM((8, keep, LANES), f32),
            pltpu.VMEM((rows, LANES), f32),
            pltpu.SemaphoreType.DMA((8, layers + 1)),
        ],
        compiler_params=pltpu.CompilerParams(vmem_limit_bytes=VMEM_LIMIT),
        cost_estimate=pl.CostEstimate(
            flops=30 * layers * rows * width,
            bytes_accessed=16 * MIB,
            transcendentals=layers * rows * width,
        ),
        name="forward_map",
    )(live, x_before, x, x_after, v_before, v, v_after, taps, order, *carry)


def backward_kernel(
    held, info, near, near_halo, top, top_halo, x_all, v_all, taps, *refs,
):
    saved = [refs[3 * i : 3 * i + 3] for i in range(held[1])]
    refs = refs[3 * held[1] :]
    if held[2]:
        gv_held, refs = refs[1], refs[2:]
    if held[4]:
        refs = refs[1:6] + refs[7:]
    if held[3]:
        dest, refs = refs[0], refs[2:]
        packed, stacked, slots_now = refs[5], refs[-2], refs[-1]
        refs = refs[:5] + refs[6:-2]
    (
        grad_send, halo_send, grads_all, gv_all, order_out,
        hid, der, scal, v_in, g, u, coef, x_in, g_in, ga_in, gx, gv, sems,
    ) = refs
    which = info[0]
    active = info[1]
    is_top = info[2]
    live = info[3]
    length, width = grad_send.shape
    rows = g.shape[0]
    chunks = width // STEP
    quarter = width // SPLIT
    first, count = held[0], held[1]
    order_out[0] = 0

    def part(q):
        return pl.ds(pl.multiple_of(q * quarter, quarter), quarter)

    def scal_copy(i):
        return pltpu.make_async_copy(saved[i][2], scal, sems.at[2, 0])

    def layer_copies(i, layer, q):
        cols = part(q)
        return (
            pltpu.make_async_copy(
                saved[i][1].at[layer, :, cols], der.at[layer, :, cols], sems.at[1, 4 * layer + q]
            ),
            pltpu.make_async_copy(
                saved[i][0].at[layer, :, cols], hid.at[layer, :, cols], sems.at[0, 4 * layer + q]
            ),
        )

    def input_copies():
        return (
            pltpu.make_async_copy(x_all.at[which], x_in, sems.at[2, 1]),
            pltpu.make_async_copy(v_all.at[which], v_in, sems.at[2, 3]),
        )

    def grad_copies(source, source_halo):
        return (
            pltpu.make_async_copy(source, g_in, sems.at[3, 0]),
            pltpu.make_async_copy(source_halo, ga_in, sems.at[3, 1]),
        )

    def pack():
        spread_heads(gv, stacked)
        into_slots(dest, stacked, slots_now)
        feature = slots_now.shape[1]
        at = pl.ds(packed.shape[1] - feature, feature)
        copy = pltpu.make_async_copy(slots_now, packed.at[:, at], sems.at[3, 3])
        copy.start()
        copy.wait()

    @pl.when(active == 1)
    def _():
        @pl.when(is_top == 1)
        def _():
            for copy in grad_copies(top.at[which], top_halo.at[which, pl.ds(HALO, HALO)]):
                copy.start()

        if held[5]:
            @pl.when(is_top == 0)
            def _():
                for copy in grad_copies(near, near_halo):
                    copy.start()

        for i in range(count):
            @pl.when(which == first + i)
            def _():
                def begin(step, carry):
                    layer = live - 1 - step
                    for q in range(SPLIT):
                        for copy in layer_copies(i, layer, q):
                            copy.start()
                    return carry

                begin(0, 0)
                scal_copy(i).start()
                lax.fori_loop(1, live, begin, 0)

        for copy in input_copies():
            copy.start()

        for copy in grad_copies(top.at[which], top_halo.at[which, pl.ds(HALO, HALO)]):
            copy.wait()

        def into_taps(layer, cols, grad):
            size = grad.shape[0]
            slope = grad * der[layer, 0:size, cols]
            out = taps[layer, 0:1, cols] * slope
            for k in range(1, 4):
                out = out + taps[layer, k : k + 1, cols] * pltpu.roll(slope, size - k, 0)
            u[0:size, cols] = out
            return fold(out * hid[layer, 0:size, cols])

        last = live - 1
        total = jnp.zeros((rows, LANES), f32)
        for q in range(SPLIT):
            for copy in layer_copies(0, last, q):
                copy.wait()

            def start(chunk, total):
                cols = columns(chunk)
                g[0:length, cols] = g_in[:, cols].astype(f32)
                g[length:rows, cols] = ga_in[:, cols].astype(f32)
                return total + into_taps(last, cols, g[:, cols])

            total = lax.fori_loop(q * chunks // SPLIT, (q + 1) * chunks // SPLIT, start, total)
        scal_copy(0).wait()

        def coefficients(layer, total):
            size = total.shape[0]
            rms = scal[layer, 0:size]
            coef[0, 0:size] = rms
            coef[1, 0:size] = -rms * rms * rms * (row_total(total) / width)

        def through_rms(layer, cols, size):
            return g[0:size, cols] + (
                wide(coef[0, 0:size]) * u[0:size, cols]
                + wide(coef[1, 0:size]) * hid[layer, 0:size, cols]
            )

        def layer_step(size, step, total):
            layer = live - 1 - step
            coefficients(layer, total)
            for q in range(SPLIT):
                for copy in layer_copies(0, layer - 1, q):
                    copy.wait()

            def one(chunk, total):
                cols = columns(chunk)
                grad = through_rms(layer, cols, size)
                g[0:size, cols] = grad
                return total + into_taps(layer - 1, cols, grad)

            return lax.fori_loop(0, chunks, one, jnp.zeros((size, LANES), f32))

        total = lax.fori_loop(
            0, jnp.minimum(live - 1, 1), functools.partial(layer_step, rows), total
        )
        fewer = rows - HALO // 2
        total = lax.fori_loop(
            1, live - 1, functools.partial(layer_step, fewer), total[0:fewer]
        )
        coefficients(0, total[0:length])
        for copy in input_copies():
            copy.wait()

        def to_gate(chunk, total):
            cols = columns(chunk)
            grad = through_rms(0, cols, length)
            g[0:length, cols] = grad
            return total + fold(grad * v_in[:, cols])

        total = row_total(lax.fori_loop(0, chunks, to_gate, jnp.zeros((length, LANES), f32)))
        rx, rv, xv, gate = (scal[i, 0:length] for i in range(4, 8))
        both = total * gate * (1.0 - gate) * (1.0 / math.sqrt(width)) * rx * rv
        mean = xv / width
        coef[0, 0:length] = both
        coef[1, 0:length] = -both * rx * rx * mean
        coef[2, 0:length] = -both * rv * rv * mean
        coef[3, 0:length] = gate

        def finish(chunk, carry):
            cols = columns(chunk)
            grad = g[0:length, cols]
            x = x_in[:, cols].astype(f32)
            v = v_in[:, cols]
            cross = wide(coef[0, 0:length])
            grad_x = grad + cross * v + wide(coef[1, 0:length]) * x
            grad_v = wide(coef[3, 0:length]) * grad + cross * x + wide(coef[2, 0:length]) * v
            gx[:, cols] = grad_x.astype(bf16)
            gv[:, cols] = grad_v.astype(bf16)
            return carry

        outs = []
        for q in range(SPLIT):
            lax.fori_loop(q * chunks // SPLIT, (q + 1) * chunks // SPLIT, finish, 0)
            cols = part(q)
            for i, (source, target) in enumerate((
                (gx.at[:, cols], grad_send.at[:, cols]),
                (gx.at[pl.ds(0, HALO), cols], halo_send.at[:, cols]),
                (gx.at[:, cols], grads_all.at[which, :, cols]),
                (gv.at[:, cols], gv_all.at[which, :, cols]),
            )):
                outs.append(pltpu.make_async_copy(source, target, sems.at[4, 4 * i + q]))
                outs[-1].start()
        if held[3]:
            pack()
        for copy in outs:
            copy.wait()

    if held[3]:
        @pl.when(active == 0)
        def _():
            copy = pltpu.make_async_copy(gv_held.at[held[3] - 1], gv, sems.at[3, 2])
            copy.start()
            copy.wait()
            pack()


def backward_map(info, near, near_halo, top, top_halo, x, v, taps, first, saved, previous, packing=None, carry=None):
    batches, length, width = x.shape
    rows = length + HALO
    layers = taps.shape[0]
    flat = [array for group in saved for array in group]
    some = pl.BlockSpec(memory_space=pl.ANY)
    hbm = pl.BlockSpec(memory_space=pltpu.HBM)
    vmem = pl.BlockSpec(memory_space=pltpu.VMEM)
    smem = pl.BlockSpec(memory_space=pltpu.SMEM)
    operands = [info, near, near_halo, top, top_halo, x, v, taps, *flat]
    specs = [smem] + [some] * 2 + [hbm] * 4 + [vmem] + [hbm] * len(flat)
    shapes = [
        jax.ShapeDtypeStruct((length, width), bf16),
        jax.ShapeDtypeStruct((HALO, width), bf16),
        jax.ShapeDtypeStruct((batches, length, width), bf16),
        jax.ShapeDtypeStruct((batches, length, width), bf16),
        jax.ShapeDtypeStruct((1,), jnp.int32),
    ]
    out_specs = [some] * 2 + [hbm] * 2 + [smem]
    scratch = [
        pltpu.VMEM((layers, rows, width), f32),
        pltpu.VMEM((layers, rows, width), f32),
        pltpu.VMEM((8, rows, LANES), f32),
        pltpu.VMEM((length, width), f32),
        pltpu.VMEM((rows, width), f32),
        pltpu.VMEM((rows, width), f32),
        pltpu.VMEM((4, rows, LANES), f32),
        pltpu.VMEM((length, width), bf16),
        pltpu.VMEM((length, width), bf16),
        pltpu.VMEM((HALO, width), bf16),
        pltpu.VMEM((length, width), bf16),
        pltpu.VMEM((length, width), bf16),
        pltpu.SemaphoreType.DMA((5, 16)),
    ]
    aliases = {}
    if previous is not None:
        aliases = {len(operands): 2, len(operands) + 1: 3}
        operands += previous
        specs += [hbm] * 2
    if packing is not None:
        batch, dest, packed = packing
        aliases[len(operands) + 1] = 5
        operands += [dest, packed]
        specs += [vmem, hbm]
        shapes.append(jax.ShapeDtypeStruct(packed.shape, packed.dtype))
        out_specs.append(hbm)
        feature = width // 8
        scratch += [pltpu.VMEM((8 * length, feature), bf16), pltpu.VMEM((packed.shape[0], feature), bf16)]
    if carry is not None:
        aliases[len(operands)] = 5
        operands.append(carry)
        specs.append(hbm)
        shapes.append(jax.ShapeDtypeStruct(carry.shape, carry.dtype))
        out_specs.append(hbm)
    pack_flag = 0 if packing is None else packing[0] + 1
    return pl.pallas_call(
        functools.partial(
            backward_kernel,
            (first, len(saved), previous is not None, pack_flag, carry is not None, near.ndim == 2),
        ),
        out_shape=shapes,
        in_specs=specs,
        out_specs=out_specs,
        scratch_shapes=scratch,
        input_output_aliases=aliases,
        compiler_params=pltpu.CompilerParams(vmem_limit_bytes=VMEM_LIMIT),
        cost_estimate=pl.CostEstimate(
            flops=25 * layers * rows * width, bytes_accessed=14 * MIB, transcendentals=0
        ),
        name="backward_map",
    )(*operands)


def spread_heads(gv, stacked):
    length, width = gv.shape[0], stacked.shape[1]
    for head in range(stacked.shape[0] // length):
        stacked[head * length : (head + 1) * length, :] = gv[:, head * width : (head + 1) * width]


def into_slots(dest, stacked, out):
    slot = lax.broadcasted_iota(jnp.int32, (out.shape[0], stacked.shape[0]), 0)
    place = jnp.where(slot == dest[...], 1.0, 0.0).astype(bf16)
    out[...] = jnp.dot(place, stacked[...], preferred_element_type=f32).astype(bf16)


def pack_kernel(dest, gv_all, order, *refs):
    out, stacked = refs[-2:]
    spread_heads(gv_all.at[0], stacked)
    into_slots(dest, stacked, out)


def pack_values(batch, dest, gv_all, slots, order, into, at, total):
    batches, length, model = gv_all.shape
    feature = model // 8
    operands = [dest, gv_all, order] + ([] if into is None else [into])
    specs = [
        pl.BlockSpec(dest.shape, lambda i: (0, 0)),
        pl.BlockSpec((1, length, model), lambda i: (batch, 0, 0)),
        pl.BlockSpec(memory_space=pltpu.SMEM),
    ] + ([] if into is None else [pl.BlockSpec(memory_space=pltpu.HBM)])
    return pl.pallas_call(
        pack_kernel,
        out_shape=jax.ShapeDtypeStruct((slots, total * feature), bf16),
        grid=(1,),
        in_specs=specs,
        out_specs=pl.BlockSpec((slots, feature), lambda i: (0, at)),
        scratch_shapes=[pltpu.VMEM((8 * length, feature), bf16)],
        input_output_aliases={} if into is None else {3: 0},
        compiler_params=pltpu.CompilerParams(vmem_limit_bytes=VMEM_LIMIT),
        cost_estimate=pl.CostEstimate(
            flops=MIB, bytes_accessed=MIB // 16, transcendentals=0
        ),
        name="pack_values",
    )(*operands)


def owner_kernel(first, count, has_table, got, place_of, row_of, groups, order, weight_in, *refs):
    if has_table:
        table_in, refs = refs[0], refs[1:]
    table, sorted_in, joined, rows, place, weight, total, sems = refs
    heads, row_width, feature = weight.shape
    table_rows = table.shape[0]
    copies = [
        pltpu.make_async_copy(weight_in.at[h], weight.at[h], sems.at[h]) for h in range(heads)
    ]
    if has_table:
        copies.append(pltpu.make_async_copy(table_in, total, sems.at[heads]))
    for copy in copies:
        copy.start()
    slots = got.shape[0]
    room = rows.shape[1] - 128
    step = 128
    half = room // 2
    for m in range(count):
        b = first + m

        def sort(tile, carry):
            at = pl.multiple_of(tile * half, half)
            slot = lax.broadcasted_iota(jnp.int32, (half, slots), 0) + at
            pick = jnp.where(slot == place_of[b : b + 1, :], 1.0, 0.0).astype(bf16)
            sorted_in[m, pl.ds(at, half), :] = jnp.dot(
                pick, got[:, m * feature : (m + 1) * feature], preferred_element_type=f32
            ).astype(bf16)
            return carry

        lax.fori_loop(0, 2, sort, 0)

        def mark(tile, carry):
            at = pl.multiple_of(tile * step, step)
            row = lax.broadcasted_iota(jnp.int32, (step, room), 0) + at
            place[pl.ds(at, step), m * room : (m + 1) * room] = jnp.where(
                row == row_of[b : b + 1, :], 1.0, 0.0
            ).astype(bf16)
            return carry

        lax.fori_loop(0, table_rows // step, mark, 0)
        rows[m, 0:room, :] = jnp.zeros((room, row_width), bf16)

    def head_step(h, carry):
        most = groups[first, heads + h]
        for m in range(1, count):
            most = jnp.maximum(most, groups[first + m, heads + h])

        def multiply(tile, carry):
            ats = []
            for m in range(count):
                at = jnp.where(
                    tile < groups[first + m, heads + h], groups[first + m, h] + tile * step, room
                )
                ats.append(pl.ds(pl.multiple_of(at, 16), step))
                joined[m * step : (m + 1) * step, :] = sorted_in[m, ats[m], :]
            out = lax.dot_general(
                joined[...], weight[h], (((1,), (1,)), ((), ())), preferred_element_type=f32
            ).astype(bf16)
            for m in range(count):
                rows[m, ats[m], :] = out[m * step : (m + 1) * step]
            return carry

        return lax.fori_loop(0, most, multiply, carry)

    for h in range(heads):
        copies[h].wait()
        head_step(h, 0)
    if has_table:
        copies[heads].wait()
    tile = 256
    outs = []
    for block in range(row_width // tile):
        cols = pl.ds(block * tile, tile)
        part = None
        for m in range(count):
            more = jnp.dot(
                place[:, m * room : (m + 1) * room], rows[m, 0:room, cols], preferred_element_type=f32
            )
            part = more if part is None else part + more
        if has_table:
            part = part + total[:, cols]
        total[:, cols] = part
        outs.append(
            pltpu.make_async_copy(
                total.at[:, cols], table.at[:, cols], sems.at[heads + 1 + block]
            )
        )
        outs[-1].start()
    for copy in outs:
        copy.wait()


def owner_add(first, count, table, got, place_of, row_of, groups, weight, order):
    heads, row_width, feature = weight.shape
    slots = got.shape[0]
    room = row_of.shape[1]
    vmem = pl.BlockSpec(memory_space=pltpu.VMEM)
    smem = pl.BlockSpec(memory_space=pltpu.SMEM)
    operands = [got, place_of, row_of, groups, order, weight]
    hbm = pl.BlockSpec(memory_space=pltpu.HBM)
    specs = [vmem, vmem, vmem, smem, smem, hbm]
    if table is not None:
        operands.append(table)
        specs.append(hbm)
    return pl.pallas_call(
        functools.partial(owner_kernel, first, count, table is not None),
        out_shape=jax.ShapeDtypeStruct((TABLE_DEV, row_width), f32),
        in_specs=specs,
        out_specs=hbm,
        scratch_shapes=[
            pltpu.VMEM((count, room + 128, feature), bf16),
            pltpu.VMEM((count * 128, feature), bf16),
            pltpu.VMEM((count, room + 128, row_width), bf16),
            pltpu.VMEM((TABLE_DEV, count * room), bf16),
            pltpu.VMEM(weight.shape, bf16),
            pltpu.VMEM((TABLE_DEV, row_width), f32),
            pltpu.SemaphoreType.DMA((heads + 1 + row_width // 256,)),
        ],
        compiler_params=pltpu.CompilerParams(vmem_limit_bytes=VMEM_LIMIT),
        cost_estimate=pl.CostEstimate(
            flops=6 * count * slots * row_width * TABLE_DEV,
            bytes_accessed=18 * MIB,
            transcendentals=0,
        ),
        name="owner_add",
    )(*operands)


def slots_of(row_ids, owners, capacity):
    batches, length, heads = row_ids.shape
    ids = row_ids.transpose(0, 2, 1).reshape(batches, heads * length)
    owner = ids // TABLE_DEV
    local = ids - owner * TABLE_DEV
    head = jnp.arange(heads * length, dtype=jnp.int32) // length
    order = jnp.arange(heads * length, dtype=jnp.int32)
    ahead = (owner[:, None, :] == owner[:, :, None]) & (order[None, :] < order[:, None])
    rank = jnp.sum(ahead.astype(jnp.int32), -1)
    dest = owner * capacity + rank
    code = local * heads + head
    slot = jnp.arange(owners * capacity, dtype=jnp.int32)
    hit = dest[:, None, :] == slot[:, None]
    holds = jnp.sum(jnp.where(hit, code[:, None, :] + 1, 0), -1) - 1
    return dest, holds


def groups_of(holds, heads):
    batches, slots = holds.shape
    room = -(-(slots + 15 * heads) // 128) * 128
    valid = holds >= 0
    head = jnp.where(valid, holds % heads, -1)
    member = head[..., None] == jnp.arange(heads, dtype=jnp.int32)
    order = jnp.arange(slots, dtype=jnp.int32)
    below = (order[None, :] < order[:, None]).astype(bf16)
    rank = jnp.einsum("ij,bjh->bih", below, member.astype(bf16), preferred_element_type=f32)
    counts = jnp.sum(member.astype(jnp.int32), 1)
    padded = (counts + 15) // 16 * 16
    number = jnp.arange(heads, dtype=jnp.int32)
    starts = jnp.sum(jnp.where(number[None, :] < number[:, None], padded[:, None, :], 0), -1)
    place = jnp.sum(jnp.where(member, rank.astype(jnp.int32) + starts[:, None, :] + 1, 0), -1) - 1
    spot = jnp.arange(room, dtype=jnp.int32)
    hit = place[:, None, :] == spot[:, None]
    row = jnp.sum(jnp.where(hit, (holds // heads)[:, None, :] + 1, 0), -1) - 1
    groups = jnp.concatenate([starts, (counts + 127) // 128], 1)
    return place, row, groups


def shards(
    saved_inputs, memory, value_weight, conv_weight, norm_gain, layer_counts, row_ids, out_grad
):
    section = lax.axis_index("section")
    sections = lax.axis_size("section")
    owners = lax.axis_size("table")
    batches, length, width = out_grad.shape
    heads = memory.shape[3]
    capacity = 3 * length * heads // (2 * owners)
    slots = owners * capacity
    weight = value_weight[0]
    live = layer_counts[0]
    x = saved_inputs[0]
    is_top = section == sections - 1

    to_next = [(i, i + 1) for i in range(owners - 1)]
    to_last = [(i + 1, i) for i in range(owners - 1)]
    down = [(i + 1, i) for i in range(sections - 1)]
    down_halo = [
        ((i + 1) * owners + t + 1, i * owners + t)
        for i in range(sections - 1)
        for t in range(owners - 1)
    ]
    for_next, for_last = edges(x, out_grad)
    x_before = lax.ppermute(for_next, "table", to_next)
    x_after = lax.ppermute(for_last, "table", to_last)
    v, (low_one, high_one, low_rest, high_rest), taps = all_values(
        memory[0], weight, conv_weight[0], norm_gain[0]
    )
    v_before = lax.ppermute(high_one, "table", to_next)
    v_after = lax.ppermute(low_one, "table", to_last)

    saved = []
    outputs = table = dest = holds = place_of = row_of = groups = got = None
    packed = [None, None]
    order = jnp.zeros((1,), jnp.int32)
    near = near_halo = order
    ticks = batches + sections - 1
    for tick in range(ticks):
        if tick < batches:
            carry = (high_rest, low_rest) if tick == 0 else ()
            *state, = forward_map(
                tick, max(tick - 1, 0), live.reshape(1), x, x_before, x_after,
                v, v_before, v_after, taps, order, carry,
            )
            saved.append(state[:3])
            if tick == 0:
                v_before = lax.ppermute(state[3], "table", to_next)
                v_after = lax.ppermute(state[4], "table", to_last)
        position = tick - (sections - 1 - section)
        which = jnp.clip(position, 0, batches - 1)
        active = (position >= 0) & (position < batches)
        info = jnp.stack([which, active, is_top, live]).astype(jnp.int32)
        first = max(0, tick - (sections - 1))
        packing = (batches - 1, dest[batches - 1][None, :], packed[1]) if tick == ticks - 1 else None
        grad_send, halo_send, *outputs = backward_map(
            info, near, near_halo, out_grad, x_after, x, v, taps,
            first, saved[first : tick + 1], outputs, packing, packed[0] if tick == ticks - 2 else None,
        )
        if tick == ticks - 2:
            packed[0] = outputs.pop()
            got = lax.all_to_all(packed[0], "table", 0, 0, tiled=True)
        if packing is not None:
            packed[1] = outputs.pop()
        order = outputs.pop()
        if tick < ticks - 1:
            near = lax.ppermute(grad_send, "section", down)
            near_halo = lax.ppermute(halo_send, ("section", "table"), down_halo)
        if tick == 0:
            dest, holds = slots_of(row_ids[0] + order, owners, capacity)
            holds = holds.reshape(batches, owners, capacity).transpose(1, 0, 2)
            holds = holds.reshape(owners, batches * capacity)
        if tick == sections:
            holds = lax.all_to_all(holds + order, "table", 0, 0, tiled=True)
            holds = holds.reshape(owners, batches, capacity).transpose(1, 0, 2)
            holds = holds.reshape(batches, slots)
        if tick == sections + 1:
            place_of, row_of, groups = groups_of(holds + order, heads)
        batch = tick - (sections - 1)
        if 0 <= batch < batches - 1:
            pair, at = batch // 2, batch % 2
            packed[pair] = pack_values(
                batch, dest[batch][None, :], outputs[1], slots, order, packed[pair], at, 2
            )
    rest = lax.all_to_all(packed[1], "table", 0, 0, tiled=True)
    table = owner_add(0, 2, None, got, place_of, row_of, groups, weight, order)
    table = owner_add(2, 2, table, rest, place_of, row_of, groups, weight, order)
    return (outputs[0][None], table[None])


def solution(mesh):
    placed = (
        P("section", None, "table", None),
        P("section", None, "table", None, None),
        P("section", None, None, None),
        P("section", None, None, None),
        P("section", None, None),
        P("section"),
        P("section", None, "table", None),
        P(None, "table", None),
    )
    return jax.shard_map(
        shards,
        mesh=mesh,
        in_specs=placed,
        out_specs=(P("section", None, "table", None), P("section", "table", None)),
        check_vma=False,
    )
```

```python
import functools
import math

import jax
import jax.numpy as jnp
from jax import lax
from jax.experimental import pallas as pl
from jax.experimental.pallas import tpu as pltpu
from jax.sharding import PartitionSpec as P

TABLE_DEV = 1024
HALO = 16
EPS = 1e-06
LANES = 128
STEP = 512
SPLIT = 4
MIB = 1 << 20
VMEM_LIMIT = 51 * MIB

f32 = jnp.float32
bf16 = jnp.bfloat16


def row_total(partial):
    return jnp.broadcast_to(jnp.sum(partial, -1, keepdims=True), partial.shape)


def columns(chunk):
    return pl.ds(pl.multiple_of(chunk * STEP, STEP), STEP)


def wide(narrow):
    return jnp.concatenate([narrow] * (STEP // LANES), 1)


def fold(chunk):
    return sum(chunk[:, i : i + LANES] for i in range(0, STEP, LANES))


def values_kernel(
    memory, weight, convs, gains, x, top, v_out, next_one, last_one, next_rest, last_rest, taps,
    held, wide_held, flat, v, for_next, for_last, sems,
):
    batches, rows = held.shape[:2]
    heads, _, feature = weight.shape
    length = rows // heads
    loads = [pltpu.make_async_copy(memory.at[b], held.at[b], sems.at[0, b]) for b in range(batches)]
    copies = [pltpu.make_async_copy(weight.at[h], flat.at[h], sems.at[1, h]) for h in range(heads)]
    low, high = pl.ds(0, HALO), pl.ds(length - HALO, HALO)
    edges = (
        pltpu.make_async_copy(x.at[:, high], for_next.at[:, pl.ds(0, HALO)], sems.at[3, 0]),
        pltpu.make_async_copy(x.at[:, low], for_last.at[:, pl.ds(0, HALO)], sems.at[3, 1]),
        pltpu.make_async_copy(top.at[:, low], for_last.at[:, pl.ds(HALO, HALO)], sems.at[3, 2]),
    )
    for copy in (*loads, *copies, *edges):
        copy.start()
    for layer in range(taps.shape[0]):
        taps[layer] = 0.5 * convs[layer] * gains[layer : layer + 1, :]
    step = 64
    for b in range(batches):
        loads[b].wait()

        def widen(tile, carry):
            at = pl.multiple_of(tile * step, step)
            block = held[b, pl.ds(at, step), :].astype(f32)
            for c in range(block.shape[1] // LANES):
                wide_held[c, pl.ds(b * rows + at, step), :] = block[:, c * LANES : (c + 1) * LANES]
            return carry

        lax.fori_loop(0, rows // step, widen, 0)
    outs = []
    for h in range(heads):
        copies[h].wait()
        taken = [
            wide_held[c, pl.ds(h, batches * length, stride=heads), :].astype(bf16)
            for c in range(wide_held.shape[0])
        ]
        cols = pl.ds(h * feature, feature)
        v[:, cols] = jnp.dot(
            jnp.concatenate(taken, 1), flat[h], preferred_element_type=f32
        )
        outs.append(pltpu.make_async_copy(v.at[:, cols], v_out.at[:, cols], sems.at[2, h]))
        outs[-1].start()
        for b in range(batches):
            for target, at, first in (
                (for_next, (b + 1) * length - HALO, HALO), (for_last, b * length, 2 * HALO)
            ):
                edge = v[at : at + HALO, cols]
                main = edge.astype(bf16)
                target[b, first : first + HALO, cols] = main
                target[b, first + HALO : first + 2 * HALO, cols] = (edge - main.astype(f32)).astype(bf16)
    for copy in edges:
        copy.wait()
    for i, (source, one, rest) in enumerate(
        ((for_next, next_one, next_rest), (for_last, last_one, last_rest))
    ):
        outs.append(pltpu.make_async_copy(source.at[pl.ds(0, 1)], one, sems.at[4, i]))
        outs.append(
            pltpu.make_async_copy(source.at[pl.ds(1, batches - 1)], rest, sems.at[4, 2 + i])
        )
        outs[-1].start()
        outs[-2].start()
    for copy in outs:
        copy.wait()


def all_values(memory, weight, convs, gains, x, top):
    batches, length, heads, row_width = memory.shape
    feature = weight.shape[2]
    width = heads * feature
    hbm = pl.BlockSpec(memory_space=pltpu.HBM)
    vmem = pl.BlockSpec(memory_space=pltpu.VMEM)
    v, *halos, taps = pl.pallas_call(
        values_kernel,
        out_shape=(
            jax.ShapeDtypeStruct((batches * length, width), f32),
            jax.ShapeDtypeStruct((1, 3 * HALO, width), bf16),
            jax.ShapeDtypeStruct((1, 4 * HALO, width), bf16),
            jax.ShapeDtypeStruct((batches - 1, 3 * HALO, width), bf16),
            jax.ShapeDtypeStruct((batches - 1, 4 * HALO, width), bf16),
            jax.ShapeDtypeStruct(convs.shape, f32),
        ),
        in_specs=[hbm] * 2 + [vmem] * 2 + [hbm] * 2,
        out_specs=[hbm] * 5 + [vmem],
        scratch_shapes=[
            pltpu.VMEM((batches, length * heads, row_width), bf16),
            pltpu.VMEM((row_width // LANES, batches * length * heads, LANES), f32),
            pltpu.VMEM(weight.shape, bf16),
            pltpu.VMEM((batches * length, width), f32),
            pltpu.VMEM((batches, 3 * HALO, width), bf16),
            pltpu.VMEM((batches, 4 * HALO, width), bf16),
            pltpu.SemaphoreType.DMA((5, heads)),
        ],
        compiler_params=pltpu.CompilerParams(vmem_limit_bytes=VMEM_LIMIT),
        cost_estimate=pl.CostEstimate(
            flops=2 * batches * length * heads * row_width * feature,
            bytes_accessed=18 * MIB,
            transcendentals=0,
        ),
        name="all_values",
    )(memory.reshape(batches, length * heads, row_width), weight, convs, gains, x, top)
    return v.reshape(batches, length, width), halos, taps


def forward_kernel(
    batch, halo, carried, live_ref, x, v, before, behind, taps, order, *refs,
):
    hid_out, der_out, scal_out = refs[carried : carried + 3]
    x_win, v_win, terms, hid, der, scal, rms_now, sems = refs[2 * carried + 3 :]
    length, width = x.shape[1:]
    rows = x_win.shape[0]
    keep = rows - HALO
    chunks = width // STEP
    live = live_ref[0]
    end = HALO + length
    parts = (
        (x.at[batch], 0, length, x_win, HALO),
        (v.at[batch], 0, length, v_win, HALO),
        (before.at[halo], 0, HALO, x_win, 0),
        (before.at[halo], HALO, 2 * HALO, terms, 0),
        (behind.at[halo], 0, HALO, x_win, end),
        (behind.at[halo], 2 * HALO, 2 * HALO, terms, 2 * HALO),
    )
    loads = []
    for q in range(SPLIT):
        cols = pl.ds(q * (width // SPLIT), width // SPLIT)
        loads.append([])
        for i, (source, first, size, window, at) in enumerate(parts):
            loads[q].append(
                pltpu.make_async_copy(
                    source.at[pl.ds(first, size), cols],
                    window.at[pl.ds(at, size), cols],
                    sems.at[2 + i, q],
                )
            )
            loads[q][-1].start()

    def load(chunk, sums):
        cols = columns(chunk)
        for at, first in ((0, 0), (end, 2 * HALO)):
            v_win[at : at + HALO, cols] = terms[first : first + HALO, cols].astype(f32) + terms[
                first + HALO : first + 2 * HALO, cols
            ].astype(f32)
        x = x_win[:, cols].astype(f32)
        v = v_win[:, cols]
        return sums[0] + fold(x * x), sums[1] + fold(v * v), sums[2] + fold(x * v)

    zero = jnp.zeros((rows, LANES), f32)
    sums = (zero, zero, zero)
    for q in range(SPLIT):
        for copy in loads[q]:
            copy.wait()
        sums = lax.fori_loop(q * chunks // SPLIT, (q + 1) * chunks // SPLIT, load, sums)
    xx, vv, xv = sums
    xv = row_total(xv)
    rx = lax.rsqrt(row_total(xx) / width + EPS)
    rv = lax.rsqrt(row_total(vv) / width + EPS)
    gate = jax.nn.sigmoid(rx * rv * xv / math.sqrt(width))
    scal[4] = rx[HALO:]
    scal[5] = rv[HALO:]
    scal[6] = xv[HALO:]
    scal[7] = gate[HALO:]
    rms_now[...] = gate

    def mix(chunk, total):
        cols = columns(chunk)
        hidden = x_win[:, cols].astype(f32) + wide(rms_now[...]) * v_win[:, cols]
        hid[0, :, cols] = hidden
        return total + fold(hidden * hidden)

    total = lax.fori_loop(0, chunks, mix, zero)

    def hidden_copy(layer):
        return pltpu.make_async_copy(
            hid.at[layer, pl.ds(HALO, keep)], hid_out.at[layer], sems.at[0, layer]
        )

    def slope_copy(layer):
        return pltpu.make_async_copy(der.at[layer], der_out.at[layer], sems.at[1, layer])

    def layer_step(layer, total):
        hidden_copy(layer).start()
        rms = lax.rsqrt(row_total(total) / width + EPS)
        scal[layer] = rms[HALO:]
        rms_now[...] = rms

        def one(chunk, total):
            cols = columns(chunk)
            hidden = hid[layer, :, cols]
            unit = hidden * wide(rms_now[...])
            mixed = taps[layer, 0:1, cols] * unit
            for k in range(1, 4):
                mixed = mixed + taps[layer, k : k + 1, cols] * pltpu.roll(unit, k, 0)
            bend = jnp.tanh(mixed)
            rise = 1.0 + bend
            silu = mixed * rise
            der[layer, :, cols] = (rise + silu * (1.0 - bend))[HALO:]
            after = hidden + silu
            hid[layer + 1, :, cols] = after
            return total + fold(after * after)

        total = lax.fori_loop(0, chunks, one, zero)
        slope_copy(layer).start()
        return total

    lax.fori_loop(0, live, layer_step, total)
    out = pltpu.make_async_copy(scal, scal_out, sems.at[0, 4])
    out.start()

    def finish(layer, carry):
        hidden_copy(layer).wait()
        slope_copy(layer).wait()
        return carry

    lax.fori_loop(0, live, finish, 0)
    out.wait()


def forward_map(batch, halo, live, x, v, before, behind, taps, order, carry):
    length, width = x.shape[1:]
    keep = length + HALO
    rows = keep + HALO
    layers = taps.shape[0]
    hbm = pl.BlockSpec(memory_space=pltpu.HBM)
    return pl.pallas_call(
        functools.partial(forward_kernel, batch, halo, len(carry)),
        out_shape=(
            jax.ShapeDtypeStruct((layers, keep, width), f32),
            jax.ShapeDtypeStruct((layers, keep, width), f32),
            jax.ShapeDtypeStruct((8, keep, LANES), f32),
            *(jax.ShapeDtypeStruct(array.shape, array.dtype) for array in carry),
        ),
        in_specs=[pl.BlockSpec(memory_space=pltpu.SMEM)]
        + [hbm] * 4
        + [pl.BlockSpec(memory_space=pltpu.VMEM), pl.BlockSpec(memory_space=pltpu.SMEM)]
        + [hbm] * len(carry),
        out_specs=[hbm] * (3 + len(carry)),
        input_output_aliases={7 + i: 3 + i for i in range(len(carry))},
        scratch_shapes=[
            pltpu.VMEM((rows, width), bf16),
            pltpu.VMEM((rows, width), f32),
            pltpu.VMEM((4 * HALO, width), bf16),
            pltpu.VMEM((layers + 1, rows, width), f32),
            pltpu.VMEM((layers, keep, width), f32),
            pltpu.VMEM((8, keep, LANES), f32),
            pltpu.VMEM((rows, LANES), f32),
            pltpu.SemaphoreType.DMA((8, layers + 1)),
        ],
        compiler_params=pltpu.CompilerParams(vmem_limit_bytes=VMEM_LIMIT),
        cost_estimate=pl.CostEstimate(
            flops=30 * layers * rows * width,
            bytes_accessed=16 * MIB,
            transcendentals=layers * rows * width,
        ),
        name="forward_map",
    )(live, x, v, before, behind, taps, order, *carry)


def backward_kernel(
    held, info, near, near_halo, top, behind_one, behind_rest, x_all, v_all, taps, *refs,
):
    saved = [refs[3 * i : 3 * i + 3] for i in range(held[1])]
    refs = refs[3 * held[1] :]
    if held[2]:
        gv_held, refs = refs[1], refs[2:]
    refs = refs[held[5] :]
    if held[3]:
        dest, refs = refs[0], refs[1:]
        packed, stacked, slots_now = refs[5], refs[-2], refs[-1]
        refs = refs[:5] + refs[6:-2]
    (
        grad_send, halo_send, grads_all, gv_all, order_out,
        hid, der, scal, v_in, g, u, coef, x_in, g_in, ga_in, gx, gv, sems,
    ) = refs
    which = info[0]
    active = info[1]
    is_top = info[2]
    live = info[3]
    length, width = grad_send.shape
    rows = g.shape[0]
    chunks = width // STEP
    quarter = width // SPLIT
    first, count = held[0], held[1]
    order_out[0] = 0

    def part(q):
        return pl.ds(pl.multiple_of(q * quarter, quarter), quarter)

    def scal_copy(i):
        return pltpu.make_async_copy(saved[i][2], scal, sems.at[2, 0])

    def layer_copies(i, layer, q):
        cols = part(q)
        return (
            pltpu.make_async_copy(
                saved[i][1].at[layer, :, cols], der.at[layer, :, cols], sems.at[1, 4 * layer + q]
            ),
            pltpu.make_async_copy(
                saved[i][0].at[layer, :, cols], hid.at[layer, :, cols], sems.at[0, 4 * layer + q]
            ),
        )

    def input_copies():
        return (
            pltpu.make_async_copy(x_all.at[which], x_in, sems.at[2, 1]),
            pltpu.make_async_copy(v_all.at[which], v_in, sems.at[2, 3]),
        )

    def grad_copies(source, source_halo):
        return (
            pltpu.make_async_copy(source, g_in, sems.at[3, 0]),
            pltpu.make_async_copy(source_halo, ga_in, sems.at[3, 1]),
        )

    def pack():
        spread_heads(gv, stacked)
        into_slots(dest, stacked, slots_now)
        copy = pltpu.make_async_copy(slots_now, packed, sems.at[3, 3])
        copy.start()
        copy.wait()

    @pl.when(active == 1)
    def _():
        @pl.when(is_top == 1)
        def _():
            for i, source in ((0, behind_one.at[0]), (1, behind_rest.at[jnp.maximum(which - 1, 0)])):
                @pl.when(jnp.minimum(which, 1) == i)
                def _():
                    for copy in grad_copies(top.at[which], source.at[pl.ds(HALO, HALO)]):
                        copy.start()

        if held[4]:
            @pl.when(is_top == 0)
            def _():
                for copy in grad_copies(near, near_halo):
                    copy.start()

        for i in range(count):
            @pl.when(which == first + i)
            def _():
                def begin(step, carry):
                    layer = live - 1 - step
                    for q in range(SPLIT):
                        for copy in layer_copies(i, layer, q):
                            copy.start()
                    return carry

                begin(0, 0)
                scal_copy(i).start()
                lax.fori_loop(1, live, begin, 0)

        for copy in input_copies():
            copy.start()

        for copy in grad_copies(top.at[which], behind_one.at[0, pl.ds(HALO, HALO)]):
            copy.wait()

        def into_taps(layer, cols, grad):
            size = grad.shape[0]
            slope = grad * der[layer, 0:size, cols]
            out = taps[layer, 0:1, cols] * slope
            for k in range(1, 4):
                out = out + taps[layer, k : k + 1, cols] * pltpu.roll(slope, size - k, 0)
            u[0:size, cols] = out
            return fold(out * hid[layer, 0:size, cols])

        last = live - 1
        total = jnp.zeros((rows, LANES), f32)
        for q in range(SPLIT):
            for copy in layer_copies(0, last, q):
                copy.wait()

            def start(chunk, total):
                cols = columns(chunk)
                g[0:length, cols] = g_in[:, cols].astype(f32)
                g[length:rows, cols] = ga_in[:, cols].astype(f32)
                return total + into_taps(last, cols, g[:, cols])

            total = lax.fori_loop(q * chunks // SPLIT, (q + 1) * chunks // SPLIT, start, total)
        scal_copy(0).wait()

        def coefficients(layer, total):
            size = total.shape[0]
            rms = scal[layer, 0:size]
            coef[0, 0:size] = rms
            coef[1, 0:size] = -rms * rms * rms * (row_total(total) / width)

        def through_rms(layer, cols, size):
            return g[0:size, cols] + (
                wide(coef[0, 0:size]) * u[0:size, cols]
                + wide(coef[1, 0:size]) * hid[layer, 0:size, cols]
            )

        def layer_step(size, step, total):
            layer = live - 1 - step
            coefficients(layer, total)
            for q in range(SPLIT):
                for copy in layer_copies(0, layer - 1, q):
                    copy.wait()

            def one(chunk, total):
                cols = columns(chunk)
                grad = through_rms(layer, cols, size)
                g[0:size, cols] = grad
                return total + into_taps(layer - 1, cols, grad)

            return lax.fori_loop(0, chunks, one, jnp.zeros((size, LANES), f32))

        total = lax.fori_loop(
            0, jnp.minimum(live - 1, 1), functools.partial(layer_step, rows), total
        )
        fewer = rows - HALO // 2
        total = lax.fori_loop(
            1, live - 1, functools.partial(layer_step, fewer), total[0:fewer]
        )
        coefficients(0, total[0:length])
        for copy in input_copies():
            copy.wait()

        def to_gate(chunk, total):
            cols = columns(chunk)
            grad = through_rms(0, cols, length)
            g[0:length, cols] = grad
            return total + fold(grad * v_in[:, cols])

        total = row_total(lax.fori_loop(0, chunks, to_gate, jnp.zeros((length, LANES), f32)))
        rx, rv, xv, gate = (scal[i, 0:length] for i in range(4, 8))
        both = total * gate * (1.0 - gate) * (1.0 / math.sqrt(width)) * rx * rv
        mean = xv / width
        coef[0, 0:length] = both
        coef[1, 0:length] = -both * rx * rx * mean
        coef[2, 0:length] = -both * rv * rv * mean
        coef[3, 0:length] = gate

        def finish(chunk, carry):
            cols = columns(chunk)
            grad = g[0:length, cols]
            x = x_in[:, cols].astype(f32)
            v = v_in[:, cols]
            cross = wide(coef[0, 0:length])
            grad_x = grad + cross * v + wide(coef[1, 0:length]) * x
            grad_v = wide(coef[3, 0:length]) * grad + cross * x + wide(coef[2, 0:length]) * v
            gx[:, cols] = grad_x.astype(bf16)
            gv[:, cols] = grad_v.astype(bf16)
            return carry

        outs = []
        for q in range(SPLIT):
            lax.fori_loop(q * chunks // SPLIT, (q + 1) * chunks // SPLIT, finish, 0)
            cols = part(q)
            for i, (source, target) in enumerate((
                (gx.at[:, cols], grad_send.at[:, cols]),
                (gx.at[pl.ds(0, HALO), cols], halo_send.at[:, cols]),
                (gx.at[:, cols], grads_all.at[which, :, cols]),
                (gv.at[:, cols], gv_all.at[which, :, cols]),
            )):
                outs.append(pltpu.make_async_copy(source, target, sems.at[4, 4 * i + q]))
                outs[-1].start()
        if held[3]:
            pack()
        for copy in outs:
            copy.wait()

    if held[3]:
        @pl.when(active == 0)
        def _():
            copy = pltpu.make_async_copy(gv_held.at[held[3] - 1], gv, sems.at[3, 2])
            copy.start()
            copy.wait()
            pack()


def backward_map(info, near, near_halo, top, behind_one, behind_rest, x, v, taps, first, saved, previous, packing, ready):
    batches, length, width = x.shape
    rows = length + HALO
    layers = taps.shape[0]
    flat = [array for group in saved for array in group]
    some = pl.BlockSpec(memory_space=pl.ANY)
    hbm = pl.BlockSpec(memory_space=pltpu.HBM)
    vmem = pl.BlockSpec(memory_space=pltpu.VMEM)
    smem = pl.BlockSpec(memory_space=pltpu.SMEM)
    operands = [info, near, near_halo, top, behind_one, behind_rest, x, v, taps, *flat]
    specs = [smem] + [some] * 2 + [hbm] * 5 + [vmem] + [hbm] * len(flat)
    shapes = [
        jax.ShapeDtypeStruct((length, width), bf16),
        jax.ShapeDtypeStruct((HALO, width), bf16),
        jax.ShapeDtypeStruct((batches, length, width), bf16),
        jax.ShapeDtypeStruct((batches, length, width), bf16),
        jax.ShapeDtypeStruct((1,), jnp.int32),
    ]
    out_specs = [some] * 2 + [hbm] * 2 + [smem]
    scratch = [
        pltpu.VMEM((layers, rows, width), f32),
        pltpu.VMEM((layers, rows, width), f32),
        pltpu.VMEM((8, rows, LANES), f32),
        pltpu.VMEM((length, width), f32),
        pltpu.VMEM((rows, width), f32),
        pltpu.VMEM((rows, width), f32),
        pltpu.VMEM((4, rows, LANES), f32),
        pltpu.VMEM((length, width), bf16),
        pltpu.VMEM((length, width), bf16),
        pltpu.VMEM((HALO, width), bf16),
        pltpu.VMEM((length, width), bf16),
        pltpu.VMEM((length, width), bf16),
        pltpu.SemaphoreType.DMA((5, 16)),
    ]
    aliases = {}
    if previous is not None:
        aliases = {len(operands): 2, len(operands) + 1: 3}
        operands += previous
        specs += [hbm] * 2
    operands += ready
    specs += [some] * len(ready)
    if packing is not None:
        batch, dest, slots = packing
        operands.append(dest)
        specs.append(vmem)
        feature = width // 8
        shapes.append(jax.ShapeDtypeStruct((slots, feature), bf16))
        out_specs.append(hbm)
        scratch += [pltpu.VMEM((8 * length, feature), bf16), pltpu.VMEM((slots, feature), bf16)]
    pack_flag = 0 if packing is None else packing[0] + 1
    return pl.pallas_call(
        functools.partial(
            backward_kernel,
            (first, len(saved), previous is not None, pack_flag, near.ndim == 2, len(ready)),
        ),
        out_shape=shapes,
        in_specs=specs,
        out_specs=out_specs,
        scratch_shapes=scratch,
        input_output_aliases=aliases,
        compiler_params=pltpu.CompilerParams(vmem_limit_bytes=VMEM_LIMIT),
        cost_estimate=pl.CostEstimate(
            flops=25 * layers * rows * width, bytes_accessed=100 * MIB, transcendentals=0
        ),
        name="backward_map",
    )(*operands)


def spread_heads(gv, stacked):
    length, width = gv.shape[0], stacked.shape[1]
    for head in range(stacked.shape[0] // length):
        stacked[head * length : (head + 1) * length, :] = gv[:, head * width : (head + 1) * width]


def into_slots(dest, stacked, out):
    slot = lax.broadcasted_iota(jnp.int32, (out.shape[0], stacked.shape[0]), 0)
    place = jnp.where(slot == dest[...], 1.0, 0.0).astype(bf16)
    out[...] = jnp.dot(place, stacked[...], preferred_element_type=f32).astype(bf16)


def pack_kernel(dest, gv_all, order, *refs):
    out, stacked = refs[-2:]
    spread_heads(gv_all.at[0], stacked)
    into_slots(dest, stacked, out)


def pack_values(batch, dest, gv_all, slots, order, into, at, total):
    batches, length, model = gv_all.shape
    feature = model // 8
    operands = [dest, gv_all, order] + ([] if into is None else [into])
    specs = [
        pl.BlockSpec(dest.shape, lambda i: (0, 0)),
        pl.BlockSpec((1, length, model), lambda i: (batch, 0, 0)),
        pl.BlockSpec(memory_space=pltpu.SMEM),
    ] + ([] if into is None else [pl.BlockSpec(memory_space=pltpu.HBM)])
    return pl.pallas_call(
        pack_kernel,
        out_shape=jax.ShapeDtypeStruct((slots, total * feature), bf16),
        grid=(1,),
        in_specs=specs,
        out_specs=pl.BlockSpec((slots, feature), lambda i: (0, at)),
        scratch_shapes=[pltpu.VMEM((8 * length, feature), bf16)],
        input_output_aliases={} if into is None else {3: 0},
        compiler_params=pltpu.CompilerParams(vmem_limit_bytes=VMEM_LIMIT),
        cost_estimate=pl.CostEstimate(
            flops=MIB, bytes_accessed=MIB // 16, transcendentals=0
        ),
        name="pack_values",
    )(*operands)


def owner_kernel(first, count, has_table, got, place_of, row_of, groups, order, weight_in, *refs):
    if has_table:
        table_in, refs = refs[0], refs[1:]
    table, sorted_in, joined, rows, place, weight, total, sems = refs
    heads, row_width, feature = weight.shape
    table_rows = table.shape[0]
    copies = [
        pltpu.make_async_copy(weight_in.at[h], weight.at[h], sems.at[h]) for h in range(heads)
    ]
    if has_table:
        copies.append(pltpu.make_async_copy(table_in, total, sems.at[heads]))
    for copy in copies:
        copy.start()
    slots = got.shape[0]
    room = rows.shape[1] - 128
    step = 128
    half = room // 2
    for m in range(count):
        b = first + m

        def sort(tile, carry):
            at = pl.multiple_of(tile * half, half)
            slot = lax.broadcasted_iota(jnp.int32, (half, slots), 0) + at
            pick = jnp.where(slot == place_of[b : b + 1, :], 1.0, 0.0).astype(bf16)
            sorted_in[m, pl.ds(at, half), :] = jnp.dot(
                pick, got[:, m * feature : (m + 1) * feature], preferred_element_type=f32
            ).astype(bf16)
            return carry

        lax.fori_loop(0, 2, sort, 0)

        def mark(tile, carry):
            at = pl.multiple_of(tile * step, step)
            row = lax.broadcasted_iota(jnp.int32, (step, room), 0) + at
            place[pl.ds(at, step), m * room : (m + 1) * room] = jnp.where(
                row == row_of[b : b + 1, :], 1.0, 0.0
            ).astype(bf16)
            return carry

        lax.fori_loop(0, table_rows // step, mark, 0)
        rows[m, 0:room, :] = jnp.zeros((room, row_width), bf16)

    def head_step(h, carry):
        most = groups[first, heads + h]
        for m in range(1, count):
            most = jnp.maximum(most, groups[first + m, heads + h])

        def multiply(tile, carry):
            ats = []
            for m in range(count):
                at = jnp.where(
                    tile < groups[first + m, heads + h], groups[first + m, h] + tile * step, room
                )
                ats.append(pl.ds(pl.multiple_of(at, 16), step))
                joined[m * step : (m + 1) * step, :] = sorted_in[m, ats[m], :]
            out = lax.dot_general(
                joined[...], weight[h], (((1,), (1,)), ((), ())), preferred_element_type=f32
            ).astype(bf16)
            for m in range(count):
                rows[m, ats[m], :] = out[m * step : (m + 1) * step]
            return carry

        return lax.fori_loop(0, most, multiply, carry)

    for h in range(heads):
        copies[h].wait()
        head_step(h, 0)
    if has_table:
        copies[heads].wait()
    tile = 256
    outs = []
    for block in range(row_width // tile):
        cols = pl.ds(block * tile, tile)
        part = None
        for m in range(count):
            more = jnp.dot(
                place[:, m * room : (m + 1) * room], rows[m, 0:room, cols], preferred_element_type=f32
            )
            part = more if part is None else part + more
        if has_table:
            part = part + total[:, cols]
        total[:, cols] = part
        outs.append(
            pltpu.make_async_copy(
                total.at[:, cols], table.at[:, cols], sems.at[heads + 1 + block]
            )
        )
        outs[-1].start()
    for copy in outs:
        copy.wait()


def owner_add(first, count, table, got, place_of, row_of, groups, weight, order):
    heads, row_width, feature = weight.shape
    slots = got.shape[0]
    room = row_of.shape[1]
    vmem = pl.BlockSpec(memory_space=pltpu.VMEM)
    smem = pl.BlockSpec(memory_space=pltpu.SMEM)
    operands = [got, place_of, row_of, groups, order, weight]
    hbm = pl.BlockSpec(memory_space=pltpu.HBM)
    specs = [vmem, vmem, vmem, smem, smem, hbm]
    if table is not None:
        operands.append(table)
        specs.append(hbm)
    return pl.pallas_call(
        functools.partial(owner_kernel, first, count, table is not None),
        out_shape=jax.ShapeDtypeStruct((TABLE_DEV, row_width), f32),
        in_specs=specs,
        out_specs=hbm,
        scratch_shapes=[
            pltpu.VMEM((count, room + 128, feature), bf16),
            pltpu.VMEM((count * 128, feature), bf16),
            pltpu.VMEM((count, room + 128, row_width), bf16),
            pltpu.VMEM((TABLE_DEV, count * room), bf16),
            pltpu.VMEM(weight.shape, bf16),
            pltpu.VMEM((TABLE_DEV, row_width), f32),
            pltpu.SemaphoreType.DMA((heads + 1 + row_width // 256,)),
        ],
        compiler_params=pltpu.CompilerParams(vmem_limit_bytes=VMEM_LIMIT),
        cost_estimate=pl.CostEstimate(
            flops=6 * count * slots * row_width * TABLE_DEV,
            bytes_accessed=18 * MIB,
            transcendentals=0,
        ),
        name="owner_add",
    )(*operands)


def slots_of(row_ids, owners, capacity):
    batches, length, heads = row_ids.shape
    ids = row_ids.transpose(0, 2, 1).reshape(batches, heads * length)
    owner = ids // TABLE_DEV
    local = ids - owner * TABLE_DEV
    head = jnp.arange(heads * length, dtype=jnp.int32) // length
    order = jnp.arange(heads * length, dtype=jnp.int32)
    ahead = (owner[:, None, :] == owner[:, :, None]) & (order[None, :] < order[:, None])
    rank = jnp.sum(ahead.astype(jnp.int32), -1)
    dest = owner * capacity + rank
    code = local * heads + head
    slot = jnp.arange(owners * capacity, dtype=jnp.int32)
    hit = dest[:, None, :] == slot[:, None]
    holds = jnp.sum(jnp.where(hit, code[:, None, :] + 1, 0), -1) - 1
    return dest, holds


def groups_of(holds, heads):
    batches, slots = holds.shape
    room = -(-(slots + 15 * heads) // 128) * 128
    valid = holds >= 0
    head = jnp.where(valid, holds % heads, -1)
    member = head[..., None] == jnp.arange(heads, dtype=jnp.int32)
    order = jnp.arange(slots, dtype=jnp.int32)
    below = (order[None, :] < order[:, None]).astype(bf16)
    rank = jnp.einsum("ij,bjh->bih", below, member.astype(bf16), preferred_element_type=f32)
    counts = jnp.sum(member.astype(jnp.int32), 1)
    padded = (counts + 15) // 16 * 16
    number = jnp.arange(heads, dtype=jnp.int32)
    starts = jnp.sum(jnp.where(number[None, :] < number[:, None], padded[:, None, :], 0), -1)
    place = jnp.sum(jnp.where(member, rank.astype(jnp.int32) + starts[:, None, :] + 1, 0), -1) - 1
    spot = jnp.arange(room, dtype=jnp.int32)
    hit = place[:, None, :] == spot[:, None]
    row = jnp.sum(jnp.where(hit, (holds // heads)[:, None, :] + 1, 0), -1) - 1
    groups = jnp.concatenate([starts, (counts + 127) // 128], 1)
    return place, row, groups


def shards(
    saved_inputs, memory, value_weight, conv_weight, norm_gain, layer_counts, row_ids, out_grad
):
    section = lax.axis_index("section")
    sections = lax.axis_size("section")
    owners = lax.axis_size("table")
    batches, length, width = out_grad.shape
    heads = memory.shape[3]
    capacity = 3 * length * heads // (2 * owners)
    slots = owners * capacity
    weight = value_weight[0]
    live = layer_counts[0]
    x = saved_inputs[0]
    is_top = section == sections - 1

    to_next = [(i, i + 1) for i in range(owners - 1)]
    to_last = [(i + 1, i) for i in range(owners - 1)]
    down = [(i + 1, i) for i in range(sections - 1)]
    down_halo = [
        ((i + 1) * owners + t + 1, i * owners + t)
        for i in range(sections - 1)
        for t in range(owners - 1)
    ]
    v, (next_one, last_one, next_rest, last_rest), taps = all_values(
        memory[0], weight, conv_weight[0], norm_gain[0], x, out_grad
    )
    before = lax.ppermute(next_one, "table", to_next)
    behind = behind_one = lax.ppermute(last_one, "table", to_last)

    saved = []
    outputs = table = dest = holds = place_of = row_of = groups = got = packed = None
    ready = []
    order = jnp.zeros((1,), jnp.int32)
    near = near_halo = order
    ticks = batches + sections - 1
    for tick in range(ticks):
        if tick < batches:
            carry = (next_rest, last_rest) if tick == 0 else ()
            state = forward_map(
                tick, max(tick - 1, 0), live.reshape(1), x, v, before, behind, taps, order, carry
            )
            saved.append(state[:3])
            if tick == 0:
                before = lax.ppermute(state[3], "table", to_next)
                behind = lax.ppermute(state[4], "table", to_last)
        position = tick - (sections - 1 - section)
        which = jnp.clip(position, 0, batches - 1)
        active = (position >= 0) & (position < batches)
        info = jnp.stack([which, active, is_top, live]).astype(jnp.int32)
        first = max(0, tick - (sections - 1))
        packing = (batches - 1, dest[batches - 1][None, :], slots) if tick == ticks - 1 else None
        grad_send, halo_send, *outputs = backward_map(
            info, near, near_halo, out_grad, behind_one, behind if tick else behind_one, x, v, taps,
            first, saved[first : tick + 1], outputs, packing, ready,
        )
        if packing is not None:
            last_packed = outputs.pop()
        order = outputs.pop()
        if tick < ticks - 1:
            near = lax.ppermute(grad_send, "section", down)
            near_halo = lax.ppermute(halo_send, ("section", "table"), down_halo)
        if tick == 0:
            dest, holds = slots_of(row_ids[0] + order, owners, capacity)
            holds = holds.reshape(batches, owners, capacity).transpose(1, 0, 2)
            holds = holds.reshape(owners, batches * capacity)
        ready = []
        if tick == sections - 1:
            holds = lax.all_to_all(holds + order, "table", 0, 0, tiled=True)
            holds = holds.reshape(owners, batches, capacity).transpose(1, 0, 2)
            holds = holds.reshape(batches, slots)
            ready = [holds]
        if tick == sections:
            place_of, row_of, groups = groups_of(holds + order, heads)
            ready = [place_of, row_of, groups]
        batch = tick - (sections - 1)
        if 0 <= batch < batches - 1:
            packed = pack_values(
                batch, dest[batch][None, :], outputs[1], slots, order, packed, batch, batches - 1
            )
            if batch == batches - 2:
                got = lax.all_to_all(packed, "table", 0, 0, tiled=True)
    last = batches - 1
    rest = lax.all_to_all(last_packed, "table", 0, 0, tiled=True)
    table = owner_add(0, last, None, got, place_of, row_of, groups, weight, order)
    table = owner_add(last, 1, table, rest, place_of, row_of, groups, weight, order)
    return (outputs[0][None], table[None])


def solution(mesh):
    placed = (
        P("section", None, "table", None),
        P("section", None, "table", None, None),
        P("section", None, None, None),
        P("section", None, None, None),
        P("section", None, None),
        P("section"),
        P("section", None, "table", None),
        P(None, "table", None),
    )
    return jax.shard_map(
        shards,
        mesh=mesh,
        in_specs=placed,
        out_specs=(P("section", None, "table", None), P("section", "table", None)),
        check_vma=False,
    )
```

```python
import functools
import math

import jax
import jax.numpy as jnp
from jax import lax
from jax.experimental import pallas as pl
from jax.experimental.pallas import tpu as pltpu
from jax.sharding import PartitionSpec as P

TABLE_DEV = 1024
HALO = 16
EPS = 1e-06
LANES = 128
STEP = 512
SPLIT = 4
MIB = 1 << 20
VMEM_LIMIT = 51 * MIB
STAGED_LIMIT = 39 * MIB

f32 = jnp.float32
bf16 = jnp.bfloat16


def row_total(partial):
    return jnp.broadcast_to(jnp.sum(partial, -1, keepdims=True), partial.shape)


def columns(chunk):
    return pl.ds(pl.multiple_of(chunk * STEP, STEP), STEP)


def wide(narrow):
    return jnp.concatenate([narrow] * (STEP // LANES), 1)


def fold(chunk):
    return sum(chunk[:, i : i + LANES] for i in range(0, STEP, LANES))


def values_kernel(
    memory, weight, convs, gains, x, top, v_out, next_one, last_one, next_rest, last_rest, taps,
    held, wide_held, flat, v, for_next, for_last, sems,
):
    batches, rows = held.shape[:2]
    heads, _, feature = weight.shape
    length = rows // heads
    loads = [pltpu.make_async_copy(memory.at[b], held.at[b], sems.at[0, b]) for b in range(batches)]
    copies = [pltpu.make_async_copy(weight.at[h], flat.at[h], sems.at[1, h]) for h in range(heads)]
    low, high = pl.ds(0, HALO), pl.ds(length - HALO, HALO)
    edges = (
        pltpu.make_async_copy(x.at[:, high], for_next.at[:, pl.ds(0, HALO)], sems.at[3, 0]),
        pltpu.make_async_copy(x.at[:, low], for_last.at[:, pl.ds(0, HALO)], sems.at[3, 1]),
        pltpu.make_async_copy(top.at[:, low], for_last.at[:, pl.ds(HALO, HALO)], sems.at[3, 2]),
    )
    for copy in (*loads, *copies, *edges):
        copy.start()
    for layer in range(taps.shape[0]):
        taps[layer] = 0.5 * convs[layer] * gains[layer : layer + 1, :]
    step = 64
    for b in range(batches):
        loads[b].wait()

        def widen(tile, carry):
            at = pl.multiple_of(tile * step, step)
            block = held[b, pl.ds(at, step), :].astype(f32)
            for c in range(block.shape[1] // LANES):
                wide_held[c, pl.ds(b * rows + at, step), :] = block[:, c * LANES : (c + 1) * LANES]
            return carry

        lax.fori_loop(0, rows // step, widen, 0)
    outs = []
    for h in range(heads):
        copies[h].wait()
        taken = [
            wide_held[c, pl.ds(h, batches * length, stride=heads), :].astype(bf16)
            for c in range(wide_held.shape[0])
        ]
        cols = pl.ds(h * feature, feature)
        v[:, cols] = jnp.dot(
            jnp.concatenate(taken, 1), flat[h], preferred_element_type=f32
        )
        outs.append(pltpu.make_async_copy(v.at[:, cols], v_out.at[:, cols], sems.at[2, h]))
        outs[-1].start()
        for b in range(batches):
            for target, at, first in (
                (for_next, (b + 1) * length - HALO, HALO), (for_last, b * length, 2 * HALO)
            ):
                edge = v[at : at + HALO, cols]
                main = edge.astype(bf16)
                target[b, first : first + HALO, cols] = main
                target[b, first + HALO : first + 2 * HALO, cols] = (edge - main.astype(f32)).astype(bf16)
    for copy in edges:
        copy.wait()
    for i, (source, one, rest) in enumerate(
        ((for_next, next_one, next_rest), (for_last, last_one, last_rest))
    ):
        outs.append(pltpu.make_async_copy(source.at[pl.ds(0, 1)], one, sems.at[4, i]))
        outs.append(
            pltpu.make_async_copy(source.at[pl.ds(1, batches - 1)], rest, sems.at[4, 2 + i])
        )
        outs[-1].start()
        outs[-2].start()
    for copy in outs:
        copy.wait()


def all_values(memory, weight, convs, gains, x, top):
    batches, length, heads, row_width = memory.shape
    feature = weight.shape[2]
    width = heads * feature
    hbm = pl.BlockSpec(memory_space=pltpu.HBM)
    vmem = pl.BlockSpec(memory_space=pltpu.VMEM)
    v, *halos, taps = pl.pallas_call(
        values_kernel,
        out_shape=(
            jax.ShapeDtypeStruct((batches * length, width), f32),
            jax.ShapeDtypeStruct((1, 3 * HALO, width), bf16),
            jax.ShapeDtypeStruct((1, 4 * HALO, width), bf16),
            jax.ShapeDtypeStruct((batches - 1, 3 * HALO, width), bf16),
            jax.ShapeDtypeStruct((batches - 1, 4 * HALO, width), bf16),
            jax.ShapeDtypeStruct(convs.shape, f32),
        ),
        in_specs=[hbm] * 2 + [vmem] * 2 + [hbm] * 2,
        out_specs=[hbm] * 5 + [vmem],
        scratch_shapes=[
            pltpu.VMEM((batches, length * heads, row_width), bf16),
            pltpu.VMEM((row_width // LANES, batches * length * heads, LANES), f32),
            pltpu.VMEM(weight.shape, bf16),
            pltpu.VMEM((batches * length, width), f32),
            pltpu.VMEM((batches, 3 * HALO, width), bf16),
            pltpu.VMEM((batches, 4 * HALO, width), bf16),
            pltpu.SemaphoreType.DMA((5, heads)),
        ],
        compiler_params=pltpu.CompilerParams(vmem_limit_bytes=VMEM_LIMIT),
        cost_estimate=pl.CostEstimate(
            flops=2 * batches * length * heads * row_width * feature,
            bytes_accessed=18 * MIB,
            transcendentals=0,
        ),
        name="all_values",
    )(memory.reshape(batches, length * heads, row_width), weight, convs, gains, x, top)
    return v.reshape(batches, length, width), halos, taps


def forward_kernel(
    batch, halo, carried, live_ref, x, v, before, behind, taps, order, *refs,
):
    hid_out, der_out, scal_out = refs[carried : carried + 3]
    x_win, v_win, terms, hid, der, scal, rms_now, sems = refs[2 * carried + 3 :]
    length, width = x.shape[1:]
    rows = x_win.shape[0]
    keep = rows - HALO
    chunks = width // STEP
    live = live_ref[0]
    end = HALO + length
    parts = (
        (x.at[batch], 0, length, x_win, HALO),
        (v.at[batch], 0, length, v_win, HALO),
        (before.at[halo], 0, HALO, x_win, 0),
        (before.at[halo], HALO, 2 * HALO, terms, 0),
        (behind.at[halo], 0, HALO, x_win, end),
        (behind.at[halo], 2 * HALO, 2 * HALO, terms, 2 * HALO),
    )
    loads = []
    for q in range(SPLIT):
        cols = pl.ds(q * (width // SPLIT), width // SPLIT)
        loads.append([])
        for i, (source, first, size, window, at) in enumerate(parts):
            loads[q].append(
                pltpu.make_async_copy(
                    source.at[pl.ds(first, size), cols],
                    window.at[pl.ds(at, size), cols],
                    sems.at[2 + i, q],
                )
            )
            loads[q][-1].start()

    def load(chunk, sums):
        cols = columns(chunk)
        for at, first in ((0, 0), (end, 2 * HALO)):
            v_win[at : at + HALO, cols] = terms[first : first + HALO, cols].astype(f32) + terms[
                first + HALO : first + 2 * HALO, cols
            ].astype(f32)
        x = x_win[:, cols].astype(f32)
        v = v_win[:, cols]
        return sums[0] + fold(x * x), sums[1] + fold(v * v), sums[2] + fold(x * v)

    zero = jnp.zeros((rows, LANES), f32)
    sums = (zero, zero, zero)
    for q in range(SPLIT):
        for copy in loads[q]:
            copy.wait()
        sums = lax.fori_loop(q * chunks // SPLIT, (q + 1) * chunks // SPLIT, load, sums)
    xx, vv, xv = sums
    xv = row_total(xv)
    rx = lax.rsqrt(row_total(xx) / width + EPS)
    rv = lax.rsqrt(row_total(vv) / width + EPS)
    gate = jax.nn.sigmoid(rx * rv * xv / math.sqrt(width))
    scal[4] = rx[HALO:]
    scal[5] = rv[HALO:]
    scal[6] = xv[HALO:]
    scal[7] = gate[HALO:]
    rms_now[...] = gate

    def mix(chunk, total):
        cols = columns(chunk)
        hidden = x_win[:, cols].astype(f32) + wide(rms_now[...]) * v_win[:, cols]
        hid[0, :, cols] = hidden
        return total + fold(hidden * hidden)

    total = lax.fori_loop(0, chunks, mix, zero)

    def hidden_copy(layer):
        return pltpu.make_async_copy(
            hid.at[layer, pl.ds(HALO, keep)], hid_out.at[layer], sems.at[0, layer]
        )

    def slope_copy(layer):
        return pltpu.make_async_copy(der.at[layer], der_out.at[layer], sems.at[1, layer])

    def layer_step(layer, total):
        hidden_copy(layer).start()
        rms = lax.rsqrt(row_total(total) / width + EPS)
        scal[layer] = rms[HALO:]
        rms_now[...] = rms

        def one(chunk, total):
            cols = columns(chunk)
            hidden = hid[layer, :, cols]
            unit = hidden * wide(rms_now[...])
            mixed = taps[layer, 0:1, cols] * unit
            for k in range(1, 4):
                mixed = mixed + taps[layer, k : k + 1, cols] * pltpu.roll(unit, k, 0)
            bend = jnp.tanh(mixed)
            rise = 1.0 + bend
            silu = mixed * rise
            der[layer, :, cols] = (rise + silu * (1.0 - bend))[HALO:]
            after = hidden + silu
            hid[layer + 1, :, cols] = after
            return total + fold(after * after)

        total = lax.fori_loop(0, chunks, one, zero)
        slope_copy(layer).start()
        return total

    lax.fori_loop(0, live, layer_step, total)
    out = pltpu.make_async_copy(scal, scal_out, sems.at[0, 4])
    out.start()

    def finish(layer, carry):
        hidden_copy(layer).wait()
        slope_copy(layer).wait()
        return carry

    lax.fori_loop(0, live, finish, 0)
    out.wait()


def forward_map(batch, halo, live, x, v, before, behind, taps, order, carry):
    length, width = x.shape[1:]
    keep = length + HALO
    rows = keep + HALO
    layers = taps.shape[0]
    hbm = pl.BlockSpec(memory_space=pltpu.HBM)
    return pl.pallas_call(
        functools.partial(forward_kernel, batch, halo, len(carry)),
        out_shape=(
            jax.ShapeDtypeStruct((layers, keep, width), f32),
            jax.ShapeDtypeStruct((layers, keep, width), f32),
            jax.ShapeDtypeStruct((8, keep, LANES), f32),
            *(jax.ShapeDtypeStruct(array.shape, array.dtype) for array in carry),
        ),
        in_specs=[pl.BlockSpec(memory_space=pltpu.SMEM)]
        + [hbm] * 4
        + [pl.BlockSpec(memory_space=pltpu.VMEM), pl.BlockSpec(memory_space=pltpu.SMEM)]
        + [hbm] * len(carry),
        out_specs=[hbm] * (3 + len(carry)),
        input_output_aliases={7 + i: 3 + i for i in range(len(carry))},
        scratch_shapes=[
            pltpu.VMEM((rows, width), bf16),
            pltpu.VMEM((rows, width), f32),
            pltpu.VMEM((4 * HALO, width), bf16),
            pltpu.VMEM((layers + 1, rows, width), f32),
            pltpu.VMEM((layers, keep, width), f32),
            pltpu.VMEM((8, keep, LANES), f32),
            pltpu.VMEM((rows, LANES), f32),
            pltpu.SemaphoreType.DMA((8, layers + 1)),
        ],
        compiler_params=pltpu.CompilerParams(vmem_limit_bytes=VMEM_LIMIT),
        cost_estimate=pl.CostEstimate(
            flops=30 * layers * rows * width,
            bytes_accessed=16 * MIB,
            transcendentals=layers * rows * width,
        ),
        name="forward_map",
    )(live, x, v, before, behind, taps, order, *carry)


def backward_kernel(
    held, info, near, near_halo, top, behind_one, behind_rest, taps, *refs,
):
    if held[6]:
        hid, der, scal, x_in, v_in = refs[:5]
        refs = refs[5:]
    else:
        x_all, v_all = refs[:2]
        saved = [refs[3 * i + 2 : 3 * i + 5] for i in range(held[1])]
        refs = refs[3 * held[1] + 2 :]
    if held[2]:
        gv_held, refs = refs[1], refs[2:]
    if held[5]:
        refs = refs[1:6] + refs[7:]
    if held[3]:
        dest, refs = refs[0], refs[2:]
        packed, stacked, slots_now = refs[5], refs[-2], refs[-1]
        refs = refs[:5] + refs[6:-2]
    if not held[6]:
        hid, der, scal, x_in, v_in = refs[5:10]
        refs = refs[:5] + refs[10:]
    grad_send, halo_send, grads_all, gv_all, order_out, g, u, coef, g_in, ga_in, gx, gv, sems = refs
    which = info[0]
    active = info[1]
    is_top = info[2]
    live = info[3]
    length, width = grad_send.shape
    rows = g.shape[0]
    chunks = width // STEP
    quarter = width // SPLIT
    first, count = held[0], held[1]
    order_out[0] = 0

    def part(q):
        return pl.ds(pl.multiple_of(q * quarter, quarter), quarter)

    def scal_copy(i):
        return pltpu.make_async_copy(saved[i][2], scal, sems.at[2, 0])

    def layer_copies(i, layer, q):
        cols = part(q)
        return (
            pltpu.make_async_copy(
                saved[i][1].at[layer, :, cols], der.at[layer, :, cols], sems.at[1, 4 * layer + q]
            ),
            pltpu.make_async_copy(
                saved[i][0].at[layer, :, cols], hid.at[layer, :, cols], sems.at[0, 4 * layer + q]
            ),
        )

    def input_copies():
        return (
            pltpu.make_async_copy(x_all.at[which], x_in, sems.at[2, 1]),
            pltpu.make_async_copy(v_all.at[which], v_in, sems.at[2, 3]),
        )

    def grad_copies(source, source_halo):
        return (
            pltpu.make_async_copy(source, g_in, sems.at[3, 0]),
            pltpu.make_async_copy(source_halo, ga_in, sems.at[3, 1]),
        )

    def pack():
        spread_heads(gv, stacked)
        into_slots(dest, stacked, slots_now)
        at = pl.ds(packed.shape[1] - slots_now.shape[1], slots_now.shape[1])
        copy = pltpu.make_async_copy(slots_now, packed.at[:, at], sems.at[3, 3])
        copy.start()
        copy.wait()

    @pl.when(active == 1)
    def _():
        @pl.when(is_top == 1)
        def _():
            for i, source in ((0, behind_one.at[0]), (1, behind_rest.at[jnp.maximum(which - 1, 0)])):
                @pl.when(jnp.minimum(which, 1) == i)
                def _():
                    for copy in grad_copies(top.at[which], source.at[pl.ds(HALO, HALO)]):
                        copy.start()

        if held[4]:
            @pl.when(is_top == 0)
            def _():
                for copy in grad_copies(near, near_halo):
                    copy.start()

        if not held[6]:
            for i in range(count):
                @pl.when(which == first + i)
                def _():
                    def begin(step, carry):
                        layer = live - 1 - step
                        for q in range(SPLIT):
                            for copy in layer_copies(i, layer, q):
                                copy.start()
                        return carry

                    begin(0, 0)
                    scal_copy(i).start()
                    lax.fori_loop(1, live, begin, 0)

            for copy in input_copies():
                copy.start()

        for copy in grad_copies(top.at[which], behind_one.at[0, pl.ds(HALO, HALO)]):
            copy.wait()

        def into_taps(layer, cols, grad):
            size = grad.shape[0]
            slope = grad * der[layer, 0:size, cols]
            out = taps[layer, 0:1, cols] * slope
            for k in range(1, 4):
                out = out + taps[layer, k : k + 1, cols] * pltpu.roll(slope, size - k, 0)
            u[0:size, cols] = out
            return fold(out * hid[layer, 0:size, cols])

        last = live - 1
        total = jnp.zeros((rows, LANES), f32)
        for q in range(SPLIT):
            if not held[6]:
                for copy in layer_copies(0, last, q):
                    copy.wait()

            def start(chunk, total):
                cols = columns(chunk)
                g[0:length, cols] = g_in[:, cols].astype(f32)
                g[length:rows, cols] = ga_in[:, cols].astype(f32)
                return total + into_taps(last, cols, g[:, cols])

            total = lax.fori_loop(q * chunks // SPLIT, (q + 1) * chunks // SPLIT, start, total)
        if not held[6]:
            scal_copy(0).wait()

        def coefficients(layer, total):
            size = total.shape[0]
            rms = scal[layer, 0:size]
            coef[0, 0:size] = rms
            coef[1, 0:size] = -rms * rms * rms * (row_total(total) / width)

        def through_rms(layer, cols, size):
            return g[0:size, cols] + (
                wide(coef[0, 0:size]) * u[0:size, cols]
                + wide(coef[1, 0:size]) * hid[layer, 0:size, cols]
            )

        def layer_step(size, step, total):
            layer = live - 1 - step
            coefficients(layer, total)
            if not held[6]:
                for q in range(SPLIT):
                    for copy in layer_copies(0, layer - 1, q):
                        copy.wait()

            def one(chunk, total):
                cols = columns(chunk)
                grad = through_rms(layer, cols, size)
                g[0:size, cols] = grad
                return total + into_taps(layer - 1, cols, grad)

            return lax.fori_loop(0, chunks, one, jnp.zeros((size, LANES), f32))

        total = lax.fori_loop(
            0, jnp.minimum(live - 1, 1), functools.partial(layer_step, rows), total
        )
        fewer = rows - HALO // 2
        total = lax.fori_loop(
            1, live - 1, functools.partial(layer_step, fewer), total[0:fewer]
        )
        coefficients(0, total[0:length])
        if not held[6]:
            for copy in input_copies():
                copy.wait()

        def to_gate(chunk, total):
            cols = columns(chunk)
            grad = through_rms(0, cols, length)
            g[0:length, cols] = grad
            return total + fold(grad * v_in[:, cols])

        total = row_total(lax.fori_loop(0, chunks, to_gate, jnp.zeros((length, LANES), f32)))
        rx, rv, xv, gate = (scal[i, 0:length] for i in range(4, 8))
        both = total * gate * (1.0 - gate) * (1.0 / math.sqrt(width)) * rx * rv
        mean = xv / width
        coef[0, 0:length] = both
        coef[1, 0:length] = -both * rx * rx * mean
        coef[2, 0:length] = -both * rv * rv * mean
        coef[3, 0:length] = gate

        def finish(chunk, carry):
            cols = columns(chunk)
            grad = g[0:length, cols]
            x = x_in[:, cols].astype(f32)
            v = v_in[:, cols]
            cross = wide(coef[0, 0:length])
            grad_x = grad + cross * v + wide(coef[1, 0:length]) * x
            grad_v = wide(coef[3, 0:length]) * grad + cross * x + wide(coef[2, 0:length]) * v
            gx[:, cols] = grad_x.astype(bf16)
            gv[:, cols] = grad_v.astype(bf16)
            return carry

        outs = []
        for q in range(SPLIT):
            lax.fori_loop(q * chunks // SPLIT, (q + 1) * chunks // SPLIT, finish, 0)
            cols = part(q)
            for i, (source, target) in enumerate((
                (gx.at[:, cols], grad_send.at[:, cols]),
                (gx.at[pl.ds(0, HALO), cols], halo_send.at[:, cols]),
                (gx.at[:, cols], grads_all.at[which, :, cols]),
                (gv.at[:, cols], gv_all.at[which, :, cols]),
            )):
                outs.append(pltpu.make_async_copy(source, target, sems.at[4, 4 * i + q]))
                outs[-1].start()
        if held[3]:
            pack()
        for copy in outs:
            copy.wait()

    if held[3]:
        @pl.when(active == 0)
        def _():
            copy = pltpu.make_async_copy(gv_held.at[held[3] - 1], gv, sems.at[3, 2])
            copy.start()
            copy.wait()
            pack()


def backward_map(info, near, near_halo, top, behind_one, behind_rest, x, v, taps, first, saved, previous, packing, carry, staged):
    batches, length, width = x.shape
    rows = length + HALO
    layers = taps.shape[0]
    flat = [array for group in saved for array in group]
    some = pl.BlockSpec(memory_space=pl.ANY)
    hbm = pl.BlockSpec(memory_space=pltpu.HBM)
    vmem = pl.BlockSpec(memory_space=pltpu.VMEM)
    smem = pl.BlockSpec(memory_space=pltpu.SMEM)
    operands = [info, near, near_halo, top, behind_one, behind_rest, taps]
    specs = [smem] + [some] * 2 + [hbm] * 3 + [vmem]
    if staged is None:
        operands += [x, v, *flat]
        specs += [hbm] * (2 + len(flat))
    else:
        operands += staged
        specs += [vmem] * len(staged)
    shapes = [
        jax.ShapeDtypeStruct((length, width), bf16),
        jax.ShapeDtypeStruct((HALO, width), bf16),
        jax.ShapeDtypeStruct((batches, length, width), bf16),
        jax.ShapeDtypeStruct((batches, length, width), bf16),
        jax.ShapeDtypeStruct((1,), jnp.int32),
    ]
    out_specs = [some] * 2 + [hbm] * 2 + [smem]
    scratch = []
    if staged is None:
        scratch = [
            pltpu.VMEM((layers, rows, width), f32),
            pltpu.VMEM((layers, rows, width), f32),
            pltpu.VMEM((8, rows, LANES), f32),
            pltpu.VMEM((length, width), bf16),
            pltpu.VMEM((length, width), f32),
        ]
    scratch += [
        pltpu.VMEM((rows, width), f32),
        pltpu.VMEM((rows, width), f32),
        pltpu.VMEM((4, rows, LANES), f32),
        pltpu.VMEM((length, width), bf16),
        pltpu.VMEM((HALO, width), bf16),
        pltpu.VMEM((length, width), bf16),
        pltpu.VMEM((length, width), bf16),
        pltpu.SemaphoreType.DMA((5, 16)),
    ]
    aliases = {}
    if previous is not None:
        aliases = {len(operands): 2, len(operands) + 1: 3}
        operands += previous
        specs += [hbm] * 2
    if carry is not None:
        aliases[len(operands)] = 5
        operands.append(carry)
        specs.append(hbm)
        shapes.append(jax.ShapeDtypeStruct(carry.shape, carry.dtype))
        out_specs.append(hbm)
    if packing is not None:
        batch, dest, packed = packing
        aliases[len(operands) + 1] = 5
        operands += [dest, packed]
        specs += [vmem, hbm]
        feature = width // 8
        shapes.append(jax.ShapeDtypeStruct(packed.shape, bf16))
        out_specs.append(hbm)
        scratch += [pltpu.VMEM((8 * length, feature), bf16), pltpu.VMEM((packed.shape[0], feature), bf16)]
    pack_flag = 0 if packing is None else packing[0] + 1
    return pl.pallas_call(
        functools.partial(
            backward_kernel,
            (first, len(saved), previous is not None, pack_flag, near.ndim == 2, carry is not None, staged is not None),
        ),
        out_shape=shapes,
        in_specs=specs,
        out_specs=out_specs,
        scratch_shapes=scratch,
        input_output_aliases=aliases,
        compiler_params=pltpu.CompilerParams(vmem_limit_bytes=VMEM_LIMIT if staged is None else STAGED_LIMIT),
        cost_estimate=pl.CostEstimate(
            flops=25 * layers * rows * width, bytes_accessed=100 * MIB, transcendentals=0
        ),
        name="backward_map",
    )(*operands)


def spread_heads(gv, stacked):
    length, width = gv.shape[0], stacked.shape[1]
    for head in range(stacked.shape[0] // length):
        stacked[head * length : (head + 1) * length, :] = gv[:, head * width : (head + 1) * width]


def into_slots(dest, stacked, out):
    slot = lax.broadcasted_iota(jnp.int32, (out.shape[0], stacked.shape[0]), 0)
    place = jnp.where(slot == dest[...], 1.0, 0.0).astype(bf16)
    out[...] = jnp.dot(place, stacked[...], preferred_element_type=f32).astype(bf16)


def pack_kernel(dest, gv_all, order, *refs):
    out, stacked = refs[-2:]
    spread_heads(gv_all.at[0], stacked)
    into_slots(dest, stacked, out)


def pack_values(batch, dest, gv_all, slots, order, into, at, total):
    batches, length, model = gv_all.shape
    feature = model // 8
    operands = [dest, gv_all, order] + ([] if into is None else [into])
    specs = [
        pl.BlockSpec(dest.shape, lambda i: (0, 0)),
        pl.BlockSpec((1, length, model), lambda i: (batch, 0, 0)),
        pl.BlockSpec(memory_space=pltpu.SMEM),
    ] + ([] if into is None else [pl.BlockSpec(memory_space=pltpu.HBM)])
    return pl.pallas_call(
        pack_kernel,
        out_shape=jax.ShapeDtypeStruct((slots, total * feature), bf16),
        grid=(1,),
        in_specs=specs,
        out_specs=pl.BlockSpec((slots, feature), lambda i: (0, at)),
        scratch_shapes=[pltpu.VMEM((8 * length, feature), bf16)],
        input_output_aliases={} if into is None else {3: 0},
        compiler_params=pltpu.CompilerParams(vmem_limit_bytes=VMEM_LIMIT),
        cost_estimate=pl.CostEstimate(
            flops=MIB, bytes_accessed=MIB // 16, transcendentals=0
        ),
        name="pack_values",
    )(*operands)


def owner_kernel(first, count, has_table, got, place_of, row_of, groups, order, weight_in, *refs):
    if has_table:
        table_in, refs = refs[0], refs[1:]
    table, sorted_in, joined, rows, place, weight, total, sems = refs
    heads, row_width, feature = weight.shape
    table_rows = table.shape[0]
    copies = [
        pltpu.make_async_copy(weight_in.at[h], weight.at[h], sems.at[h]) for h in range(heads)
    ]
    if has_table:
        copies.append(pltpu.make_async_copy(table_in, total, sems.at[heads]))
    for copy in copies:
        copy.start()
    slots = got.shape[0]
    room = rows.shape[1] - 128
    step = 128
    half = room // 2
    for m in range(count):
        b = first + m

        def sort(tile, carry):
            at = pl.multiple_of(tile * half, half)
            slot = lax.broadcasted_iota(jnp.int32, (half, slots), 0) + at
            pick = jnp.where(slot == place_of[b : b + 1, :], 1.0, 0.0).astype(bf16)
            sorted_in[m, pl.ds(at, half), :] = jnp.dot(
                pick, got[:, m * feature : (m + 1) * feature], preferred_element_type=f32
            ).astype(bf16)
            return carry

        lax.fori_loop(0, 2, sort, 0)

        def mark(tile, carry):
            at = pl.multiple_of(tile * step, step)
            row = lax.broadcasted_iota(jnp.int32, (step, room), 0) + at
            place[pl.ds(at, step), m * room : (m + 1) * room] = jnp.where(
                row == row_of[b : b + 1, :], 1.0, 0.0
            ).astype(bf16)
            return carry

        lax.fori_loop(0, table_rows // step, mark, 0)
        rows[m, 0:room, :] = jnp.zeros((room, row_width), bf16)

    def head_step(h, carry):
        most = groups[first, heads + h]
        for m in range(1, count):
            most = jnp.maximum(most, groups[first + m, heads + h])

        def multiply(tile, carry):
            ats = []
            for m in range(count):
                at = jnp.where(
                    tile < groups[first + m, heads + h], groups[first + m, h] + tile * step, room
                )
                ats.append(pl.ds(pl.multiple_of(at, 16), step))
                joined[m * step : (m + 1) * step, :] = sorted_in[m, ats[m], :]
            out = lax.dot_general(
                joined[...], weight[h], (((1,), (1,)), ((), ())), preferred_element_type=f32
            ).astype(bf16)
            for m in range(count):
                rows[m, ats[m], :] = out[m * step : (m + 1) * step]
            return carry

        return lax.fori_loop(0, most, multiply, carry)

    for h in range(heads):
        copies[h].wait()
        head_step(h, 0)
    if has_table:
        copies[heads].wait()
    tile = 256
    outs = []
    for block in range(row_width // tile):
        cols = pl.ds(block * tile, tile)
        part = None
        for m in range(count):
            more = jnp.dot(
                place[:, m * room : (m + 1) * room], rows[m, 0:room, cols], preferred_element_type=f32
            )
            part = more if part is None else part + more
        if has_table:
            part = part + total[:, cols]
        total[:, cols] = part
        outs.append(
            pltpu.make_async_copy(
                total.at[:, cols], table.at[:, cols], sems.at[heads + 1 + block]
            )
        )
        outs[-1].start()
    for copy in outs:
        copy.wait()


def owner_add(first, count, table, got, place_of, row_of, groups, weight, order):
    heads, row_width, feature = weight.shape
    slots = got.shape[0]
    room = row_of.shape[1]
    vmem = pl.BlockSpec(memory_space=pltpu.VMEM)
    smem = pl.BlockSpec(memory_space=pltpu.SMEM)
    operands = [got, place_of, row_of, groups, order, weight]
    hbm = pl.BlockSpec(memory_space=pltpu.HBM)
    specs = [vmem, vmem, vmem, smem, smem, hbm]
    if table is not None:
        operands.append(table)
        specs.append(hbm)
    return pl.pallas_call(
        functools.partial(owner_kernel, first, count, table is not None),
        out_shape=jax.ShapeDtypeStruct((TABLE_DEV, row_width), f32),
        in_specs=specs,
        out_specs=hbm,
        scratch_shapes=[
            pltpu.VMEM((count, room + 128, feature), bf16),
            pltpu.VMEM((count * 128, feature), bf16),
            pltpu.VMEM((count, room + 128, row_width), bf16),
            pltpu.VMEM((TABLE_DEV, count * room), bf16),
            pltpu.VMEM(weight.shape, bf16),
            pltpu.VMEM((TABLE_DEV, row_width), f32),
            pltpu.SemaphoreType.DMA((heads + 1 + row_width // 256,)),
        ],
        compiler_params=pltpu.CompilerParams(vmem_limit_bytes=VMEM_LIMIT),
        cost_estimate=pl.CostEstimate(
            flops=6 * count * slots * row_width * TABLE_DEV,
            bytes_accessed=18 * MIB,
            transcendentals=0,
        ),
        name="owner_add",
    )(*operands)


def slots_of(row_ids, owners, capacity):
    batches, length, heads = row_ids.shape
    ids = row_ids.transpose(0, 2, 1).reshape(batches, heads * length)
    owner = ids // TABLE_DEV
    local = ids - owner * TABLE_DEV
    head = jnp.arange(heads * length, dtype=jnp.int32) // length
    order = jnp.arange(heads * length, dtype=jnp.int32)
    ahead = (owner[:, None, :] == owner[:, :, None]) & (order[None, :] < order[:, None])
    rank = jnp.sum(ahead.astype(jnp.int32), -1)
    dest = owner * capacity + rank
    code = local * heads + head
    slot = jnp.arange(owners * capacity, dtype=jnp.int32)
    hit = dest[:, None, :] == slot[:, None]
    holds = jnp.sum(jnp.where(hit, code[:, None, :] + 1, 0), -1) - 1
    return dest, holds


def groups_of(holds, heads):
    batches, slots = holds.shape
    room = -(-(slots + 15 * heads) // 128) * 128
    valid = holds >= 0
    head = jnp.where(valid, holds % heads, -1)
    member = head[..., None] == jnp.arange(heads, dtype=jnp.int32)
    order = jnp.arange(slots, dtype=jnp.int32)
    below = (order[None, :] < order[:, None]).astype(bf16)
    rank = jnp.einsum("ij,bjh->bih", below, member.astype(bf16), preferred_element_type=f32)
    counts = jnp.sum(member.astype(jnp.int32), 1)
    padded = (counts + 15) // 16 * 16
    number = jnp.arange(heads, dtype=jnp.int32)
    starts = jnp.sum(jnp.where(number[None, :] < number[:, None], padded[:, None, :], 0), -1)
    place = jnp.sum(jnp.where(member, rank.astype(jnp.int32) + starts[:, None, :] + 1, 0), -1) - 1
    spot = jnp.arange(room, dtype=jnp.int32)
    hit = place[:, None, :] == spot[:, None]
    row = jnp.sum(jnp.where(hit, (holds // heads)[:, None, :] + 1, 0), -1) - 1
    groups = jnp.concatenate([starts, (counts + 127) // 128], 1)
    return place, row, groups


def shards(
    saved_inputs, memory, value_weight, conv_weight, norm_gain, layer_counts, row_ids, out_grad
):
    section = lax.axis_index("section")
    sections = lax.axis_size("section")
    owners = lax.axis_size("table")
    batches, length, width = out_grad.shape
    heads = memory.shape[3]
    capacity = 3 * length * heads // (2 * owners)
    slots = owners * capacity
    weight = value_weight[0]
    live = layer_counts[0]
    x = saved_inputs[0]
    is_top = section == sections - 1

    to_next = [(i, i + 1) for i in range(owners - 1)]
    to_last = [(i + 1, i) for i in range(owners - 1)]
    down = [(i + 1, i) for i in range(sections - 1)]
    down_halo = [
        ((i + 1) * owners + t + 1, i * owners + t)
        for i in range(sections - 1)
        for t in range(owners - 1)
    ]
    v, (next_one, last_one, next_rest, last_rest), taps = all_values(
        memory[0], weight, conv_weight[0], norm_gain[0], x, out_grad
    )
    before = lax.ppermute(next_one, "table", to_next)
    behind = behind_one = lax.ppermute(last_one, "table", to_last)

    saved = []
    outputs = table = dest = holds = place_of = row_of = groups = got = staged = None
    packed = [None, None]
    order = jnp.zeros((1,), jnp.int32)
    near = near_halo = order
    ticks = batches + sections - 1
    for tick in range(ticks):
        if tick < batches:
            carry = (next_rest, last_rest) if tick == 0 else ()
            state = forward_map(
                tick, max(tick - 1, 0), live.reshape(1), x, v, before, behind, taps, order, carry
            )
            saved.append(state[:3])
            if tick == 0:
                before = lax.ppermute(state[3], "table", to_next)
                behind = lax.ppermute(state[4], "table", to_last)
        first = max(0, tick - (sections - 1))
        position = tick - (sections - 1 - section)
        which = jnp.clip(position, 0, batches - 1)
        active = (position >= 0) & (position < batches)
        info = jnp.stack([which, active, is_top, live]).astype(jnp.int32)
        packing = (batches - 1, dest[batches - 1][None, :], packed[1]) if tick == ticks - 1 else None
        grad_send, halo_send, *outputs = backward_map(
            info, near, near_halo, out_grad, behind_one, behind if tick else behind_one, x, v, taps,
            first, saved[first : tick + 1], outputs, packing, packed[0] if tick == ticks - 2 else None, staged,
        )
        if tick == ticks - 2:
            packed[0] = outputs.pop()
            got = lax.all_to_all(packed[0], "table", 0, 0, tiled=True)
        if packing is not None:
            packed[1] = outputs.pop()
        order = outputs.pop()
        if tick < ticks - 1:
            near = lax.ppermute(grad_send, "section", down)
            near_halo = lax.ppermute(halo_send, ("section", "table"), down_halo)
        if tick == 0:
            dest, holds = slots_of(row_ids[0] + order, owners, capacity)
            holds = holds.reshape(batches, owners, capacity).transpose(1, 0, 2)
            holds = holds.reshape(owners, batches * capacity)
        if tick == sections:
            holds = lax.all_to_all(holds + order, "table", 0, 0, tiled=True)
            holds = holds.reshape(owners, batches, capacity).transpose(1, 0, 2)
            holds = holds.reshape(batches, slots)
        if tick == sections + 1:
            place_of, row_of, groups = groups_of(holds + order, heads)
        batch = tick - (sections - 1)
        if 0 <= batch < batches - 1:
            pair, at = batch // 2, batch % 2
            packed[pair] = pack_values(
                batch, dest[batch][None, :], outputs[1], slots, order, packed[pair], at, 2
            )
    rest = lax.all_to_all(packed[1], "table", 0, 0, tiled=True)
    table = owner_add(0, 2, None, got, place_of, row_of, groups, weight, order)
    table = owner_add(2, 2, table, rest, place_of, row_of, groups, weight, order)
    return (outputs[0][None], table[None])


def solution(mesh):
    placed = (
        P("section", None, "table", None),
        P("section", None, "table", None, None),
        P("section", None, None, None),
        P("section", None, None, None),
        P("section", None, None),
        P("section"),
        P("section", None, "table", None),
        P(None, "table", None),
    )
    return jax.shard_map(
        shards,
        mesh=mesh,
        in_specs=placed,
        out_specs=(P("section", None, "table", None), P("section", "table", None)),
        check_vma=False,
    )
```

```python
import functools
import math

import jax
import jax.numpy as jnp
from jax import lax
from jax.experimental import pallas as pl
from jax.experimental.pallas import tpu as pltpu
from jax.sharding import PartitionSpec as P

TABLE_DEV = 1024
HALO = 16
EPS = 1e-06
LANES = 128
STEP = 512
SPLIT = 4
MIB = 1 << 20
VMEM_LIMIT = 51 * MIB

f32 = jnp.float32
bf16 = jnp.bfloat16


def row_total(partial):
    return jnp.broadcast_to(jnp.sum(partial, -1, keepdims=True), partial.shape)


def columns(chunk):
    return pl.ds(pl.multiple_of(chunk * STEP, STEP), STEP)


def wide(narrow):
    return jnp.concatenate([narrow] * (STEP // LANES), 1)


def fold(chunk):
    return sum(chunk[:, i : i + LANES] for i in range(0, STEP, LANES))


def values_kernel(
    memory, weight, convs_in, gains_in, x, top, v_out, next_one, last_one, next_rest, last_rest, taps,
    held, wide_held, flat, v, for_next, for_last, convs, gains, sems,
):
    batches, rows = held.shape[:2]
    heads, _, feature = weight.shape
    length = rows // heads
    loads = [pltpu.make_async_copy(memory.at[b], held.at[b], sems.at[0, b]) for b in range(batches)]
    copies = [pltpu.make_async_copy(weight.at[h], flat.at[h], sems.at[1, h]) for h in range(heads)]
    low, high = pl.ds(0, HALO), pl.ds(length - HALO, HALO)
    edges = (
        pltpu.make_async_copy(x.at[:, high], for_next.at[:, pl.ds(0, HALO)], sems.at[3, 0]),
        pltpu.make_async_copy(x.at[:, low], for_last.at[:, pl.ds(0, HALO)], sems.at[3, 1]),
        pltpu.make_async_copy(top.at[:, low], for_last.at[:, pl.ds(HALO, HALO)], sems.at[3, 2]),
    )
    factors = (
        pltpu.make_async_copy(convs_in, convs, sems.at[3, 3]),
        pltpu.make_async_copy(gains_in, gains, sems.at[3, 4]),
    )
    for copy in (*loads, *copies, *edges, *factors):
        copy.start()
    step = 64
    for b in range(batches):
        loads[b].wait()

        def widen(tile, carry):
            at = pl.multiple_of(tile * step, step)
            block = held[b, pl.ds(at, step), :].astype(f32)
            for c in range(block.shape[1] // LANES):
                wide_held[c, pl.ds(b * rows + at, step), :] = block[:, c * LANES : (c + 1) * LANES]
            return carry

        lax.fori_loop(0, rows // step, widen, 0)
    outs = []
    for h in range(heads):
        copies[h].wait()
        taken = [
            wide_held[c, pl.ds(h, batches * length, stride=heads), :].astype(bf16)
            for c in range(wide_held.shape[0])
        ]
        cols = pl.ds(h * feature, feature)
        v[:, cols] = jnp.dot(
            jnp.concatenate(taken, 1), flat[h], preferred_element_type=f32
        )
        outs.append(pltpu.make_async_copy(v.at[:, cols], v_out.at[:, cols], sems.at[2, h]))
        outs[-1].start()
        for b in range(batches):
            for target, at, first in (
                (for_next, (b + 1) * length - HALO, HALO), (for_last, b * length, 2 * HALO)
            ):
                edge = v[at : at + HALO, cols]
                main = edge.astype(bf16)
                target[b, first : first + HALO, cols] = main
                target[b, first + HALO : first + 2 * HALO, cols] = (edge - main.astype(f32)).astype(bf16)
    for copy in (*edges, *factors):
        copy.wait()
    for i, (source, one, rest) in enumerate(
        ((for_next, next_one, next_rest), (for_last, last_one, last_rest))
    ):
        outs.append(pltpu.make_async_copy(source.at[pl.ds(0, 1)], one, sems.at[4, i]))
        outs.append(
            pltpu.make_async_copy(source.at[pl.ds(1, batches - 1)], rest, sems.at[4, 2 + i])
        )
        outs[-1].start()
        outs[-2].start()
    for layer in range(taps.shape[0]):
        taps[layer] = 0.5 * convs[layer] * gains[layer : layer + 1, :]
    for copy in outs:
        copy.wait()


def all_values(memory, weight, convs, gains, x, top):
    batches, length, heads, row_width = memory.shape
    feature = weight.shape[2]
    width = heads * feature
    hbm = pl.BlockSpec(memory_space=pltpu.HBM)
    vmem = pl.BlockSpec(memory_space=pltpu.VMEM)
    v, *halos, taps = pl.pallas_call(
        values_kernel,
        out_shape=(
            jax.ShapeDtypeStruct((batches * length, width), f32),
            jax.ShapeDtypeStruct((1, 3 * HALO, width), bf16),
            jax.ShapeDtypeStruct((1, 4 * HALO, width), bf16),
            jax.ShapeDtypeStruct((batches - 1, 3 * HALO, width), bf16),
            jax.ShapeDtypeStruct((batches - 1, 4 * HALO, width), bf16),
            jax.ShapeDtypeStruct(convs.shape, f32),
        ),
        in_specs=[hbm] * 6,
        out_specs=[hbm] * 5 + [vmem],
        scratch_shapes=[
            pltpu.VMEM((batches, length * heads, row_width), bf16),
            pltpu.VMEM((row_width // LANES, batches * length * heads, LANES), f32),
            pltpu.VMEM(weight.shape, bf16),
            pltpu.VMEM((batches * length, width), f32),
            pltpu.VMEM((batches, 3 * HALO, width), bf16),
            pltpu.VMEM((batches, 4 * HALO, width), bf16),
            pltpu.VMEM(convs.shape, f32),
            pltpu.VMEM(gains.shape, f32),
            pltpu.SemaphoreType.DMA((5, heads)),
        ],
        compiler_params=pltpu.CompilerParams(vmem_limit_bytes=VMEM_LIMIT + 8 * MIB),
        cost_estimate=pl.CostEstimate(
            flops=2 * batches * length * heads * row_width * feature,
            bytes_accessed=18 * MIB,
            transcendentals=0,
        ),
        name="all_values",
    )(memory.reshape(batches, length * heads, row_width), weight, convs, gains, x, top)
    return v.reshape(batches, length, width), halos, taps


def forward_kernel(
    batch, halo, carried, live_ref, x, v, before, behind, taps, order, *refs,
):
    hid_out, der_out, scal_out = refs[carried : carried + 3]
    x_win, v_win, terms, hid, der, scal, rms_now, sems = refs[2 * carried + 3 :]
    length, width = x.shape[1:]
    rows = x_win.shape[0]
    keep = rows - HALO
    chunks = width // STEP
    live = live_ref[0]
    end = HALO + length
    parts = (
        (x.at[batch], 0, length, x_win, HALO),
        (v.at[batch], 0, length, v_win, HALO),
        (before.at[halo], 0, HALO, x_win, 0),
        (before.at[halo], HALO, 2 * HALO, terms, 0),
        (behind.at[halo], 0, HALO, x_win, end),
        (behind.at[halo], 2 * HALO, 2 * HALO, terms, 2 * HALO),
    )
    loads = []
    for q in range(SPLIT):
        cols = pl.ds(q * (width // SPLIT), width // SPLIT)
        loads.append([])
        for i, (source, first, size, window, at) in enumerate(parts):
            loads[q].append(
                pltpu.make_async_copy(
                    source.at[pl.ds(first, size), cols],
                    window.at[pl.ds(at, size), cols],
                    sems.at[2 + i, q],
                )
            )
            loads[q][-1].start()

    def load(chunk, sums):
        cols = columns(chunk)
        for at, first in ((0, 0), (end, 2 * HALO)):
            v_win[at : at + HALO, cols] = terms[first : first + HALO, cols].astype(f32) + terms[
                first + HALO : first + 2 * HALO, cols
            ].astype(f32)
        x = x_win[:, cols].astype(f32)
        v = v_win[:, cols]
        return sums[0] + fold(x * x), sums[1] + fold(v * v), sums[2] + fold(x * v)

    zero = jnp.zeros((rows, LANES), f32)
    sums = (zero, zero, zero)
    for q in range(SPLIT):
        for copy in loads[q]:
            copy.wait()
        sums = lax.fori_loop(q * chunks // SPLIT, (q + 1) * chunks // SPLIT, load, sums)
    xx, vv, xv = sums
    xv = row_total(xv)
    rx = lax.rsqrt(row_total(xx) / width + EPS)
    rv = lax.rsqrt(row_total(vv) / width + EPS)
    gate = jax.nn.sigmoid(rx * rv * xv / math.sqrt(width))
    scal[4] = rx[HALO:]
    scal[5] = rv[HALO:]
    scal[6] = xv[HALO:]
    scal[7] = gate[HALO:]
    rms_now[...] = gate

    def mix(chunk, total):
        cols = columns(chunk)
        hidden = x_win[:, cols].astype(f32) + wide(rms_now[...]) * v_win[:, cols]
        hid[0, :, cols] = hidden
        return total + fold(hidden * hidden)

    total = lax.fori_loop(0, chunks, mix, zero)

    def hidden_copy(layer):
        return pltpu.make_async_copy(
            hid.at[layer, pl.ds(HALO, keep)], hid_out.at[layer], sems.at[0, layer]
        )

    def slope_copy(layer):
        return pltpu.make_async_copy(der.at[layer], der_out.at[layer], sems.at[1, layer])

    def layer_step(layer, total):
        hidden_copy(layer).start()
        rms = lax.rsqrt(row_total(total) / width + EPS)
        scal[layer] = rms[HALO:]
        rms_now[...] = rms

        def one(chunk, total):
            cols = columns(chunk)
            hidden = hid[layer, :, cols]
            unit = hidden * wide(rms_now[...])
            mixed = taps[layer, 0:1, cols] * unit
            for k in range(1, 4):
                mixed = mixed + taps[layer, k : k + 1, cols] * pltpu.roll(unit, k, 0)
            bend = jnp.tanh(mixed)
            rise = 1.0 + bend
            silu = mixed * rise
            der[layer, :, cols] = (rise + silu * (1.0 - bend))[HALO:]
            after = hidden + silu
            hid[layer + 1, :, cols] = after
            return total + fold(after * after)

        total = lax.fori_loop(0, chunks, one, zero)
        slope_copy(layer).start()
        return total

    lax.fori_loop(0, live, layer_step, total)
    out = pltpu.make_async_copy(scal, scal_out, sems.at[0, 4])
    out.start()

    def finish(layer, carry):
        hidden_copy(layer).wait()
        slope_copy(layer).wait()
        return carry

    lax.fori_loop(0, live, finish, 0)
    out.wait()


def forward_map(batch, halo, live, x, v, before, behind, taps, order, carry):
    length, width = x.shape[1:]
    keep = length + HALO
    rows = keep + HALO
    layers = taps.shape[0]
    hbm = pl.BlockSpec(memory_space=pltpu.HBM)
    return pl.pallas_call(
        functools.partial(forward_kernel, batch, halo, len(carry)),
        out_shape=(
            jax.ShapeDtypeStruct((layers, keep, width), f32),
            jax.ShapeDtypeStruct((layers, keep, width), f32),
            jax.ShapeDtypeStruct((8, keep, LANES), f32),
            *(jax.ShapeDtypeStruct(array.shape, array.dtype) for array in carry),
        ),
        in_specs=[pl.BlockSpec(memory_space=pltpu.SMEM)]
        + [hbm] * 4
        + [pl.BlockSpec(memory_space=pltpu.VMEM), pl.BlockSpec(memory_space=pltpu.SMEM)]
        + [hbm] * len(carry),
        out_specs=[hbm] * (3 + len(carry)),
        input_output_aliases={7 + i: 3 + i for i in range(len(carry))},
        scratch_shapes=[
            pltpu.VMEM((rows, width), bf16),
            pltpu.VMEM((rows, width), f32),
            pltpu.VMEM((4 * HALO, width), bf16),
            pltpu.VMEM((layers + 1, rows, width), f32),
            pltpu.VMEM((layers, keep, width), f32),
            pltpu.VMEM((8, keep, LANES), f32),
            pltpu.VMEM((rows, LANES), f32),
            pltpu.SemaphoreType.DMA((8, layers + 1)),
        ],
        compiler_params=pltpu.CompilerParams(vmem_limit_bytes=VMEM_LIMIT),
        cost_estimate=pl.CostEstimate(
            flops=30 * layers * rows * width,
            bytes_accessed=16 * MIB,
            transcendentals=layers * rows * width,
        ),
        name="forward_map",
    )(live, x, v, before, behind, taps, order, *carry)


def backward_kernel(
    held, info, near, near_halo, top, behind_one, behind_rest, taps, *refs,
):
    if held[6]:
        hid, der, scal, x_in, v_in = refs[:5]
        refs = refs[5:]
    else:
        x_all, v_all = refs[:2]
        saved = [refs[3 * i + 2 : 3 * i + 5] for i in range(held[1])]
        refs = refs[3 * held[1] + 2 :]
    if held[2]:
        gv_held, refs = refs[1], refs[2:]
    if held[5]:
        refs = refs[1:6] + refs[7:]
    if held[3]:
        dest, refs = refs[0], refs[2:]
        packed, stacked, slots_now = refs[5], refs[-2], refs[-1]
        refs = refs[:5] + refs[6:-2]
    if not held[6]:
        hid, der, scal, x_in, v_in = refs[5:10]
        refs = refs[:5] + refs[10:]
    grad_send, halo_send, grads_all, gv_all, order_out, g, u, coef, g_in, ga_in, gx, gv, sems = refs
    which = info[0]
    active = info[1]
    is_top = info[2]
    live = info[3]
    length, width = grad_send.shape
    rows = g.shape[0]
    chunks = width // STEP
    quarter = width // SPLIT
    first, count = held[0], held[1]
    order_out[0] = 0

    def part(q):
        return pl.ds(pl.multiple_of(q * quarter, quarter), quarter)

    def scal_copy(i):
        return pltpu.make_async_copy(saved[i][2], scal, sems.at[2, 0])

    def layer_copies(i, layer, q):
        cols = part(q)
        return (
            pltpu.make_async_copy(
                saved[i][1].at[layer, :, cols], der.at[layer, :, cols], sems.at[1, 4 * layer + q]
            ),
            pltpu.make_async_copy(
                saved[i][0].at[layer, :, cols], hid.at[layer, :, cols], sems.at[0, 4 * layer + q]
            ),
        )

    def input_copies():
        return (
            pltpu.make_async_copy(x_all.at[which], x_in, sems.at[2, 1]),
            pltpu.make_async_copy(v_all.at[which], v_in, sems.at[2, 3]),
        )

    def grad_copies(source, source_halo):
        return (
            pltpu.make_async_copy(source, g_in, sems.at[3, 0]),
            pltpu.make_async_copy(source_halo, ga_in, sems.at[3, 1]),
        )

    def pack():
        spread_heads(gv, stacked)
        into_slots(dest, stacked, slots_now)
        at = pl.ds(packed.shape[1] - slots_now.shape[1], slots_now.shape[1])
        copy = pltpu.make_async_copy(slots_now, packed.at[:, at], sems.at[3, 3])
        copy.start()
        copy.wait()

    @pl.when(active == 1)
    def _():
        @pl.when(is_top == 1)
        def _():
            for i, source in ((0, behind_one.at[0]), (1, behind_rest.at[jnp.maximum(which - 1, 0)])):
                @pl.when(jnp.minimum(which, 1) == i)
                def _():
                    for copy in grad_copies(top.at[which], source.at[pl.ds(HALO, HALO)]):
                        copy.start()

        if held[4]:
            @pl.when(is_top == 0)
            def _():
                for copy in grad_copies(near, near_halo):
                    copy.start()

        if not held[6]:
            for i in range(count):
                @pl.when(which == first + i)
                def _():
                    def begin(step, carry):
                        layer = live - 1 - step
                        for q in range(SPLIT):
                            for copy in layer_copies(i, layer, q):
                                copy.start()
                        return carry

                    begin(0, 0)
                    scal_copy(i).start()
                    lax.fori_loop(1, live, begin, 0)

            for copy in input_copies():
                copy.start()

        for copy in grad_copies(top.at[which], behind_one.at[0, pl.ds(HALO, HALO)]):
            copy.wait()

        def into_taps(layer, cols, grad):
            size = grad.shape[0]
            slope = grad * der[layer, 0:size, cols]
            out = taps[layer, 0:1, cols] * slope
            for k in range(1, 4):
                out = out + taps[layer, k : k + 1, cols] * pltpu.roll(slope, size - k, 0)
            u[0:size, cols] = out
            return fold(out * hid[layer, 0:size, cols])

        last = live - 1
        total = jnp.zeros((rows, LANES), f32)
        for q in range(SPLIT):
            if not held[6]:
                for copy in layer_copies(0, last, q):
                    copy.wait()

            def start(chunk, total):
                cols = columns(chunk)
                g[0:length, cols] = g_in[:, cols].astype(f32)
                g[length:rows, cols] = ga_in[:, cols].astype(f32)
                return total + into_taps(last, cols, g[:, cols])

            total = lax.fori_loop(q * chunks // SPLIT, (q + 1) * chunks // SPLIT, start, total)
        if not held[6]:
            scal_copy(0).wait()

        def coefficients(layer, total):
            size = total.shape[0]
            rms = scal[layer, 0:size]
            coef[0, 0:size] = rms
            coef[1, 0:size] = -rms * rms * rms * (row_total(total) / width)

        def through_rms(layer, cols, size):
            return g[0:size, cols] + (
                wide(coef[0, 0:size]) * u[0:size, cols]
                + wide(coef[1, 0:size]) * hid[layer, 0:size, cols]
            )

        def layer_step(size, step, total):
            layer = live - 1 - step
            coefficients(layer, total)
            if not held[6]:
                for q in range(SPLIT):
                    for copy in layer_copies(0, layer - 1, q):
                        copy.wait()

            def one(chunk, total):
                cols = columns(chunk)
                grad = through_rms(layer, cols, size)
                g[0:size, cols] = grad
                return total + into_taps(layer - 1, cols, grad)

            return lax.fori_loop(0, chunks, one, jnp.zeros((size, LANES), f32))

        total = lax.fori_loop(
            0, jnp.minimum(live - 1, 1), functools.partial(layer_step, rows), total
        )
        fewer = rows - HALO // 2
        total = lax.fori_loop(
            1, live - 1, functools.partial(layer_step, fewer), total[0:fewer]
        )
        coefficients(0, total[0:length])
        if not held[6]:
            for copy in input_copies():
                copy.wait()

        def to_gate(chunk, total):
            cols = columns(chunk)
            grad = through_rms(0, cols, length)
            g[0:length, cols] = grad
            return total + fold(grad * v_in[:, cols])

        total = row_total(lax.fori_loop(0, chunks, to_gate, jnp.zeros((length, LANES), f32)))
        rx, rv, xv, gate = (scal[i, 0:length] for i in range(4, 8))
        both = total * gate * (1.0 - gate) * (1.0 / math.sqrt(width)) * rx * rv
        mean = xv / width
        coef[0, 0:length] = both
        coef[1, 0:length] = -both * rx * rx * mean
        coef[2, 0:length] = -both * rv * rv * mean
        coef[3, 0:length] = gate

        def finish(chunk, carry):
            cols = columns(chunk)
            grad = g[0:length, cols]
            x = x_in[:, cols].astype(f32)
            v = v_in[:, cols]
            cross = wide(coef[0, 0:length])
            grad_x = grad + cross * v + wide(coef[1, 0:length]) * x
            grad_v = wide(coef[3, 0:length]) * grad + cross * x + wide(coef[2, 0:length]) * v
            gx[:, cols] = grad_x.astype(bf16)
            gv[:, cols] = grad_v.astype(bf16)
            return carry

        outs = []
        for q in range(SPLIT):
            lax.fori_loop(q * chunks // SPLIT, (q + 1) * chunks // SPLIT, finish, 0)
            cols = part(q)
            for i, (source, target) in enumerate((
                (gx.at[:, cols], grad_send.at[:, cols]),
                (gx.at[pl.ds(0, HALO), cols], halo_send.at[:, cols]),
                (gx.at[:, cols], grads_all.at[which, :, cols]),
                (gv.at[:, cols], gv_all.at[which, :, cols]),
            )):
                outs.append(pltpu.make_async_copy(source, target, sems.at[4, 4 * i + q]))
                outs[-1].start()
        if held[3]:
            pack()
        for copy in outs:
            copy.wait()

    if held[3]:
        @pl.when(active == 0)
        def _():
            copy = pltpu.make_async_copy(gv_held.at[held[3] - 1], gv, sems.at[3, 2])
            copy.start()
            copy.wait()
            pack()


def backward_map(info, near, near_halo, top, behind_one, behind_rest, x, v, taps, first, saved, previous, packing, carry, staged):
    batches, length, width = x.shape
    rows = length + HALO
    layers = taps.shape[0]
    flat = [array for group in saved for array in group]
    some = pl.BlockSpec(memory_space=pl.ANY)
    hbm = pl.BlockSpec(memory_space=pltpu.HBM)
    vmem = pl.BlockSpec(memory_space=pltpu.VMEM)
    smem = pl.BlockSpec(memory_space=pltpu.SMEM)
    operands = [info, near, near_halo, top, behind_one, behind_rest, taps]
    specs = [smem] + [some] * 2 + [hbm] * 3 + [vmem]
    if staged is None:
        operands += [x, v, *flat]
        specs += [hbm] * (2 + len(flat))
    else:
        operands += staged
        specs += [vmem] * len(staged)
    shapes = [
        jax.ShapeDtypeStruct((length, width), bf16),
        jax.ShapeDtypeStruct((HALO, width), bf16),
        jax.ShapeDtypeStruct((batches, length, width), bf16),
        jax.ShapeDtypeStruct((batches, length, width), bf16),
        jax.ShapeDtypeStruct((1,), jnp.int32),
    ]
    out_specs = [some] * 2 + [hbm] * 2 + [smem]
    scratch = []
    if staged is None:
        scratch = [
            pltpu.VMEM((layers, rows, width), f32),
            pltpu.VMEM((layers, rows, width), f32),
            pltpu.VMEM((8, rows, LANES), f32),
            pltpu.VMEM((length, width), bf16),
            pltpu.VMEM((length, width), f32),
        ]
    scratch += [
        pltpu.VMEM((rows, width), f32),
        pltpu.VMEM((rows, width), f32),
        pltpu.VMEM((4, rows, LANES), f32),
        pltpu.VMEM((length, width), bf16),
        pltpu.VMEM((HALO, width), bf16),
        pltpu.VMEM((length, width), bf16),
        pltpu.VMEM((length, width), bf16),
        pltpu.SemaphoreType.DMA((5, 16)),
    ]
    aliases = {}
    if previous is not None:
        aliases = {len(operands): 2, len(operands) + 1: 3}
        operands += previous
        specs += [hbm] * 2
    if carry is not None:
        aliases[len(operands)] = 5
        operands.append(carry)
        specs.append(hbm)
        shapes.append(jax.ShapeDtypeStruct(carry.shape, carry.dtype))
        out_specs.append(hbm)
    if packing is not None:
        batch, dest, packed = packing
        aliases[len(operands) + 1] = 5
        operands += [dest, packed]
        specs += [vmem, hbm]
        feature = width // 8
        shapes.append(jax.ShapeDtypeStruct(packed.shape, bf16))
        out_specs.append(hbm)
        scratch += [pltpu.VMEM((8 * length, feature), bf16), pltpu.VMEM((packed.shape[0], feature), bf16)]
    pack_flag = 0 if packing is None else packing[0] + 1
    return pl.pallas_call(
        functools.partial(
            backward_kernel,
            (first, len(saved), previous is not None, pack_flag, near.ndim == 2, carry is not None, staged is not None),
        ),
        out_shape=shapes,
        in_specs=specs,
        out_specs=out_specs,
        scratch_shapes=scratch,
        input_output_aliases=aliases,
        compiler_params=pltpu.CompilerParams(vmem_limit_bytes=VMEM_LIMIT),
        cost_estimate=pl.CostEstimate(
            flops=25 * layers * rows * width, bytes_accessed=100 * MIB, transcendentals=0
        ),
        name="backward_map",
    )(*operands)


def spread_heads(gv, stacked):
    length, width = gv.shape[0], stacked.shape[1]
    for head in range(stacked.shape[0] // length):
        stacked[head * length : (head + 1) * length, :] = gv[:, head * width : (head + 1) * width]


def into_slots(dest, stacked, out):
    slot = lax.broadcasted_iota(jnp.int32, (out.shape[0], stacked.shape[0]), 0)
    place = jnp.where(slot == dest[...], 1.0, 0.0).astype(bf16)
    out[...] = jnp.dot(place, stacked[...], preferred_element_type=f32).astype(bf16)


def pack_kernel(dest, gv_all, order, *refs):
    out, stacked = refs[-2:]
    spread_heads(gv_all.at[0], stacked)
    into_slots(dest, stacked, out)


def pack_values(batch, dest, gv_all, slots, order, into, at, total):
    batches, length, model = gv_all.shape
    feature = model // 8
    operands = [dest, gv_all, order] + ([] if into is None else [into])
    specs = [
        pl.BlockSpec(dest.shape, lambda i: (0, 0)),
        pl.BlockSpec((1, length, model), lambda i: (batch, 0, 0)),
        pl.BlockSpec(memory_space=pltpu.SMEM),
    ] + ([] if into is None else [pl.BlockSpec(memory_space=pltpu.HBM)])
    return pl.pallas_call(
        pack_kernel,
        out_shape=jax.ShapeDtypeStruct((slots, total * feature), bf16),
        grid=(1,),
        in_specs=specs,
        out_specs=pl.BlockSpec((slots, feature), lambda i: (0, at)),
        scratch_shapes=[pltpu.VMEM((8 * length, feature), bf16)],
        input_output_aliases={} if into is None else {3: 0},
        compiler_params=pltpu.CompilerParams(vmem_limit_bytes=VMEM_LIMIT),
        cost_estimate=pl.CostEstimate(
            flops=MIB, bytes_accessed=MIB // 16, transcendentals=0
        ),
        name="pack_values",
    )(*operands)


def owner_kernel(first, count, has_table, got, place_of, row_of, groups, order, weight_in, *refs):
    if has_table:
        table_in, refs = refs[0], refs[1:]
    table, sorted_in, joined, rows, place, weight, total, sems = refs
    heads, row_width, feature = weight.shape
    table_rows = table.shape[0]
    copies = [
        pltpu.make_async_copy(weight_in.at[h], weight.at[h], sems.at[h]) for h in range(heads)
    ]
    if has_table:
        copies.append(pltpu.make_async_copy(table_in, total, sems.at[heads]))
    for copy in copies:
        copy.start()
    slots = got.shape[0]
    room = rows.shape[1] - 128
    step = 128
    few = room - 2 * step
    used = groups[first, 2 * heads]
    for m in range(1, count):
        used = jnp.maximum(used, groups[first + m, 2 * heads])
    sizes = ((used <= few, few), (used > few, room))

    def sort(size):
        half = size // 2
        for m in range(count):
            b = first + m

            def one(tile, carry):
                at = pl.multiple_of(tile * half, half)
                slot = lax.broadcasted_iota(jnp.int32, (half, slots), 0) + at
                pick = jnp.where(slot == place_of[b : b + 1, :], 1.0, 0.0).astype(bf16)
                sorted_in[m, pl.ds(at, half), :] = jnp.dot(
                    pick, got[:, m * feature : (m + 1) * feature], preferred_element_type=f32
                ).astype(bf16)
                return carry

            lax.fori_loop(0, 2, one, 0)

            def mark(tile, carry):
                at = pl.multiple_of(tile * step, step)
                row = lax.broadcasted_iota(jnp.int32, (step, size), 0) + at
                place[pl.ds(at, step), m * room : m * room + size] = jnp.where(
                    row == row_of[b : b + 1, 0:size], 1.0, 0.0
                ).astype(bf16)
                return carry

            lax.fori_loop(0, table_rows // step, mark, 0)
            rows[m, 0:size, :] = jnp.zeros((size, row_width), bf16)

    for fits, size in sizes:
        pl.when(fits)(functools.partial(sort, size))

    def head_step(h, carry):
        most = groups[first, heads + h]
        for m in range(1, count):
            most = jnp.maximum(most, groups[first + m, heads + h])

        def multiply(tile, carry):
            ats = []
            for m in range(count):
                at = jnp.where(
                    tile < groups[first + m, heads + h], groups[first + m, h] + tile * step, room
                )
                ats.append(pl.ds(pl.multiple_of(at, 16), step))
                joined[m * step : (m + 1) * step, :] = sorted_in[m, ats[m], :]
            out = lax.dot_general(
                joined[...], weight[h], (((1,), (1,)), ((), ())), preferred_element_type=f32
            ).astype(bf16)
            for m in range(count):
                rows[m, ats[m], :] = out[m * step : (m + 1) * step]
            return carry

        return lax.fori_loop(0, most, multiply, carry)

    for h in range(heads):
        copies[h].wait()
        head_step(h, 0)
    if has_table:
        copies[heads].wait()
    tile = 256

    def out_copy(block):
        cols = pl.ds(block * tile, tile)
        return pltpu.make_async_copy(
            total.at[:, cols], table.at[:, cols], sems.at[heads + 1 + block]
        )

    def add(size):
        for block in range(row_width // tile):
            cols = pl.ds(block * tile, tile)
            part = None
            for m in range(count):
                more = jnp.dot(
                    place[:, m * room : m * room + size],
                    rows[m, 0:size, cols],
                    preferred_element_type=f32,
                )
                part = more if part is None else part + more
            if has_table:
                part = part + total[:, cols]
            total[:, cols] = part
            out_copy(block).start()

    for fits, size in sizes:
        pl.when(fits)(functools.partial(add, size))
    for block in range(row_width // tile):
        out_copy(block).wait()


def owner_add(first, count, table, got, place_of, row_of, groups, weight, order):
    heads, row_width, feature = weight.shape
    slots = got.shape[0]
    room = row_of.shape[1]
    vmem = pl.BlockSpec(memory_space=pltpu.VMEM)
    smem = pl.BlockSpec(memory_space=pltpu.SMEM)
    operands = [got, place_of, row_of, groups, order, weight]
    hbm = pl.BlockSpec(memory_space=pltpu.HBM)
    specs = [vmem, vmem, vmem, smem, smem, hbm]
    if table is not None:
        operands.append(table)
        specs.append(hbm)
    return pl.pallas_call(
        functools.partial(owner_kernel, first, count, table is not None),
        out_shape=jax.ShapeDtypeStruct((TABLE_DEV, row_width), f32),
        in_specs=specs,
        out_specs=hbm,
        scratch_shapes=[
            pltpu.VMEM((count, room + 128, feature), bf16),
            pltpu.VMEM((count * 128, feature), bf16),
            pltpu.VMEM((count, room + 128, row_width), bf16),
            pltpu.VMEM((TABLE_DEV, count * room), bf16),
            pltpu.VMEM(weight.shape, bf16),
            pltpu.VMEM((TABLE_DEV, row_width), f32),
            pltpu.SemaphoreType.DMA((heads + 1 + row_width // 256,)),
        ],
        compiler_params=pltpu.CompilerParams(vmem_limit_bytes=VMEM_LIMIT),
        cost_estimate=pl.CostEstimate(
            flops=6 * count * slots * row_width * TABLE_DEV,
            bytes_accessed=18 * MIB,
            transcendentals=0,
        ),
        name="owner_add",
    )(*operands)


def slots_of(row_ids, owners, capacity):
    batches, length, heads = row_ids.shape
    ids = row_ids.transpose(0, 2, 1).reshape(batches, heads * length)
    owner = ids // TABLE_DEV
    local = ids - owner * TABLE_DEV
    head = jnp.arange(heads * length, dtype=jnp.int32) // length
    order = jnp.arange(heads * length, dtype=jnp.int32)
    ahead = (owner[:, None, :] == owner[:, :, None]) & (order[None, :] < order[:, None])
    rank = jnp.sum(ahead.astype(jnp.int32), -1)
    dest = owner * capacity + rank
    code = local * heads + head
    slot = jnp.arange(owners * capacity, dtype=jnp.int32)
    hit = dest[:, None, :] == slot[:, None]
    holds = jnp.sum(jnp.where(hit, code[:, None, :] + 1, 0), -1) - 1
    return dest, holds


def groups_of(holds, heads):
    batches, slots = holds.shape
    room = -(-(slots + 15 * heads) // 128) * 128
    valid = holds >= 0
    head = jnp.where(valid, holds % heads, -1)
    member = head[..., None] == jnp.arange(heads, dtype=jnp.int32)
    order = jnp.arange(slots, dtype=jnp.int32)
    below = (order[None, :] < order[:, None]).astype(bf16)
    rank = jnp.einsum("ij,bjh->bih", below, member.astype(bf16), preferred_element_type=f32)
    counts = jnp.sum(member.astype(jnp.int32), 1)
    padded = (counts + 15) // 16 * 16
    number = jnp.arange(heads, dtype=jnp.int32)
    starts = jnp.sum(jnp.where(number[None, :] < number[:, None], padded[:, None, :], 0), -1)
    place = jnp.sum(jnp.where(member, rank.astype(jnp.int32) + starts[:, None, :] + 1, 0), -1) - 1
    spot = jnp.arange(room, dtype=jnp.int32)
    hit = place[:, None, :] == spot[:, None]
    row = jnp.sum(jnp.where(hit, (holds // heads)[:, None, :] + 1, 0), -1) - 1
    used = jnp.sum(padded, 1, keepdims=True)
    groups = jnp.concatenate([starts, (counts + 127) // 128, used], 1)
    return place, row, groups


def shards(
    saved_inputs, memory, value_weight, conv_weight, norm_gain, layer_counts, row_ids, out_grad
):
    section = lax.axis_index("section")
    sections = lax.axis_size("section")
    owners = lax.axis_size("table")
    batches, length, width = out_grad.shape
    heads = memory.shape[3]
    capacity = 3 * length * heads // (2 * owners)
    slots = owners * capacity
    weight = value_weight[0]
    live = layer_counts[0]
    x = saved_inputs[0]
    is_top = section == sections - 1

    to_next = [(i, i + 1) for i in range(owners - 1)]
    to_last = [(i + 1, i) for i in range(owners - 1)]
    down = [(i + 1, i) for i in range(sections - 1)]
    down_halo = [
        ((i + 1) * owners + t + 1, i * owners + t)
        for i in range(sections - 1)
        for t in range(owners - 1)
    ]
    v, (next_one, last_one, next_rest, last_rest), taps = all_values(
        memory[0], weight, conv_weight[0], norm_gain[0], x, out_grad
    )
    before = lax.ppermute(next_one, "table", to_next)
    behind = behind_one = lax.ppermute(last_one, "table", to_last)

    saved = []
    outputs = table = dest = holds = place_of = row_of = groups = got = staged = None
    packed = [None, None]
    order = jnp.zeros((1,), jnp.int32)
    near = near_halo = order
    ticks = batches + sections - 1
    for tick in range(ticks):
        if tick < batches:
            carry = (next_rest, last_rest) if tick == 0 else ()
            state = forward_map(
                tick, max(tick - 1, 0), live.reshape(1), x, v, before, behind, taps, order, carry
            )
            saved.append(state[:3])
            if tick == 0:
                before = lax.ppermute(state[3], "table", to_next)
                behind = lax.ppermute(state[4], "table", to_last)
        first = max(0, tick - (sections - 1))
        position = tick - (sections - 1 - section)
        which = jnp.clip(position, 0, batches - 1)
        active = (position >= 0) & (position < batches)
        info = jnp.stack([which, active, is_top, live]).astype(jnp.int32)
        packing = (batches - 1, dest[batches - 1][None, :], packed[1]) if tick == ticks - 1 else None
        grad_send, halo_send, *outputs = backward_map(
            info, near, near_halo, out_grad, behind_one, behind if tick else behind_one, x, v, taps,
            first, saved[first : tick + 1], outputs, packing, packed[0] if tick == ticks - 2 else None, staged,
        )
        if tick == ticks - 2:
            packed[0] = outputs.pop()
            got = lax.all_to_all(packed[0], "table", 0, 0, tiled=True)
        if packing is not None:
            packed[1] = outputs.pop()
        order = outputs.pop()
        if tick < ticks - 1:
            near = lax.ppermute(grad_send, "section", down)
            near_halo = lax.ppermute(halo_send, ("section", "table"), down_halo)
        if tick == 0:
            dest, holds = slots_of(row_ids[0] + order, owners, capacity)
            holds = holds.reshape(batches, owners, capacity).transpose(1, 0, 2)
            holds = holds.reshape(owners, batches * capacity)
        if tick == sections:
            holds = lax.all_to_all(holds + order, "table", 0, 0, tiled=True)
            holds = holds.reshape(owners, batches, capacity).transpose(1, 0, 2)
            holds = holds.reshape(batches, slots)
        if tick == sections + 1:
            place_of, row_of, groups = groups_of(holds + order, heads)
        batch = tick - (sections - 1)
        if 0 <= batch < batches - 1:
            pair, at = batch // 2, batch % 2
            packed[pair] = pack_values(
                batch, dest[batch][None, :], outputs[1], slots, order, packed[pair], at, 2
            )
    rest = lax.all_to_all(packed[1], "table", 0, 0, tiled=True)
    table = owner_add(0, 2, None, got, place_of, row_of, groups, weight, order)
    table = owner_add(2, 2, table, rest, place_of, row_of, groups, weight, order)
    return (outputs[0][None], table[None])


def solution(mesh):
    placed = (
        P("section", None, "table", None),
        P("section", None, "table", None, None),
        P("section", None, None, None),
        P("section", None, None, None),
        P("section", None, None),
        P("section"),
        P("section", None, "table", None),
        P(None, "table", None),
    )
    return jax.shard_map(
        shards,
        mesh=mesh,
        in_specs=placed,
        out_specs=(P("section", None, "table", None), P("section", "table", None)),
        check_vma=False,
    )
```

```python
import functools
import math

import jax
import jax.numpy as jnp
from jax import lax
from jax.experimental import pallas as pl
from jax.experimental.pallas import tpu as pltpu
from jax.sharding import PartitionSpec as P

TABLE_DEV = 1024
HALO = 16
EPS = 1e-06
LANES = 128
STEP = 512
SPLIT = 4
MIB = 1 << 20
VMEM_LIMIT = 51 * MIB

f32 = jnp.float32
bf16 = jnp.bfloat16


def row_total(partial):
    return jnp.broadcast_to(jnp.sum(partial, -1, keepdims=True), partial.shape)


def columns(chunk):
    return pl.ds(pl.multiple_of(chunk * STEP, STEP), STEP)


def wide(narrow):
    return jnp.concatenate([narrow] * (STEP // LANES), 1)


def fold(chunk):
    return sum(chunk[:, i : i + LANES] for i in range(0, STEP, LANES))


def values_kernel(
    memory, weight, convs_in, gains_in, x, top, v_out, next_one, last_one, next_rest, last_rest, taps,
    held, wide_held, flat, v, for_next, for_last, convs, gains, sems,
):
    batches, rows = held.shape[:2]
    heads, _, feature = weight.shape
    length = rows // heads
    loads = [pltpu.make_async_copy(memory.at[b], held.at[b], sems.at[0, b]) for b in range(batches)]
    copies = [pltpu.make_async_copy(weight.at[h], flat.at[h], sems.at[1, h]) for h in range(heads)]
    low, high = pl.ds(0, HALO), pl.ds(length - HALO, HALO)
    edges = (
        pltpu.make_async_copy(x.at[:, high], for_next.at[:, pl.ds(0, HALO)], sems.at[3, 0]),
        pltpu.make_async_copy(x.at[:, low], for_last.at[:, pl.ds(0, HALO)], sems.at[3, 1]),
        pltpu.make_async_copy(top.at[:, low], for_last.at[:, pl.ds(HALO, HALO)], sems.at[3, 2]),
    )
    factors = (
        pltpu.make_async_copy(convs_in, convs, sems.at[3, 3]),
        pltpu.make_async_copy(gains_in, gains, sems.at[3, 4]),
    )
    for copy in (*loads, *copies, *edges, *factors):
        copy.start()
    step = 64
    for b in range(batches):
        loads[b].wait()

        def widen(tile, carry):
            at = pl.multiple_of(tile * step, step)
            block = held[b, pl.ds(at, step), :].astype(f32)
            for c in range(block.shape[1] // LANES):
                wide_held[c, pl.ds(b * rows + at, step), :] = block[:, c * LANES : (c + 1) * LANES]
            return carry

        lax.fori_loop(0, rows // step, widen, 0)
    outs = []
    for h in range(heads):
        copies[h].wait()
        taken = [
            wide_held[c, pl.ds(h, batches * length, stride=heads), :].astype(bf16)
            for c in range(wide_held.shape[0])
        ]
        cols = pl.ds(h * feature, feature)
        v[:, cols] = jnp.dot(
            jnp.concatenate(taken, 1), flat[h], preferred_element_type=f32
        )
        outs.append(pltpu.make_async_copy(v.at[:, cols], v_out.at[:, cols], sems.at[2, h]))
        outs[-1].start()
        for b in range(batches):
            for target, at, first in (
                (for_next, (b + 1) * length - HALO, HALO), (for_last, b * length, 2 * HALO)
            ):
                edge = v[at : at + HALO, cols]
                main = edge.astype(bf16)
                target[b, first : first + HALO, cols] = main
                target[b, first + HALO : first + 2 * HALO, cols] = (edge - main.astype(f32)).astype(bf16)
    for copy in (*edges, *factors):
        copy.wait()
    for i, (source, one, rest) in enumerate(
        ((for_next, next_one, next_rest), (for_last, last_one, last_rest))
    ):
        outs.append(pltpu.make_async_copy(source.at[pl.ds(0, 1)], one, sems.at[4, i]))
        outs.append(
            pltpu.make_async_copy(source.at[pl.ds(1, batches - 1)], rest, sems.at[4, 2 + i])
        )
        outs[-1].start()
        outs[-2].start()
    for layer in range(taps.shape[0]):
        taps[layer] = 0.5 * convs[layer] * gains[layer : layer + 1, :]
    for copy in outs:
        copy.wait()


def all_values(memory, weight, convs, gains, x, top):
    batches, length, heads, row_width = memory.shape
    feature = weight.shape[2]
    width = heads * feature
    hbm = pl.BlockSpec(memory_space=pltpu.HBM)
    vmem = pl.BlockSpec(memory_space=pltpu.VMEM)
    v, *halos, taps = pl.pallas_call(
        values_kernel,
        out_shape=(
            jax.ShapeDtypeStruct((batches * length, width), f32),
            jax.ShapeDtypeStruct((1, 3 * HALO, width), bf16),
            jax.ShapeDtypeStruct((1, 4 * HALO, width), bf16),
            jax.ShapeDtypeStruct((batches - 1, 3 * HALO, width), bf16),
            jax.ShapeDtypeStruct((batches - 1, 4 * HALO, width), bf16),
            jax.ShapeDtypeStruct(convs.shape, f32),
        ),
        in_specs=[hbm] * 6,
        out_specs=[hbm] * 5 + [vmem],
        scratch_shapes=[
            pltpu.VMEM((batches, length * heads, row_width), bf16),
            pltpu.VMEM((row_width // LANES, batches * length * heads, LANES), f32),
            pltpu.VMEM(weight.shape, bf16),
            pltpu.VMEM((batches * length, width), f32),
            pltpu.VMEM((batches, 3 * HALO, width), bf16),
            pltpu.VMEM((batches, 4 * HALO, width), bf16),
            pltpu.VMEM(convs.shape, f32),
            pltpu.VMEM(gains.shape, f32),
            pltpu.SemaphoreType.DMA((5, heads)),
        ],
        compiler_params=pltpu.CompilerParams(vmem_limit_bytes=VMEM_LIMIT + 8 * MIB),
        cost_estimate=pl.CostEstimate(
            flops=2 * batches * length * heads * row_width * feature,
            bytes_accessed=18 * MIB,
            transcendentals=0,
        ),
        name="all_values",
    )(memory.reshape(batches, length * heads, row_width), weight, convs, gains, x, top)
    return v.reshape(batches, length, width), halos, taps


def forward_kernel(
    batch, halo, carried, live_ref, x, v, before, behind, taps, order, *refs,
):
    hid_out, der_out, scal_out = refs[carried : carried + 3]
    x_win, v_win, terms, hid, der, scal, rms_now, sems = refs[2 * carried + 3 :]
    length, width = x.shape[1:]
    rows = x_win.shape[0]
    keep = rows - HALO
    chunks = width // STEP
    live = live_ref[0]
    end = HALO + length
    parts = (
        (x.at[batch], 0, length, x_win, HALO),
        (v.at[batch], 0, length, v_win, HALO),
        (before.at[halo], 0, HALO, x_win, 0),
        (before.at[halo], HALO, 2 * HALO, terms, 0),
        (behind.at[halo], 0, HALO, x_win, end),
        (behind.at[halo], 2 * HALO, 2 * HALO, terms, 2 * HALO),
    )
    loads = []
    for q in range(SPLIT):
        cols = pl.ds(q * (width // SPLIT), width // SPLIT)
        loads.append([])
        for i, (source, first, size, window, at) in enumerate(parts):
            loads[q].append(
                pltpu.make_async_copy(
                    source.at[pl.ds(first, size), cols],
                    window.at[pl.ds(at, size), cols],
                    sems.at[2 + i, q],
                )
            )
            loads[q][-1].start()

    def load(chunk, sums):
        cols = columns(chunk)
        for at, first in ((0, 0), (end, 2 * HALO)):
            v_win[at : at + HALO, cols] = terms[first : first + HALO, cols].astype(f32) + terms[
                first + HALO : first + 2 * HALO, cols
            ].astype(f32)
        x = x_win[:, cols].astype(f32)
        v = v_win[:, cols]
        return sums[0] + fold(x * x), sums[1] + fold(v * v), sums[2] + fold(x * v)

    zero = jnp.zeros((rows, LANES), f32)
    sums = (zero, zero, zero)
    for q in range(SPLIT):
        for copy in loads[q]:
            copy.wait()
        sums = lax.fori_loop(q * chunks // SPLIT, (q + 1) * chunks // SPLIT, load, sums)
    xx, vv, xv = sums
    xv = row_total(xv)
    rx = lax.rsqrt(row_total(xx) / width + EPS)
    rv = lax.rsqrt(row_total(vv) / width + EPS)
    gate = jax.nn.sigmoid(rx * rv * xv / math.sqrt(width))
    scal[4] = rx[HALO:]
    scal[5] = rv[HALO:]
    scal[6] = xv[HALO:]
    scal[7] = gate[HALO:]
    rms_now[...] = gate

    def mix(chunk, total):
        cols = columns(chunk)
        hidden = x_win[:, cols].astype(f32) + wide(rms_now[...]) * v_win[:, cols]
        hid[0, :, cols] = hidden
        return total + fold(hidden * hidden)

    total = lax.fori_loop(0, chunks, mix, zero)

    def hidden_copy(layer):
        return pltpu.make_async_copy(
            hid.at[layer, pl.ds(HALO, keep)], hid_out.at[layer], sems.at[0, layer]
        )

    def slope_copy(layer):
        return pltpu.make_async_copy(der.at[layer], der_out.at[layer], sems.at[1, layer])

    def layer_step(layer, total):
        hidden_copy(layer).start()
        rms = lax.rsqrt(row_total(total) / width + EPS)
        scal[layer] = rms[HALO:]
        rms_now[...] = rms

        def one(chunk, total):
            cols = columns(chunk)
            hidden = hid[layer, :, cols]
            unit = hidden * wide(rms_now[...])
            mixed = taps[layer, 0:1, cols] * unit
            for k in range(1, 4):
                mixed = mixed + taps[layer, k : k + 1, cols] * pltpu.roll(unit, k, 0)
            bend = jnp.tanh(mixed)
            rise = 1.0 + bend
            silu = mixed * rise
            der[layer, :, cols] = (rise + silu * (1.0 - bend))[HALO:]
            after = hidden + silu
            hid[layer + 1, :, cols] = after
            return total + fold(after * after)

        total = lax.fori_loop(0, chunks, one, zero)
        slope_copy(layer).start()
        return total

    lax.fori_loop(0, live, layer_step, total)
    out = pltpu.make_async_copy(scal, scal_out, sems.at[0, 4])
    out.start()

    def finish(layer, carry):
        hidden_copy(layer).wait()
        slope_copy(layer).wait()
        return carry

    lax.fori_loop(0, live, finish, 0)
    out.wait()


def forward_map(batch, halo, live, x, v, before, behind, taps, order, carry):
    length, width = x.shape[1:]
    keep = length + HALO
    rows = keep + HALO
    layers = taps.shape[0]
    hbm = pl.BlockSpec(memory_space=pltpu.HBM)
    return pl.pallas_call(
        functools.partial(forward_kernel, batch, halo, len(carry)),
        out_shape=(
            jax.ShapeDtypeStruct((layers, keep, width), f32),
            jax.ShapeDtypeStruct((layers, keep, width), f32),
            jax.ShapeDtypeStruct((8, keep, LANES), f32),
            *(jax.ShapeDtypeStruct(array.shape, array.dtype) for array in carry),
        ),
        in_specs=[pl.BlockSpec(memory_space=pltpu.SMEM)]
        + [hbm] * 4
        + [pl.BlockSpec(memory_space=pltpu.VMEM), pl.BlockSpec(memory_space=pltpu.SMEM)]
        + [hbm] * len(carry),
        out_specs=[hbm] * (3 + len(carry)),
        input_output_aliases={7 + i: 3 + i for i in range(len(carry))},
        scratch_shapes=[
            pltpu.VMEM((rows, width), bf16),
            pltpu.VMEM((rows, width), f32),
            pltpu.VMEM((4 * HALO, width), bf16),
            pltpu.VMEM((layers + 1, rows, width), f32),
            pltpu.VMEM((layers, keep, width), f32),
            pltpu.VMEM((8, keep, LANES), f32),
            pltpu.VMEM((rows, LANES), f32),
            pltpu.SemaphoreType.DMA((8, layers + 1)),
        ],
        compiler_params=pltpu.CompilerParams(vmem_limit_bytes=VMEM_LIMIT),
        cost_estimate=pl.CostEstimate(
            flops=30 * layers * rows * width,
            bytes_accessed=16 * MIB,
            transcendentals=layers * rows * width,
        ),
        name="forward_map",
    )(live, x, v, before, behind, taps, order, *carry)


def backward_kernel(
    held, info, near, near_halo, top, behind_one, behind_rest, taps, *refs,
):
    if held[6]:
        hid, der, scal, x_in, v_in = refs[:5]
        refs = refs[5:]
    else:
        x_all, v_all = refs[:2]
        saved = [refs[3 * i + 2 : 3 * i + 5] for i in range(held[1])]
        refs = refs[3 * held[1] + 2 :]
    if held[2]:
        gv_held, refs = refs[1], refs[2:]
    if held[9]:
        refs = refs[1:]
    if held[7]:
        near_right, refs = refs[0], refs[1:]
    if held[5]:
        refs = refs[1:6] + refs[7:]
    if held[3]:
        dest, refs = refs[0], refs[2:]
        packed, stacked, slots_now = refs[5], refs[-2], refs[-1]
        refs = refs[:5] + refs[6:-2]
    if held[8]:
        send_right, refs = refs[5], refs[:5] + refs[6:]
    if not held[6]:
        hid, der, scal, x_in, v_in = refs[5:10]
        refs = refs[:5] + refs[10:]
    grad_send, halo_send, grads_all, gv_all, order_out, g, u, coef, g_in, ga_in, gx, gv, sems = refs
    which = info[0]
    active = info[1]
    is_top = info[2]
    live = info[3]
    length = grad_send.shape[0]
    rows, width = g.shape
    chunks = width // STEP
    quarter = width // SPLIT
    first, count = held[0], held[1]
    order_out[0] = 0

    def part(q):
        return pl.ds(pl.multiple_of(q * quarter, quarter), quarter)

    def scal_copy(i):
        return pltpu.make_async_copy(saved[i][2], scal, sems.at[2, 0])

    def layer_copies(i, layer, q):
        cols = part(q)
        return (
            pltpu.make_async_copy(
                saved[i][1].at[layer, :, cols], der.at[layer, :, cols], sems.at[1, 4 * layer + q]
            ),
            pltpu.make_async_copy(
                saved[i][0].at[layer, :, cols], hid.at[layer, :, cols], sems.at[0, 4 * layer + q]
            ),
        )

    def input_copies():
        return (
            pltpu.make_async_copy(x_all.at[which], x_in, sems.at[2, 1]),
            pltpu.make_async_copy(v_all.at[which], v_in, sems.at[2, 3]),
        )

    def grad_copies(source, source_halo):
        return (
            pltpu.make_async_copy(source, g_in, sems.at[3, 0]),
            pltpu.make_async_copy(source_halo, ga_in, sems.at[3, 1]),
        )

    def pack():
        spread_heads(gv, stacked)
        into_slots(dest, stacked, slots_now)
        at = pl.ds(packed.shape[1] - slots_now.shape[1], slots_now.shape[1])
        copy = pltpu.make_async_copy(slots_now, packed.at[:, at], sems.at[3, 3])
        copy.start()
        copy.wait()

    @pl.when(active == 1)
    def _():
        @pl.when(is_top == 1)
        def _():
            for i, source in ((0, behind_one.at[0]), (1, behind_rest.at[jnp.maximum(which - 1, 0)])):
                @pl.when(jnp.minimum(which, 1) == i)
                def _():
                    for copy in grad_copies(top.at[which], source.at[pl.ds(HALO, HALO)]):
                        copy.start()

        if held[4]:
            @pl.when(is_top == 0)
            def _():
                if held[7]:
                    for i, source in enumerate((near, near_right)):
                        cols = pl.ds(i * (width // 2), width // 2)
                        pltpu.make_async_copy(source, g_in.at[:, cols], sems.at[3, 0]).start()
                    pltpu.make_async_copy(near_halo, ga_in, sems.at[3, 1]).start()
                else:
                    for copy in grad_copies(near, near_halo):
                        copy.start()

        if not held[6]:
            for i in range(count):
                @pl.when(which == first + i)
                def _():
                    def begin(step, carry):
                        layer = live - 1 - step
                        for q in range(SPLIT):
                            for copy in layer_copies(i, layer, q):
                                copy.start()
                        return carry

                    begin(0, 0)
                    scal_copy(i).start()
                    lax.fori_loop(1, live, begin, 0)

            for copy in input_copies():
                copy.start()

        for copy in grad_copies(top.at[which], behind_one.at[0, pl.ds(HALO, HALO)]):
            copy.wait()

        def into_taps(layer, cols, grad):
            size = grad.shape[0]
            slope = grad * der[layer, 0:size, cols]
            out = taps[layer, 0:1, cols] * slope
            for k in range(1, 4):
                out = out + taps[layer, k : k + 1, cols] * pltpu.roll(slope, size - k, 0)
            u[0:size, cols] = out
            return fold(out * hid[layer, 0:size, cols])

        last = live - 1
        total = jnp.zeros((rows, LANES), f32)
        for q in range(SPLIT):
            if not held[6]:
                for copy in layer_copies(0, last, q):
                    copy.wait()

            def start(chunk, total):
                cols = columns(chunk)
                g[0:length, cols] = g_in[:, cols].astype(f32)
                g[length:rows, cols] = ga_in[:, cols].astype(f32)
                return total + into_taps(last, cols, g[:, cols])

            total = lax.fori_loop(q * chunks // SPLIT, (q + 1) * chunks // SPLIT, start, total)
        if not held[6]:
            scal_copy(0).wait()

        def coefficients(layer, total):
            size = total.shape[0]
            rms = scal[layer, 0:size]
            coef[0, 0:size] = rms
            coef[1, 0:size] = -rms * rms * rms * (row_total(total) / width)

        def through_rms(layer, cols, size):
            return g[0:size, cols] + (
                wide(coef[0, 0:size]) * u[0:size, cols]
                + wide(coef[1, 0:size]) * hid[layer, 0:size, cols]
            )

        def layer_step(size, step, total):
            layer = live - 1 - step
            coefficients(layer, total)
            if not held[6]:
                for q in range(SPLIT):
                    for copy in layer_copies(0, layer - 1, q):
                        copy.wait()

            def one(chunk, total):
                cols = columns(chunk)
                grad = through_rms(layer, cols, size)
                g[0:size, cols] = grad
                return total + into_taps(layer - 1, cols, grad)

            return lax.fori_loop(0, chunks, one, jnp.zeros((size, LANES), f32))

        total = lax.fori_loop(
            0, jnp.minimum(live - 1, 1), functools.partial(layer_step, rows), total
        )
        fewer = rows - HALO // 2
        total = lax.fori_loop(
            1, live - 1, functools.partial(layer_step, fewer), total[0:fewer]
        )
        coefficients(0, total[0:length])
        if not held[6]:
            for copy in input_copies():
                copy.wait()

        def to_gate(chunk, total):
            cols = columns(chunk)
            grad = through_rms(0, cols, length)
            g[0:length, cols] = grad
            return total + fold(grad * v_in[:, cols])

        total = row_total(lax.fori_loop(0, chunks, to_gate, jnp.zeros((length, LANES), f32)))
        rx, rv, xv, gate = (scal[i, 0:length] for i in range(4, 8))
        both = total * gate * (1.0 - gate) * (1.0 / math.sqrt(width)) * rx * rv
        mean = xv / width
        coef[0, 0:length] = both
        coef[1, 0:length] = -both * rx * rx * mean
        coef[2, 0:length] = -both * rv * rv * mean
        coef[3, 0:length] = gate

        def finish(chunk, carry):
            cols = columns(chunk)
            grad = g[0:length, cols]
            x = x_in[:, cols].astype(f32)
            v = v_in[:, cols]
            cross = wide(coef[0, 0:length])
            grad_x = grad + cross * v + wide(coef[1, 0:length]) * x
            grad_v = wide(coef[3, 0:length]) * grad + cross * x + wide(coef[2, 0:length]) * v
            gx[:, cols] = grad_x.astype(bf16)
            gv[:, cols] = grad_v.astype(bf16)
            return carry

        def half_of(q):
            if not held[8]:
                return grad_send.at[:, part(q)]
            side = grad_send if q < SPLIT // 2 else send_right
            return side.at[:, part(q % (SPLIT // 2))]

        outs = []
        for q in range(SPLIT):
            lax.fori_loop(q * chunks // SPLIT, (q + 1) * chunks // SPLIT, finish, 0)
            cols = part(q)
            for i, (source, target) in enumerate((
                (gx.at[:, cols], half_of(q)),
                (gx.at[pl.ds(0, HALO), cols], halo_send.at[:, cols]),
                (gx.at[:, cols], grads_all.at[which, :, cols]),
                (gv.at[:, cols], gv_all.at[which, :, cols]),
            )):
                outs.append(pltpu.make_async_copy(source, target, sems.at[4, 4 * i + q]))
                outs[-1].start()
        if held[3]:
            pack()
        for copy in outs:
            copy.wait()

    if held[3]:
        @pl.when(active == 0)
        def _():
            copy = pltpu.make_async_copy(gv_held.at[held[3] - 1], gv, sems.at[3, 2])
            copy.start()
            copy.wait()
            pack()


def backward_map(
    info, near, near_halo, top, behind_one, behind_rest, x, v, taps, first, saved, previous, packing, carry, staged,
    near_right, halves, ready,
):
    batches, length, width = x.shape
    rows = length + HALO
    layers = taps.shape[0]
    flat = [array for group in saved for array in group]
    some = pl.BlockSpec(memory_space=pl.ANY)
    hbm = pl.BlockSpec(memory_space=pltpu.HBM)
    vmem = pl.BlockSpec(memory_space=pltpu.VMEM)
    smem = pl.BlockSpec(memory_space=pltpu.SMEM)
    operands = [info, near, near_halo, top, behind_one, behind_rest, taps]
    specs = [smem] + [some] * 2 + [hbm] * 3 + [vmem]
    if staged is None:
        operands += [x, v, *flat]
        specs += [hbm] * (2 + len(flat))
    else:
        operands += staged
        specs += [vmem] * len(staged)
    shapes = [
        jax.ShapeDtypeStruct((length, width // 2 if halves else width), bf16),
        jax.ShapeDtypeStruct((HALO, width), bf16),
        jax.ShapeDtypeStruct((batches, length, width), bf16),
        jax.ShapeDtypeStruct((batches, length, width), bf16),
        jax.ShapeDtypeStruct((1,), jnp.int32),
    ]
    out_specs = [some] * 2 + [hbm] * 2 + [smem]
    scratch = []
    if staged is None:
        scratch = [
            pltpu.VMEM((layers, rows, width), f32),
            pltpu.VMEM((layers, rows, width), f32),
            pltpu.VMEM((8, rows, LANES), f32),
            pltpu.VMEM((length, width), bf16),
            pltpu.VMEM((length, width), f32),
        ]
    scratch += [
        pltpu.VMEM((rows, width), f32),
        pltpu.VMEM((rows, width), f32),
        pltpu.VMEM((4, rows, LANES), f32),
        pltpu.VMEM((length, width), bf16),
        pltpu.VMEM((HALO, width), bf16),
        pltpu.VMEM((length, width), bf16),
        pltpu.VMEM((length, width), bf16),
        pltpu.SemaphoreType.DMA((5, 16)),
    ]
    aliases = {}
    if previous is not None:
        aliases = {len(operands): 2, len(operands) + 1: 3}
        operands += previous
        specs += [hbm] * 2
    if ready is not None:
        operands.append(ready)
        specs.append(some)
    if near_right is not None:
        operands.append(near_right)
        specs.append(some)
    if carry is not None:
        aliases[len(operands)] = 5
        operands.append(carry)
        specs.append(hbm)
        shapes.append(jax.ShapeDtypeStruct(carry.shape, carry.dtype))
        out_specs.append(hbm)
    if packing is not None:
        batch, dest, packed = packing
        aliases[len(operands) + 1] = 5
        operands += [dest, packed]
        specs += [vmem, hbm]
        feature = width // 8
        shapes.append(jax.ShapeDtypeStruct(packed.shape, bf16))
        out_specs.append(hbm)
        scratch += [pltpu.VMEM((8 * length, feature), bf16), pltpu.VMEM((packed.shape[0], feature), bf16)]
    if halves:
        shapes.append(jax.ShapeDtypeStruct((length, width // 2), bf16))
        out_specs.append(some)
    pack_flag = 0 if packing is None else packing[0] + 1
    return pl.pallas_call(
        functools.partial(
            backward_kernel,
            (first, len(saved), previous is not None, pack_flag, near.ndim == 2, carry is not None, staged is not None, near_right is not None, halves, ready is not None),
        ),
        out_shape=shapes,
        in_specs=specs,
        out_specs=out_specs,
        scratch_shapes=scratch,
        input_output_aliases=aliases,
        compiler_params=pltpu.CompilerParams(vmem_limit_bytes=VMEM_LIMIT),
        cost_estimate=pl.CostEstimate(
            flops=25 * layers * rows * width, bytes_accessed=100 * MIB, transcendentals=0
        ),
        name="backward_map",
    )(*operands)


def spread_heads(gv, stacked):
    length, width = gv.shape[0], stacked.shape[1]
    for head in range(stacked.shape[0] // length):
        stacked[head * length : (head + 1) * length, :] = gv[:, head * width : (head + 1) * width]


def into_slots(dest, stacked, out):
    slot = lax.broadcasted_iota(jnp.int32, (out.shape[0], stacked.shape[0]), 0)
    place = jnp.where(slot == dest[...], 1.0, 0.0).astype(bf16)
    out[...] = jnp.dot(place, stacked[...], preferred_element_type=f32).astype(bf16)


def pack_kernel(dest, gv_all, order, *refs):
    out, stacked = refs[-2:]
    spread_heads(gv_all.at[0], stacked)
    into_slots(dest, stacked, out)


def pack_values(batch, dest, gv_all, slots, order, into, at, total):
    batches, length, model = gv_all.shape
    feature = model // 8
    operands = [dest, gv_all, order] + ([] if into is None else [into])
    specs = [
        pl.BlockSpec(dest.shape, lambda i: (0, 0)),
        pl.BlockSpec((1, length, model), lambda i: (batch, 0, 0)),
        pl.BlockSpec(memory_space=pltpu.SMEM),
    ] + ([] if into is None else [pl.BlockSpec(memory_space=pltpu.HBM)])
    return pl.pallas_call(
        pack_kernel,
        out_shape=jax.ShapeDtypeStruct((slots, total * feature), bf16),
        grid=(1,),
        in_specs=specs,
        out_specs=pl.BlockSpec((slots, feature), lambda i: (0, at)),
        scratch_shapes=[pltpu.VMEM((8 * length, feature), bf16)],
        input_output_aliases={} if into is None else {3: 0},
        compiler_params=pltpu.CompilerParams(vmem_limit_bytes=VMEM_LIMIT),
        cost_estimate=pl.CostEstimate(
            flops=MIB, bytes_accessed=MIB // 16, transcendentals=0
        ),
        name="pack_values",
    )(*operands)


def hold_kernel(array, *refs):
    pass


def hold(array, *ready):
    some = pl.BlockSpec(memory_space=pl.ANY)
    hbm = pl.BlockSpec(memory_space=pltpu.HBM)
    return pl.pallas_call(
        hold_kernel,
        out_shape=jax.ShapeDtypeStruct(array.shape, array.dtype),
        in_specs=[hbm] + [some] * len(ready),
        out_specs=hbm,
        input_output_aliases={0: 0},
        compiler_params=pltpu.CompilerParams(vmem_limit_bytes=VMEM_LIMIT),
        cost_estimate=pl.CostEstimate(flops=0, bytes_accessed=0, transcendentals=0),
        name="hold",
    )(array, *ready)


def owner_kernel(first, count, has_table, got, place_of, row_of, groups, order, weight_in, *refs):
    if has_table:
        table_in, refs = refs[0], refs[1:]
    table, sorted_in, joined, rows, place, weight, total, sems = refs
    heads, row_width, feature = weight.shape
    table_rows = table.shape[0]
    copies = [
        pltpu.make_async_copy(weight_in.at[h], weight.at[h], sems.at[h]) for h in range(heads)
    ]
    if has_table:
        copies.append(pltpu.make_async_copy(table_in, total, sems.at[heads]))
    for copy in copies:
        copy.start()
    slots = got.shape[0]
    room = rows.shape[1] - 128
    step = 128
    few = room - 2 * step
    used = groups[first, 2 * heads]
    for m in range(1, count):
        used = jnp.maximum(used, groups[first + m, 2 * heads])
    sizes = ((used <= few, few), (used > few, room))

    def sort(size):
        half = size // 2
        for m in range(count):
            b = first + m

            def one(tile, carry):
                at = pl.multiple_of(tile * half, half)
                slot = lax.broadcasted_iota(jnp.int32, (half, slots), 0) + at
                pick = jnp.where(slot == place_of[b : b + 1, :], 1.0, 0.0).astype(bf16)
                sorted_in[m, pl.ds(at, half), :] = jnp.dot(
                    pick, got[:, m * feature : (m + 1) * feature], preferred_element_type=f32
                ).astype(bf16)
                return carry

            lax.fori_loop(0, 2, one, 0)

            def mark(tile, carry):
                at = pl.multiple_of(tile * step, step)
                row = lax.broadcasted_iota(jnp.int32, (step, size), 0) + at
                place[pl.ds(at, step), m * room : m * room + size] = jnp.where(
                    row == row_of[b : b + 1, 0:size], 1.0, 0.0
                ).astype(bf16)
                return carry

            lax.fori_loop(0, table_rows // step, mark, 0)
            rows[m, 0:size, :] = jnp.zeros((size, row_width), bf16)

    for fits, size in sizes:
        pl.when(fits)(functools.partial(sort, size))

    def head_step(h, carry):
        most = groups[first, heads + h]
        for m in range(1, count):
            most = jnp.maximum(most, groups[first + m, heads + h])

        def multiply(tile, carry):
            ats = []
            for m in range(count):
                at = jnp.where(
                    tile < groups[first + m, heads + h], groups[first + m, h] + tile * step, room
                )
                ats.append(pl.ds(pl.multiple_of(at, 16), step))
                joined[m * step : (m + 1) * step, :] = sorted_in[m, ats[m], :]
            out = lax.dot_general(
                joined[...], weight[h], (((1,), (1,)), ((), ())), preferred_element_type=f32
            ).astype(bf16)
            for m in range(count):
                rows[m, ats[m], :] = out[m * step : (m + 1) * step]
            return carry

        return lax.fori_loop(0, most, multiply, carry)

    for h in range(heads):
        copies[h].wait()
        head_step(h, 0)
    if has_table:
        copies[heads].wait()
    tile = 256

    def out_copy(block):
        cols = pl.ds(block * tile, tile)
        return pltpu.make_async_copy(
            total.at[:, cols], table.at[:, cols], sems.at[heads + 1 + block]
        )

    def add(size):
        for block in range(row_width // tile):
            cols = pl.ds(block * tile, tile)
            part = None
            for m in range(count):
                more = jnp.dot(
                    place[:, m * room : m * room + size],
                    rows[m, 0:size, cols],
                    preferred_element_type=f32,
                )
                part = more if part is None else part + more
            if has_table:
                part = part + total[:, cols]
            total[:, cols] = part
            out_copy(block).start()

    for fits, size in sizes:
        pl.when(fits)(functools.partial(add, size))
    for block in range(row_width // tile):
        out_copy(block).wait()


def owner_add(first, count, table, got, place_of, row_of, groups, weight, order):
    heads, row_width, feature = weight.shape
    slots = got.shape[0]
    room = row_of.shape[1]
    vmem = pl.BlockSpec(memory_space=pltpu.VMEM)
    smem = pl.BlockSpec(memory_space=pltpu.SMEM)
    operands = [got, place_of, row_of, groups, order, weight]
    hbm = pl.BlockSpec(memory_space=pltpu.HBM)
    specs = [vmem, vmem, vmem, smem, smem, hbm]
    if table is not None:
        operands.append(table)
        specs.append(hbm)
    return pl.pallas_call(
        functools.partial(owner_kernel, first, count, table is not None),
        out_shape=jax.ShapeDtypeStruct((TABLE_DEV, row_width), f32),
        in_specs=specs,
        out_specs=hbm,
        scratch_shapes=[
            pltpu.VMEM((count, room + 128, feature), bf16),
            pltpu.VMEM((count * 128, feature), bf16),
            pltpu.VMEM((count, room + 128, row_width), bf16),
            pltpu.VMEM((TABLE_DEV, count * room), bf16),
            pltpu.VMEM(weight.shape, bf16),
            pltpu.VMEM((TABLE_DEV, row_width), f32),
            pltpu.SemaphoreType.DMA((heads + 1 + row_width // 256,)),
        ],
        compiler_params=pltpu.CompilerParams(vmem_limit_bytes=VMEM_LIMIT),
        cost_estimate=pl.CostEstimate(
            flops=6 * count * slots * row_width * TABLE_DEV,
            bytes_accessed=18 * MIB,
            transcendentals=0,
        ),
        name="owner_add",
    )(*operands)


def slots_of(row_ids, owners, capacity):
    batches, length, heads = row_ids.shape
    ids = row_ids.transpose(0, 2, 1).reshape(batches, heads * length)
    owner = ids // TABLE_DEV
    local = ids - owner * TABLE_DEV
    head = jnp.arange(heads * length, dtype=jnp.int32) // length
    order = jnp.arange(heads * length, dtype=jnp.int32)
    ahead = (owner[:, None, :] == owner[:, :, None]) & (order[None, :] < order[:, None])
    rank = jnp.sum(ahead.astype(jnp.int32), -1)
    dest = owner * capacity + rank
    code = local * heads + head
    slot = jnp.arange(owners * capacity, dtype=jnp.int32)
    hit = dest[:, None, :] == slot[:, None]
    holds = jnp.sum(jnp.where(hit, code[:, None, :] + 1, 0), -1) - 1
    return dest, holds


def groups_of(holds, heads):
    batches, slots = holds.shape
    room = -(-(slots + 15 * heads) // 128) * 128
    valid = holds >= 0
    head = jnp.where(valid, holds % heads, -1)
    member = head[..., None] == jnp.arange(heads, dtype=jnp.int32)
    order = jnp.arange(slots, dtype=jnp.int32)
    below = (order[None, :] < order[:, None]).astype(bf16)
    rank = jnp.einsum("ij,bjh->bih", below, member.astype(bf16), preferred_element_type=f32)
    counts = jnp.sum(member.astype(jnp.int32), 1)
    padded = (counts + 15) // 16 * 16
    number = jnp.arange(heads, dtype=jnp.int32)
    starts = jnp.sum(jnp.where(number[None, :] < number[:, None], padded[:, None, :], 0), -1)
    place = jnp.sum(jnp.where(member, rank.astype(jnp.int32) + starts[:, None, :] + 1, 0), -1) - 1
    spot = jnp.arange(room, dtype=jnp.int32)
    hit = place[:, None, :] == spot[:, None]
    row = jnp.sum(jnp.where(hit, (holds // heads)[:, None, :] + 1, 0), -1) - 1
    used = jnp.sum(padded, 1, keepdims=True)
    groups = jnp.concatenate([starts, (counts + 127) // 128, used], 1)
    return place, row, groups


def shards(
    saved_inputs, memory, value_weight, conv_weight, norm_gain, layer_counts, row_ids, out_grad
):
    section = lax.axis_index("section")
    sections = lax.axis_size("section")
    owners = lax.axis_size("table")
    batches, length, width = out_grad.shape
    heads = memory.shape[3]
    capacity = 3 * length * heads // (2 * owners)
    slots = owners * capacity
    weight = value_weight[0]
    live = layer_counts[0]
    x = saved_inputs[0]
    is_top = section == sections - 1

    to_next = [(i, i + 1) for i in range(owners - 1)]
    to_last = [(i + 1, i) for i in range(owners - 1)]
    down = [(i + 1, i) for i in range(sections - 1)]
    down_halo = [
        ((i + 1) * owners + t + 1, i * owners + t)
        for i in range(sections - 1)
        for t in range(owners - 1)
    ]
    v, (next_one, last_one, next_rest, last_rest), taps = all_values(
        memory[0], weight, conv_weight[0], norm_gain[0], x, out_grad
    )
    before = lax.ppermute(next_one, "table", to_next)
    behind = behind_one = lax.ppermute(last_one, "table", to_last)

    saved = []
    outputs = table = dest = holds = place_of = row_of = groups = got = staged = near_right = None
    packed = [None, None]
    order = jnp.zeros((1,), jnp.int32)
    near = near_halo = order
    ticks = batches + sections - 1
    for tick in range(ticks):
        if tick < batches:
            carry = (next_rest, last_rest) if tick == 0 else ()
            state = forward_map(
                tick, max(tick - 1, 0), live.reshape(1), x, v, before, behind, taps, order, carry
            )
            saved.append(state[:3])
            if tick == 0:
                before = lax.ppermute(state[3], "table", to_next)
                behind = lax.ppermute(state[4], "table", to_last)
        first = max(0, tick - (sections - 1))
        position = tick - (sections - 1 - section)
        which = jnp.clip(position, 0, batches - 1)
        active = (position >= 0) & (position < batches)
        info = jnp.stack([which, active, is_top, live]).astype(jnp.int32)
        packing = (batches - 1, dest[batches - 1][None, :], packed[1]) if tick == ticks - 1 else None
        grad_send, halo_send, *outputs = backward_map(
            info, near, near_halo, out_grad, behind_one, behind if tick else behind_one, x, v, taps,
            first, saved[first : tick + 1], outputs, packing, packed[0] if tick == ticks - 2 else None, staged,
            near_right, tick == ticks - 2, holds if tick == ticks - 2 else None,
        )
        if tick == ticks - 2:
            send_right = outputs.pop()
            packed[0] = outputs.pop()
        if packing is not None:
            packed[1] = outputs.pop()
        order = outputs.pop()
        if tick < ticks - 1:
            near = lax.ppermute(grad_send, "section", down)
            near_halo = lax.ppermute(halo_send, ("section", "table"), down_halo)
        if tick == ticks - 2:
            near_right = lax.ppermute(send_right, "section", down)
            got = lax.all_to_all(hold(packed[0], near_halo, near), "table", 0, 0, tiled=True)
        if tick == 0:
            dest, holds = slots_of(row_ids[0] + order, owners, capacity)
            holds = holds.reshape(batches, owners, capacity).transpose(1, 0, 2)
            holds = holds.reshape(owners, batches * capacity)
        if tick == sections:
            holds = lax.all_to_all(holds + order, "table", 0, 0, tiled=True)
            holds = holds.reshape(owners, batches, capacity).transpose(1, 0, 2)
            holds = holds.reshape(batches, slots)
        if tick == sections + 1:
            place_of, row_of, groups = groups_of(holds + order, heads)
        batch = tick - (sections - 1)
        if 0 <= batch < batches - 1:
            pair, at = batch // 2, batch % 2
            packed[pair] = pack_values(
                batch, dest[batch][None, :], outputs[1], slots, order, packed[pair], at, 2
            )
    rest = lax.all_to_all(packed[1], "table", 0, 0, tiled=True)
    table = owner_add(0, 2, None, got, place_of, row_of, groups, weight, order)
    table = owner_add(2, 2, table, rest, place_of, row_of, groups, weight, order)
    return (outputs[0][None], table[None])


def solution(mesh):
    placed = (
        P("section", None, "table", None),
        P("section", None, "table", None, None),
        P("section", None, None, None),
        P("section", None, None, None),
        P("section", None, None),
        P("section"),
        P("section", None, "table", None),
        P(None, "table", None),
    )
    return jax.shard_map(
        shards,
        mesh=mesh,
        in_specs=placed,
        out_specs=(P("section", None, "table", None), P("section", "table", None)),
        check_vma=False,
    )
```
